32 devices in a mesh: cfg: 2 (over y), ta: 4 (over z), gz: 2 (over x), gy: 2 (over core).
Axes of the slice: x: 2, y: 2, z: 4, core: 2. Of those that a mesh axis runs over, the one named last changes fastest.
Arguments:
- eigen_store: bfloat16 [20, 3, 2, 24, 6, 256], P(None, None, None, ('cfg', 'ta'), 'gz', 'gy'), parts along dimension 3, may hold values from -6 to 6
- fat_links: bfloat16 [2, 4, 3, 3, 2, 24, 6, 256], P(None, None, None, None, None, ('cfg', 'ta'), 'gz', 'gy'), parts along dimension 5, may hold values from -0.59765625 to 0.59765625
- long_links: bfloat16 [2, 4, 3, 3, 2, 24, 6, 256], P(None, None, None, None, None, ('cfg', 'ta'), 'gz', 'gy'), parts along dimension 5, may hold values from -0.29882812 to 0.29882812
- chosen: int32 [32], P('cfg'), parts along dimension 0, may hold values from 0 to 19, as said below
- momenta: int32 [8, 3], replicated, may hold values from -2 to 2
- current_dirs: int32 [4], replicated, may hold values from 1 to 3
- taste_masks: int32 [4], replicated, may hold values from 0 to 7
Outputs:
- odd_vectors: bfloat16 [16, 3, 2, 24, 6, 256], P(None, None, None, ('cfg', 'ta'), 'gz', 'gy'), parts along dimension 3
- meson_fields: float32 [32, 24, 2, 16, 16], P(('gz', 'gy'), ('cfg', 'ta')), parts along dimension 1
The draws below stay inside these ranges and needn't reach their ends.
There are 2 independent parts, one for each index of `cfg`. The reference program is written for one: setup_inputs(seed, part) draws one part's arguments, and reference() takes and returns one part's arrays. A program takes and returns all parts, laid end to end along the dimension named above; an argument that names none is the same for every part. Nothing has to cross between parts.
Inputs may be any that keep to these rules, and one draw needn't show every extreme that they name: `chosen`: the 16 indices are distinct.
All inputs are finite; a program needn't handle non-finite values.
Results may differ from the reference program's by a relative error of at most 0.001.
Values may be sent and summed in bfloat16 or wider, within the bound.
No kernel may reach another device: no remote copies, remote signals or barrier semaphores. Data moves between devices by JAX's collectives and lax.ppermute only.
A program may use at most 128 MiB of HBM per device.

```python
import math
import jax
import jax.numpy as jnp
from jax import lax

NSTORE = 20
NEV = 16
NC = 4
NP = 8
NX = 64
NT = 12
NZ = 6
NY = 8


def draw_chosen(key, part):
    key = jax.random.fold_in(key, 7)
    first_key, second_key = jax.random.split(key)
    middle = jax.random.permutation(first_key, NSTORE - 2)[:NEV - 2].astype(jnp.int32) + 1
    ends = jnp.array([0, NSTORE - 1], jnp.int32)
    return jax.random.permutation(second_key, jnp.concatenate([ends, middle]))


def plant(entries, rng, smallest, high):
    spot = [jax.random.randint(jax.random.fold_in(rng, axis), (), 0, length) for axis, length in enumerate(entries.shape)]
    longest = entries.shape.index(max(entries.shape))
    next_to = spot[:longest] + [(spot[longest] + 1) % entries.shape[longest]] + spot[longest + 1:]
    return entries.at[tuple(spot)].set(smallest).at[tuple(next_to)].set(high)


def block_levels(rng, shape, cuts, low, high):
    loudness = 1.0
    for axis_at, blocks in cuts:
        heights = jax.random.uniform(jax.random.fold_in(jax.random.fold_in(rng, 6), axis_at), (blocks,), jnp.float32, low / len(cuts), high / len(cuts))
        loudness = loudness * jnp.repeat(jnp.exp(heights), shape[axis_at] // blocks).reshape((-1,) + (1,) * (len(shape) - 1 - axis_at))
    return loudness


def bell_draw(key, shape, scale, reach, shards=(), held_as=jnp.bfloat16):
    factor_of = block_levels(key, shape, shards, -0.22, 0.18) if shards else 1.0
    values = jax.random.normal(key, shape, jnp.float32) * scale * factor_of
    return jnp.minimum(jnp.maximum(values, -reach), reach).astype(held_as)


def setup_inputs(seed: int = 0, part: int = 0) -> dict:
    keys = jax.random.split(jax.random.key(seed), 8)
    part_splits = jax.random.split(jax.random.fold_in(keys[7], part), 8)
    return {
        "eigen_store": bell_draw(part_splits[0], (NSTORE, 3, 2, NT, NZ, NY * NX // 2), 1.0, 6.0, ((3, 4), (4, 2), (5, 2))),
        "fat_links": bell_draw(part_splits[1], (2, 4, 3, 3, 2, NT, NZ, NY * NX // 2), 0.1, 0.59765625, ((5, 4), (6, 2), (7, 2))),
        "long_links": bell_draw(part_splits[2], (2, 4, 3, 3, 2, NT, NZ, NY * NX // 2), 0.05, 0.29882812, ((5, 4), (6, 2), (7, 2))),
        "chosen": draw_chosen(jax.random.fold_in(jax.random.fold_in(keys[7], part), 71), part),
        "momenta": plant(jax.random.randint(keys[4], (NP, 3), -2, 3), jax.random.fold_in(keys[4], 1), -2, 2).astype(jnp.int32),
        "current_dirs": plant(jax.random.randint(keys[5], (NC,), 1, 4), jax.random.fold_in(keys[5], 1), 1, 3).astype(jnp.int32),
        "taste_masks": plant(jax.random.randint(keys[6], (NC,), 0, 8), jax.random.fold_in(keys[6], 1), 0, 7).astype(jnp.int32),
    }


highest = lax.Precision.HIGHEST

def matvec(matrix, vector):
    matrix_f = matrix.astype(jnp.float32)
    vector_f = vector.astype(jnp.float32)
    rows_out = []
    for row in range(3):
        out_real = jnp.zeros(vector_f[:, 0, 0].shape, jnp.float32)
        out_imag = jnp.zeros(vector_f[:, 0, 0].shape, jnp.float32)
        for column in range(3):
            real_m = matrix_f[row, column, 0]
            imag_m = matrix_f[row, column, 1]
            real_v = vector_f[:, column, 0]
            imag_v = vector_f[:, column, 1]
            out_real = out_real + (real_m * real_v - imag_m * imag_v)
            out_imag = out_imag + (real_m * imag_v + imag_m * real_v)
        rows_out.append(jnp.stack([out_real, out_imag], axis=1))
    return jnp.stack(rows_out, axis=1)

def meson_slice(left_all, right_vec, cosine, sine_row):
    currents = left_all.shape[0]
    vectors = left_all.shape[1]
    mom_count = cosine.shape[0]
    left_real = left_all[:, :, :, 0]
    left_imag = left_all[:, :, :, 1]
    left_turn = jnp.stack([-left_imag, left_real], axis=3)
    left_rows = jnp.stack([left_all, left_turn], axis=1)
    left_rows = left_rows.reshape(currents * 2 * vectors, 3, 2, left_all.shape[4])
    weights = jnp.concatenate([cosine, sine_row], axis=0)
    weighted = right_vec[:, :, :, None, :] * weights[None, None, None]
    summed = lax.dot_general(left_rows, weighted, (((1, 2, 3), (1, 2, 4)), ((), ())), precision=highest, preferred_element_type=jnp.float32)
    summed = summed.reshape(currents, 2, vectors, vectors, 2 * mom_count)
    real_out = summed[:, 0, :, :, :mom_count] + summed[:, 1, :, :, mom_count:]
    imag_out = summed[:, 1, :, :, :mom_count] - summed[:, 0, :, :, mom_count:]
    result = jnp.moveaxis(jnp.stack([real_out, imag_out], axis=1), 4, 1)
    return result.reshape(currents * mom_count, 2, vectors, vectors)

def reference(eigen_store, fat_links, long_links, chosen, momenta, current_dirs, taste_masks):
    half_x = NX // 2
    picked = jnp.take(eigen_store, chosen, axis=0)
    site_count = NZ * NY * half_x
    grid_shape = (NZ, NY, half_x)
    depth_glob = lax.broadcasted_iota(jnp.int32, grid_shape, 0)
    row_glob = lax.broadcasted_iota(jnp.int32, grid_shape, 1)
    x_half = lax.broadcasted_iota(jnp.int32, grid_shape, 2)
    norm_scale = 1.0 / math.sqrt(NX * NY * NZ / 2)

    def one_slice(tslice):
        parity = (tslice + depth_glob + row_glob) % 2
        x_glob = 2 * x_half + 1 - parity
        here_vec = lax.dynamic_index_in_dim(picked, tslice, 3, keepdims=False).reshape(NEV, 3, 2, NZ, NY, half_x)

        def hopped(direction, offset):
            if direction == 0:
                moved = lax.dynamic_index_in_dim(picked, (tslice + offset) % NT, 3, keepdims=False)
                moved = moved.reshape(NEV, 3, 2, NZ, NY, half_x)
            elif direction == 1:
                moved = jnp.roll(here_vec, -offset, axis=3)
            elif direction == 2:
                moved = jnp.roll(here_vec, -offset, axis=4)
            else:
                lead_step = (offset + 1) // 2
                forward_x = jnp.roll(here_vec, -lead_step, axis=5)
                behind = jnp.roll(here_vec, 1 - lead_step, axis=5)
                moved = jnp.where(parity == 0, forward_x, behind)
            return moved.reshape(NEV, 3, 2, site_count)
        fat_here = lax.dynamic_index_in_dim(fat_links, tslice, 5, keepdims=False).reshape(2, 4, 3, 3, 2, site_count)
        long_here = lax.dynamic_index_in_dim(long_links, tslice, 5, keepdims=False).reshape(2, 4, 3, 3, 2, site_count)
        dirac_out = jnp.zeros((NEV, 3, 2, site_count), jnp.float32)
        back_list = []
        for direction in range(4):
            back_hop = matvec(fat_here[1, direction], hopped(direction, -1))
            dirac_out = dirac_out + matvec(fat_here[0, direction], hopped(direction, 1)) - back_hop
            dirac_out = dirac_out + matvec(long_here[0, direction], hopped(direction, 3)) - matvec(long_here[1, direction], hopped(direction, -3))
            if direction > 0:
                back_list.append(back_hop)
        back_stack = jnp.stack(back_list)
        x_flat = x_glob.reshape(1, site_count)
        y_flat = jnp.broadcast_to(row_glob, grid_shape).reshape(1, site_count)
        z_flat = jnp.broadcast_to(depth_glob, grid_shape).reshape(1, site_count)
        fraction = (momenta[:, 0][:, None, None] * x_flat[None] % NX).astype(jnp.float32) / NX
        fraction = fraction + (momenta[:, 1][:, None, None] * y_flat[None] % NY).astype(jnp.float32) / NY
        fraction = fraction + (momenta[:, 2][:, None, None] * z_flat[None] % NZ).astype(jnp.float32) / NZ
        phase_angle = 2.0 * math.pi * fraction.reshape(NP, site_count)
        cosine = jnp.cos(phase_angle)
        sine_row = jnp.sin(phase_angle)
        left_list = []
        for current in range(NC):
            chosen_back = lax.dynamic_index_in_dim(back_stack, current_dirs[current] - 1, 0, keepdims=False)
            mask_bits = taste_masks[current]
            exponent = mask_bits % 2 * x_flat + mask_bits // 2 % 2 * y_flat + mask_bits // 4 % 2 * z_flat
            taste_sign = (1 - 2 * (exponent % 2)).astype(jnp.float32)
            left_list.append(chosen_back * taste_sign[0])
        meson_out = meson_slice(jnp.stack(left_list), dirac_out, cosine, sine_row) * norm_scale
        return (dirac_out.astype(jnp.bfloat16), meson_out)
    odd_all, meson_all = lax.map(one_slice, jnp.arange(NT, dtype=jnp.int32))
    odd_vectors = odd_all.reshape(NT, NEV, 3, 2, NZ, NY * half_x).transpose(1, 2, 3, 0, 4, 5)
    meson_fields = jnp.moveaxis(meson_all, 0, 1)
    return (odd_vectors, meson_fields)
```

```python
import functools
import math

import jax
import jax.numpy as jnp
from jax import lax
from jax.experimental import pallas as pl
from jax.experimental.pallas import tpu as pltpu
from jax.sharding import PartitionSpec as P

NX = 64
HALF = NX // 2
LANES = 128
F32 = jnp.float32
BF16 = jnp.bfloat16
VM = pl.BlockSpec(memory_space=pltpu.VMEM)
SM = pl.BlockSpec(memory_space=pltpu.SMEM)
HB = pl.BlockSpec(memory_space=pl.ANY)


def call(body, outs, ins, scratch, flops, bytes_accessed):
    return pl.pallas_call(
        body,
        out_shape=outs,
        in_specs=ins,
        out_specs=[VM] * len(outs),
        scratch_shapes=scratch,
        compiler_params=pltpu.CompilerParams(vmem_limit_bytes=40 * 1024 * 1024),
        cost_estimate=pl.CostEstimate(
            flops=flops, bytes_accessed=bytes_accessed, transcendentals=0
        ),
    )


def gather_kernel(chosen, store, out, wide, turned):
    vectors = chosen.shape[0]
    rows = out.shape[0] // vectors
    wide[: store.shape[0], :] = store[...].astype(F32)
    full = rows // 8
    rest = rows - 8 * full
    for n in range(vectors):
        start = chosen[n] * rows
        for q in range(full):
            turned[pl.ds(q * 8 * vectors + n, 8, stride=vectors), :] = wide[
                pl.ds(start + 8 * q, 8), :
            ]
        if rest:
            turned[pl.ds(full * 8 * vectors + n, rest, stride=vectors), :] = wide[
                pl.ds(start + 8 * full, rest), :
            ]
    out[...] = turned[...].astype(BF16)


class Links:
    def __init__(self, ref, times, depth):
        self.ref, self.times, self.depth = ref, times, depth

    def row(self, w, mu, a, b, t, z, ri):
        at = (((((w * 4 + mu) * 3 + a) * 3 + b) * self.times + t) * self.depth + z) * 2 + ri
        return self.ref[at : at + 1, :]


def add_hop(acc, links, w, mu, t, z, vec, minus):
    for a in range(3):
        for b in range(3):
            lr = links.row(w, mu, a, b, t, z, 0)
            li = links.row(w, mu, a, b, t, z, 1)
            vr, vi = vec[b]
            if minus:
                acc[a][0] = (acc[a][0] - lr * vr) + li * vi
                acc[a][1] = (acc[a][1] - lr * vi) - li * vr
            else:
                acc[a][0] = (acc[a][0] + lr * vr) - li * vi
                acc[a][1] = (acc[a][1] + lr * vi) + li * vr


def zeros(vectors):
    return [[jnp.zeros((vectors, LANES), F32) for _ in range(2)] for _ in range(3)]


def read(ref, t, z):
    return [[ref[a, t, z, ri].astype(F32) for ri in range(2)] for a in range(3)]


def write(ref, t, z, acc):
    for a in range(3):
        for ri in range(2):
            ref[a, t, z, ri] = acc[a][ri].astype(ref.dtype)


def subtract(acc, other):
    for a in range(3):
        for ri in range(2):
            acc[a][ri] = acc[a][ri] - other[a][ri]


def split_hops(product, vectors, count):
    out = []
    for h in range(count):
        cols = product[:, h * LANES : (h + 1) * LANES]
        out.append(
            [
                [cols[(a * 2 + ri) * vectors : (a * 2 + ri + 1) * vectors] for ri in range(2)]
                for a in range(3)
            ]
        )
    return out


OFFSETS = (1, -1, 3, -3)


def x_permutation(e):
    src = lax.broadcasted_iota(jnp.int32, (LANES, 4 * LANES), 0)
    col = lax.broadcasted_iota(jnp.int32, (LANES, 4 * LANES), 1)
    h = col // LANES
    dst = col % LANES
    y = dst // HALF
    k = dst % HALF
    s = (e + y) % 2
    lead = jnp.where(h == 0, 1, jnp.where(h == 1, 0, jnp.where(h == 2, 2, -1)))
    want = y * HALF + (k + lead - s + HALF) % HALF
    return jnp.where(src == want, 1.0, 0.0).astype(BF16)


def y_permutation():
    rows = LANES // HALF
    src = lax.broadcasted_iota(jnp.int32, (2 * LANES, 4 * LANES), 0)
    col = lax.broadcasted_iota(jnp.int32, (2 * LANES, 4 * LANES), 1)
    h = col // LANES
    dst = col % LANES
    y = dst // HALF
    k = dst % HALF
    d = jnp.where(h == 0, 1, jnp.where(h == 1, -1, jnp.where(h == 2, 3, -3)))
    want = ((y + d + 2 * rows) % (2 * rows)) * HALF + k
    return jnp.where(src == want, 1.0, 0.0).astype(BF16)


def local_kernel(times, depth, field, fat, long, dacc, back_x, fatf, longf, perm):
    vectors = field.shape[4]
    fatf[...] = fat[...].astype(F32)
    longf[...] = long[...].astype(F32)
    fat_l, long_l = Links(fatf, times, depth), Links(longf, times, depth)
    origin = lax.axis_index("ta") * times + lax.axis_index("gz") * depth
    for e in range(2):
        perm[e] = x_permutation(origin + e)
    for t in range(times):
        for z in range(depth):
            here = field[:, t, z].reshape(6 * vectors, LANES)
            moved = jnp.dot(here, perm[(t + z) % 2], preferred_element_type=F32)
            plus1, minus1, plus3, minus3 = split_hops(moved, vectors, 4)
            acc = zeros(vectors)
            add_hop(acc, fat_l, 1, 3, t, z, minus1, False)
            write(back_x, t, z, acc)
            for a in range(3):
                for ri in range(2):
                    acc[a][ri] = -acc[a][ri]
            add_hop(acc, fat_l, 0, 3, t, z, plus1, False)
            add_hop(acc, long_l, 0, 3, t, z, plus3, False)
            add_hop(acc, long_l, 1, 3, t, z, minus3, True)
            if t + 1 < times:
                add_hop(acc, fat_l, 0, 0, t, z, read(field, t + 1, z), False)
            if t >= 1:
                add_hop(acc, fat_l, 1, 0, t, z, read(field, t - 1, z), True)
            if z + 1 < depth:
                add_hop(acc, fat_l, 0, 1, t, z, read(field, t, z + 1), False)
            write(dacc, t, z, acc)


def turn_split(value):
    high = value.astype(BF16)
    low = (value - high.astype(F32)).astype(BF16)
    return high, low


def sincos_turns(turns):
    quarters = 4.0 * (turns - jnp.floor(turns + 0.5))
    near = jnp.floor(quarters + 0.5)
    x = (quarters - near) * (0.5 * math.pi)
    x2 = x * x
    s = x * (1.0 + x2 * (-1.0 / 6 + x2 * (1.0 / 120 + x2 * (-1.0 / 5040 + x2 / 362880))))
    c = 1.0 + x2 * (-0.5 + x2 * (1.0 / 24 + x2 * (-1.0 / 720 + x2 * (1.0 / 40320))))
    which = near.astype(jnp.int32) & 3
    odd = (which & 1) == 1
    cosine = jnp.where(odd, s, c)
    sine = jnp.where(odd, c, s)
    cosine = jnp.where((which == 1) | (which == 2), -cosine, cosine)
    sine = jnp.where(which >= 2, -sine, sine)
    return cosine, sine


def side_kernel(
    times, depth, sizes, rotate,
    momenta, dirs, masks, field, yfield, zprev, znext, fat, long, dacc_in, back_x,
    dacc, left_hi, left_lo, weights, fatf, longf, perm, back,
):
    vectors = field.shape[4]
    total_y, total_z, scale = sizes
    fatf[...] = fat[...].astype(F32)
    longf[...] = long[...].astype(F32)
    fat_l, long_l = Links(fatf, times, depth), Links(longf, times, depth)
    perm[...] = y_permutation()
    lane = lax.broadcasted_iota(jnp.int32, (8, LANES), 1)
    sub = lax.broadcasted_iota(jnp.int32, (8, LANES), 0)
    k = lane % HALF
    y_glob = lax.axis_index("gy") * (LANES // HALF) + lane // HALF
    quarters = [jnp.zeros((8, LANES), F32) for _ in range(3)]
    for p in range(8):
        for axis in range(3):
            quarters[axis] = jnp.where(sub == p, momenta[axis, p].astype(F32), quarters[axis])
    slots = dirs.shape[0]
    if rotate:
        gz, gy = lax.axis_index("gz"), lax.axis_index("gy")
        current_of = [((gz + d // 2) % 2) * 2 + (gy + d % 2) % 2 for d in range(slots)]
    else:
        current_of = list(range(slots))
    for t in range(times):
        for z in range(depth):
            here = jnp.concatenate(
                [
                    field[:, t, z].reshape(6 * vectors, LANES),
                    yfield[:, t, z].reshape(6 * vectors, LANES),
                ],
                axis=1,
            )
            moved = jnp.dot(here, perm[...], preferred_element_type=F32)
            plus1, minus1, plus3, minus3 = split_hops(moved, vectors, 4)
            back_y, back_z = zeros(vectors), zeros(vectors)
            add_hop(back_y, fat_l, 1, 2, t, z, minus1, False)
            for a in range(3):
                for ri in range(2):
                    back[1, a, t, z, ri] = back_y[a][ri]
                    back[2, a, t, z, ri] = back_x[a, t, z, ri]
            acc = read(dacc_in, t, z)
            subtract(acc, back_y)
            source = read(field, t, z - 1) if z >= 1 else read(zprev, t, depth - 1)
            add_hop(back_z, fat_l, 1, 1, t, z, source, False)
            for a in range(3):
                for ri in range(2):
                    back[0, a, t, z, ri] = back_z[a][ri]
            subtract(acc, back_z)
            add_hop(acc, fat_l, 0, 2, t, z, plus1, False)
            add_hop(acc, long_l, 0, 2, t, z, plus3, False)
            add_hop(acc, long_l, 1, 2, t, z, minus3, True)
            if z + 1 == depth:
                add_hop(acc, fat_l, 0, 1, t, z, read(znext, t, 0), False)
            add_hop(acc, long_l, 0, 1, t, z, read(znext, t, z), False)
            add_hop(acc, long_l, 1, 1, t, z, read(zprev, t, z), True)
            write(dacc, t, z, acc)

            t_glob = lax.axis_index("ta") * times + t
            z_glob = lax.axis_index("gz") * depth + z
            x_glob = 2 * k + 1 - (t_glob + z_glob + y_glob) % 2
            turns = (
                quarters[0] * (x_glob.astype(F32) * (1.0 / NX))
                + quarters[1] * (y_glob.astype(F32) * (1.0 / total_y))
                + quarters[2] * (z_glob.astype(F32) * (1.0 / total_z))
            )
            cosine, sine = sincos_turns(turns)
            weights[t * depth + z, 0:8] = cosine * scale
            weights[t * depth + z, 8:16] = sine * scale

            x_row, y_row = x_glob[0:1], y_glob[0:1]
            for slot in range(slots):
                current = current_of[slot]
                direction = dirs[current] - 1
                mask = masks[current]
                exponent = (
                    (mask & 1) * x_row + ((mask >> 1) & 1) * y_row + ((mask >> 2) & 1) * z_glob
                )
                sign = (1 - 2 * (exponent & 1)).astype(F32)
                for a in range(3):
                    real_h, real_l = turn_split(back[direction, a, t, z, 0] * sign)
                    imag_h, imag_l = turn_split(back[direction, a, t, z, 1] * sign)
                    col = (z * 3 + a) * 2 * LANES
                    first = slice(col, col + LANES)
                    other = slice(col + LANES, col + 2 * LANES)
                    top = slice(slot * 2 * vectors, slot * 2 * vectors + vectors)
                    low = slice(slot * 2 * vectors + vectors, (slot + 1) * 2 * vectors)
                    for ref, re, im in (
                        (left_hi, real_h, imag_h),
                        (left_lo, real_l, imag_l),
                    ):
                        ref[t, top, first] = re
                        ref[t, top, other] = im
                        ref[t, low, first] = -im
                        ref[t, low, other] = re


NT_DIMS = (((1,), (1,)), ((), ()))


def last_kernel(
    times, depth,
    dacc, afield, bfield, fat, long, weights, left_hi_hbm, left_lo_hbm,
    dirac16, *rest,
):
    pieces = rest[:4]
    fatf, longf, dirac, left_hi, left_lo, right_hi, right_lo, sems = rest[4:]
    vectors = dacc.shape[4]
    copies = [
        pltpu.make_async_copy(left_hi_hbm, left_hi, sems.at[0]),
        pltpu.make_async_copy(left_lo_hbm, left_lo, sems.at[1]),
    ]
    for copy in copies:
        copy.start()
    fatf[...] = fat[...].astype(F32)
    longf[...] = long[...].astype(F32)
    fat_l, long_l = Links(fatf, times, depth), Links(longf, times, depth)

    def hops(after, before):
        for t in range(times):
            for z in range(depth):
                acc = read(dacc, t, z)
                add_hop(acc, long_l, 0, 0, t, z, read(after, t, z), False)
                add_hop(acc, long_l, 1, 0, t, z, read(before, t, z), True)
                if t + 1 == times:
                    add_hop(acc, fat_l, 0, 0, t, z, read(after, 0, z), False)
                if t == 0:
                    add_hop(acc, fat_l, 1, 0, t, z, read(before, times - 1, z), True)
                write(dirac, t, z, acc)

    even = lax.axis_index("ta") % 2 == 0

    @pl.when(even)
    def _():
        hops(afield, bfield)

    @pl.when(jnp.logical_not(even))
    def _():
        hops(bfield, afield)

    dirac16[...] = dirac[...].astype(BF16)
    for copy in copies:
        copy.wait()
    rows = 2 * vectors
    for t in range(times):
        for z in range(depth):
            for a in range(3):
                for ri in range(2):
                    col = ((z * 3 + a) * 2 + ri) * LANES
                    value = dirac[a, t, z, ri]
                    for w in range(16):
                        high, low = turn_split(value * weights[t * depth + z, w : w + 1, :])
                        right_hi[w * vectors : (w + 1) * vectors, col : col + LANES] = high
                        right_lo[w * vectors : (w + 1) * vectors, col : col + LANES] = low
        lh, ll = left_hi[t], left_lo[t]
        rh, rl = right_hi[...], right_lo[...]
        total = lax.dot_general(lh, rh, NT_DIMS, preferred_element_type=F32)
        total = total + lax.dot_general(ll, rh, NT_DIMS, preferred_element_type=F32)
        total = total + lax.dot_general(lh, rl, NT_DIMS, preferred_element_type=F32)
        half = 8 * vectors
        for slot, piece in enumerate(pieces):
            plain = total[slot * rows : slot * rows + vectors]
            turned = total[slot * rows + vectors : (slot + 1) * rows]
            piece[t, 0] = plain[:, :half] + turned[:, half:]
            piece[t, 1] = turned[:, :half] - plain[:, half:]


def spread_kernel(dirac16, out, wide):
    rows, vectors = dirac16.shape[0], dirac16.shape[1]
    for r in range(rows):
        wide[pl.ds(r, vectors, stride=rows), :] = dirac16[r].astype(F32)
    out[...] = wide[...].astype(BF16)


def final_kernel(kept, arrived, other, out):
    times = kept.shape[0]
    for t in range(times):
        for ri in range(2):
            total = kept[t, ri] + arrived[t, ri] + other[t, ri]
            for p in range(out.shape[0]):
                width = out.shape[4]
                out[p, t, ri] = total[:, p * width : (p + 1) * width]


def exchange(value, axis):
    size = lax.axis_size(axis)
    up = [(i, (i + 1) % size) for i in range(size)]
    down = [(j, i) for i, j in up]
    before = lax.ppermute(value, axis, up)
    if size == 2:
        return before, before
    return before, lax.ppermute(value, axis, down)


def on_device(eigen_store, fat_links, long_links, chosen, momenta, current_dirs, taste_masks):
    stored, _, _, times, depth, _ = eigen_store.shape
    vectors = chosen.shape[0]
    per_vector = 6 * times * depth
    n_ta, n_gz, n_gy = (lax.axis_size(a) for a in ("ta", "gz", "gy"))
    total_y = (LANES // HALF) * n_gy
    total_z = depth * n_gz

    store = eigen_store.transpose(0, 1, 3, 4, 2, 5).reshape(stored * per_vector, LANES)
    fat = fat_links.transpose(0, 1, 2, 3, 5, 6, 4, 7).reshape(-1, LANES)
    long = long_links.transpose(0, 1, 2, 3, 5, 6, 4, 7).reshape(-1, LANES)
    link_rows = fat.shape[0]
    link_scratch = [pltpu.VMEM((link_rows, LANES), F32)] * 2
    shape6 = (3, times, depth, 2, vectors, LANES)
    field_f32 = jax.ShapeDtypeStruct(shape6, F32)

    (packed,) = call(
        gather_kernel,
        [jax.ShapeDtypeStruct((per_vector * vectors, LANES), BF16)],
        [SM, VM],
        [
            pltpu.VMEM((stored * per_vector, LANES), F32),
            pltpu.VMEM((per_vector * vectors, LANES), F32),
        ],
        10000,
        500000,
    )(chosen, store)
    near = [(i, i ^ 1) for i in range(n_ta)]
    far = [((i + 1) % n_ta, ((i ^ 1) + 1) % n_ta) for i in range(n_ta)]
    afield = lax.ppermute(packed, "ta", near)
    bfield = lax.ppermute(packed, "ta", far)
    zprev, znext = exchange(packed, "gz")
    yfield, _ = exchange(packed, "gy")
    field, afield, bfield, zprev, znext, yfield = (
        f.reshape(shape6) for f in (packed, afield, bfield, zprev, znext, yfield)
    )

    dacc, back_x = call(
        functools.partial(local_kernel, times, depth),
        [field_f32, field_f32],
        [VM] * 3,
        link_scratch + [pltpu.VMEM((2, LANES, 4 * LANES), BF16)],
        20000000,
        3000000,
    )(field, fat, long)

    slots = current_dirs.shape[0]
    momentum_count = momenta.shape[0]
    width = depth * 6 * LANES
    left_rows = slots * 2 * vectors
    left = jax.ShapeDtypeStruct((times, left_rows, width), BF16)
    rotate = n_gz == 2 and n_gy == 2
    scale = 1.0 / math.sqrt(NX * total_y * total_z / 2)
    dacc, left_hi, left_lo, weights = call(
        functools.partial(side_kernel, times, depth, (total_y, total_z, scale), rotate),
        [
            field_f32,
            left,
            left,
            jax.ShapeDtypeStruct((times * depth, 2 * momentum_count, LANES), F32),
        ],
        [SM] * 3 + [VM] * 8,
        link_scratch
        + [
            pltpu.VMEM((2 * LANES, 4 * LANES), BF16),
            pltpu.VMEM((3,) + shape6, F32),
        ],
        20000000,
        6000000,
    )(
        momenta.T, current_dirs, taste_masks,
        field, yfield, zprev, znext, fat, long, dacc, back_x,
    )

    piece = jax.ShapeDtypeStruct((times, 2, vectors, momentum_count * vectors), F32)
    dirac16, *pieces = call(
        functools.partial(last_kernel, times, depth),
        [jax.ShapeDtypeStruct(shape6, BF16)] + [piece] * slots,
        [VM] * 6 + [HB] * 2,
        link_scratch
        + [
            pltpu.VMEM(shape6, F32),
            pltpu.VMEM((times, left_rows, width), BF16),
            pltpu.VMEM((times, left_rows, width), BF16),
            pltpu.VMEM((2 * momentum_count * vectors, width), BF16),
            pltpu.VMEM((2 * momentum_count * vectors, width), BF16),
            pltpu.SemaphoreType.DMA((2,)),
        ],
        400000000,
        6000000,
    )(dacc, afield, bfield, fat, long, weights, left_hi, left_lo)

    (odd_rows,) = call(
        spread_kernel,
        [jax.ShapeDtypeStruct((vectors * per_vector, LANES), BF16)],
        [VM],
        [pltpu.VMEM((vectors * per_vector, LANES), F32)],
        10000,
        500000,
    )(dirac16.reshape(per_vector, vectors, LANES))
    odd_vectors = odd_rows.reshape(vectors, 3, times, depth, 2, LANES).transpose(0, 1, 4, 2, 3, 5)

    if rotate:
        swap = [(0, 1), (1, 0)]
        got = lax.ppermute(jnp.stack([pieces[1], pieces[3]]), "gy", swap)
        other = lax.ppermute(pieces[2] + got[1], "gz", swap)
        (meson_fields,) = call(
            final_kernel,
            [jax.ShapeDtypeStruct((momentum_count, times, 2, vectors, vectors), F32)],
            [VM] * 3,
            [],
            100000,
            600000,
        )(pieces[0], got[0], other)
    else:
        whole = jnp.stack(pieces).reshape(slots, times, 2, vectors, momentum_count, vectors)
        whole = whole.transpose(0, 4, 1, 2, 3, 5).reshape(
            slots * momentum_count, times, 2, vectors, vectors
        )
        meson_fields = lax.psum_scatter(whole, ("gz", "gy"), scatter_dimension=0, tiled=True)
    return odd_vectors, meson_fields


def solution(mesh):
    in_specs = (
        P(None, None, None, ("cfg", "ta"), "gz", "gy"),
        P(None, None, None, None, None, ("cfg", "ta"), "gz", "gy"),
        P(None, None, None, None, None, ("cfg", "ta"), "gz", "gy"),
        P("cfg"),
        P(),
        P(),
        P(),
    )
    out_specs = (
        P(None, None, None, ("cfg", "ta"), "gz", "gy"),
        P(("gz", "gy"), ("cfg", "ta"), None, None, None),
    )
    return jax.shard_map(
        on_device, mesh=mesh, in_specs=in_specs, out_specs=out_specs, check_vma=False
    )
```

```python
import functools
import math

import jax
import jax.numpy as jnp
from jax import lax
from jax.experimental import pallas as pl
from jax.experimental.pallas import tpu as pltpu
from jax.sharding import PartitionSpec as P

NX = 64
HALF = NX // 2
LANES = 128
F32 = jnp.float32
BF16 = jnp.bfloat16
VM = pl.BlockSpec(memory_space=pltpu.VMEM)
SM = pl.BlockSpec(memory_space=pltpu.SMEM)
HB = pl.BlockSpec(memory_space=pltpu.HBM)


def call(body, outs, ins, scratch, cost):
    return pl.pallas_call(
        body,
        out_shape=outs,
        in_specs=ins,
        out_specs=[VM] * len(outs),
        scratch_shapes=scratch,
        compiler_params=pltpu.CompilerParams(vmem_limit_bytes=40 * 1024 * 1024),
        cost_estimate=pl.CostEstimate(flops=cost, bytes_accessed=cost, transcendentals=0),
    )


def gather_kernel(
    vectors, chosen_hbm, store_hbm, fat_hbm, long_hbm,
    far, side, out, fat, long,
    chosen, store, wide, turned, sems,
):
    first = [
        pltpu.make_async_copy(chosen_hbm, chosen, sems.at[0]),
        pltpu.make_async_copy(store_hbm, store, sems.at[1]),
    ]
    later = [
        pltpu.make_async_copy(fat_hbm, fat, sems.at[2]),
        pltpu.make_async_copy(long_hbm, long, sems.at[3]),
    ]
    for copy in first + later:
        copy.start()
    for copy in first:
        copy.wait()
    size = out.shape[0]
    rows = size // vectors
    wide[...] = store[...].astype(F32)
    full = rows // 8
    rest = rows - 8 * full
    for n in range(vectors):
        start = chosen[n] * rows
        for q in range(full):
            turned[pl.ds(q * 8 * vectors + n, 8, stride=vectors), :] = wide[
                pl.ds(start + 8 * q, 8), :
            ]
        if rest:
            turned[pl.ds(full * 8 * vectors + n, rest, stride=vectors), :] = wide[
                pl.ds(start + 8 * full, rest), :
            ]
    for r in range(0, size, 16):
        block = turned[r : r + 16, :].astype(BF16)
        out[r : r + 16, :] = block
        far[r : r + 16, :] = block
        side[r : r + 16, :] = block
    for ref in (far, side):
        ref[size:, :] = jnp.zeros((ref.shape[0] - size, LANES), BF16)
    for copy in later:
        copy.wait()


class Links:
    def __init__(self, ref, times, depth):
        self.ref, self.times, self.depth = ref, times, depth

    def row(self, w, mu, a, b, t, z, ri):
        at = (((((w * 4 + mu) * 3 + a) * 3 + b) * self.times + t) * self.depth + z) * 2 + ri
        return self.ref[at : at + 1, :]


def add_hop(acc, links, w, mu, t, z, vec, minus):
    for a in range(3):
        for b in range(3):
            lr = links.row(w, mu, a, b, t, z, 0)
            li = links.row(w, mu, a, b, t, z, 1)
            vr, vi = vec[b]
            if minus:
                acc[a][0] = (acc[a][0] - lr * vr) + li * vi
                acc[a][1] = (acc[a][1] - lr * vi) - li * vr
            else:
                acc[a][0] = (acc[a][0] + lr * vr) - li * vi
                acc[a][1] = (acc[a][1] + lr * vi) + li * vr


class Field:
    def __init__(self, ref, times, depth, vectors):
        self.ref, self.times, self.depth, self.vectors = ref, times, depth, vectors

    def raw(self, t, z):
        out = []
        for a in range(3):
            pair = []
            for ri in range(2):
                at = (((a * self.times + t) * self.depth + z) * 2 + ri) * self.vectors
                pair.append(self.ref[at : at + self.vectors, :])
            out.append(pair)
        return out

    def read(self, t, z):
        return widen(self.raw(t, z))

    def stacked(self, t, z):
        return jnp.concatenate([v for pair in self.raw(t, z) for v in pair], axis=0)


def widen(parts):
    return [[v.astype(F32) for v in pair] for pair in parts]


def zeros(vectors):
    return [[jnp.zeros((vectors, LANES), F32) for _ in range(2)] for _ in range(3)]


def read(ref, t, z):
    return [[ref[a, t, z, ri] for ri in range(2)] for a in range(3)]


def write(ref, t, z, acc):
    for a in range(3):
        for ri in range(2):
            ref[a, t, z, ri] = acc[a][ri].astype(ref.dtype)


def subtract(acc, other):
    for a in range(3):
        for ri in range(2):
            acc[a][ri] = acc[a][ri] - other[a][ri]


def split_hops(product, vectors, count):
    out = []
    for h in range(count):
        cols = product[:, h * LANES : (h + 1) * LANES]
        out.append(
            [
                [cols[(a * 2 + ri) * vectors : (a * 2 + ri + 1) * vectors] for ri in range(2)]
                for a in range(3)
            ]
        )
    return out


def x_permutation(e):
    src = lax.broadcasted_iota(jnp.int32, (LANES, 4 * LANES), 0)
    col = lax.broadcasted_iota(jnp.int32, (LANES, 4 * LANES), 1)
    h = col // LANES
    dst = col % LANES
    y = dst // HALF
    k = dst % HALF
    s = (e + y) % 2
    lead = jnp.where(h == 0, 1, jnp.where(h == 1, 0, jnp.where(h == 2, 2, -1)))
    want = y * HALF + (k + lead - s + HALF) % HALF
    return jnp.where(src == want, 1.0, 0.0).astype(BF16)


def y_permutation():
    rows = LANES // HALF
    src = lax.broadcasted_iota(jnp.int32, (2 * LANES, 4 * LANES), 0)
    col = lax.broadcasted_iota(jnp.int32, (2 * LANES, 4 * LANES), 1)
    h = col // LANES
    dst = col % LANES
    y = dst // HALF
    k = dst % HALF
    d = jnp.where(h == 0, 1, jnp.where(h == 1, -1, jnp.where(h == 2, 3, -3)))
    want = ((y + d + 2 * rows) % (2 * rows)) * HALF + k
    return jnp.where(src == want, 1.0, 0.0).astype(BF16)


def local_kernel(
    times, depth, vectors, sizes,
    momenta_hbm, field_ref, y_ref, fat, long,
    dacc, back_xy, weights, fatf, longf,
    momenta, x_perm, y_perm, sem,
):
    total_y, total_z, scale = sizes
    copy = pltpu.make_async_copy(momenta_hbm, momenta, sem)
    copy.start()
    fatf[...] = fat[...].astype(F32)
    longf[...] = long[...].astype(F32)
    fat_l, long_l = Links(fatf, times, depth), Links(longf, times, depth)
    field = Field(field_ref, times, depth, vectors)
    y_field = Field(y_ref, times, depth, vectors)
    origin = lax.axis_index("ta") * times + lax.axis_index("gz") * depth
    for e in range(2):
        x_perm[e] = x_permutation(origin + e)
    y_perm[...] = y_permutation()
    for t in range(times):
        for z in range(depth):
            here = field.stacked(t, z)
            moved = jnp.dot(here, x_perm[(t + z) % 2], preferred_element_type=F32)
            plus1, minus1, plus3, minus3 = split_hops(moved, vectors, 4)
            back = zeros(vectors)
            add_hop(back, fat_l, 1, 3, t, z, minus1, False)
            write(back_xy.at[1], t, z, back)
            acc = [[-v for v in pair] for pair in back]
            add_hop(acc, fat_l, 0, 3, t, z, plus1, False)
            add_hop(acc, long_l, 0, 3, t, z, plus3, False)
            add_hop(acc, long_l, 1, 3, t, z, minus3, True)
            both = jnp.concatenate([here, y_field.stacked(t, z)], axis=1)
            moved = jnp.dot(both, y_perm[...], preferred_element_type=F32)
            plus1, minus1, plus3, minus3 = split_hops(moved, vectors, 4)
            back = zeros(vectors)
            add_hop(back, fat_l, 1, 2, t, z, minus1, False)
            write(back_xy.at[0], t, z, back)
            subtract(acc, back)
            add_hop(acc, fat_l, 0, 2, t, z, plus1, False)
            add_hop(acc, long_l, 0, 2, t, z, plus3, False)
            add_hop(acc, long_l, 1, 2, t, z, minus3, True)
            if t + 1 < times:
                add_hop(acc, fat_l, 0, 0, t, z, field.read(t + 1, z), False)
            if t >= 1:
                add_hop(acc, fat_l, 1, 0, t, z, field.read(t - 1, z), True)
            if z + 1 < depth:
                add_hop(acc, fat_l, 0, 1, t, z, field.read(t, z + 1), False)
            write(dacc, t, z, acc)
    copy.wait()
    count = momenta.shape[1]
    lane = lax.broadcasted_iota(jnp.int32, (count, LANES), 1)
    sub = lax.broadcasted_iota(jnp.int32, (count, LANES), 0)
    y_glob = lax.axis_index("gy") * (LANES // HALF) + lane // HALF
    q = [jnp.zeros((count, LANES), F32) for _ in range(3)]
    for p in range(count):
        for axis in range(3):
            q[axis] = jnp.where(sub == p, momenta[axis, p].astype(F32), q[axis])
    for t in range(times):
        for z in range(depth):
            z_glob = lax.axis_index("gz") * depth + z
            x_glob = 2 * (lane % HALF) + 1 - (origin + t + z + y_glob) % 2
            turns = (
                q[0] * (x_glob.astype(F32) * (1.0 / NX))
                + q[1] * (y_glob.astype(F32) * (1.0 / total_y))
                + q[2] * (z_glob.astype(F32) * (1.0 / total_z))
            )
            cosine, sine = sincos_turns(turns)
            weights[t * depth + z, 0:count] = cosine * scale
            weights[t * depth + z, count : 2 * count] = sine * scale


def turn_split(value):
    high = value.astype(BF16)
    low = (value - high.astype(F32)).astype(BF16)
    return high, low


def sincos_turns(turns):
    quarters = 4.0 * (turns - jnp.floor(turns + 0.5))
    near = jnp.floor(quarters + 0.5)
    x = (quarters - near) * (0.5 * math.pi)
    x2 = x * x
    s = x * (1.0 + x2 * (-1.0 / 6 + x2 * (1.0 / 120 + x2 * (-1.0 / 5040 + x2 / 362880))))
    c = 1.0 + x2 * (-0.5 + x2 * (1.0 / 24 + x2 * (-1.0 / 720 + x2 * (1.0 / 40320))))
    which = near.astype(jnp.int32) & 3
    odd = (which & 1) == 1
    cosine = jnp.where(odd, s, c)
    sine = jnp.where(odd, c, s)
    cosine = jnp.where((which == 1) | (which == 2), -cosine, cosine)
    sine = jnp.where(which >= 2, -sine, sine)
    return cosine, sine


def side_kernel(
    times, depth, vectors, rotate,
    dirs_hbm, masks_hbm, field_ref, before_ref, after_ref, fatf, longf, dacc_in, back_xy,
    dacc, left,
    dirs, masks, back, sems,
):
    copies = [
        pltpu.make_async_copy(dirs_hbm, dirs, sems.at[0]),
        pltpu.make_async_copy(masks_hbm, masks, sems.at[1]),
    ]
    for copy in copies:
        copy.start()
    fat_l, long_l = Links(fatf, times, depth), Links(longf, times, depth)
    field = Field(field_ref, times, depth, vectors)
    before = Field(before_ref, times, depth, vectors)
    after = Field(after_ref, times, depth, vectors)
    for t in range(times):
        for z in range(depth):
            acc = read(dacc_in, t, z)
            back_z = zeros(vectors)
            source = field.read(t, z - 1) if z >= 1 else before.read(t, depth - 1)
            add_hop(back_z, fat_l, 1, 1, t, z, source, False)
            write(back.at[0], t, z, back_z)
            for d in range(2):
                write(back.at[1 + d], t, z, read(back_xy.at[d], t, z))
            subtract(acc, back_z)
            if z + 1 == depth:
                add_hop(acc, fat_l, 0, 1, t, z, after.read(t, 0), False)
            add_hop(acc, long_l, 0, 1, t, z, after.read(t, z), False)
            add_hop(acc, long_l, 1, 1, t, z, before.read(t, z), True)
            write(dacc, t, z, acc)
    for copy in copies:
        copy.wait()
    slots = dirs.shape[0]
    if rotate:
        gz, gy = lax.axis_index("gz"), lax.axis_index("gy")
        current_of = [((gz + d // 2) % 2) * 2 + (gy + d % 2) % 2 for d in range(slots)]
    else:
        current_of = list(range(slots))
    lane = lax.broadcasted_iota(jnp.int32, (1, LANES), 1)
    y_glob = lax.axis_index("gy") * (LANES // HALF) + lane // HALF
    origin = lax.axis_index("ta") * times + lax.axis_index("gz") * depth
    low_part = slots * 2 * vectors
    for slot in range(slots):
        direction = dirs[current_of[slot]] - 1
        mask = masks[current_of[slot]]
        for t in range(times):
            for z in range(depth):
                z_glob = lax.axis_index("gz") * depth + z
                x_glob = 2 * (lane % HALF) + 1 - (origin + t + z + y_glob) % 2
                exponent = (
                    (mask & 1) * x_glob + ((mask >> 1) & 1) * y_glob + ((mask >> 2) & 1) * z_glob
                )
                sign = (1 - 2 * (exponent & 1)).astype(F32)
                for a in range(3):
                    col = (z * 3 + a) * 2 * LANES
                    first = slice(col, col + LANES)
                    other = slice(col + LANES, col + 2 * LANES)
                    real = turn_split(back[direction, a, t, z, 0] * sign)
                    imag = turn_split(back[direction, a, t, z, 1] * sign)
                    for part in range(2):
                        top = part * low_part + slot * 2 * vectors
                        turned = top + vectors
                        left[t, top : top + vectors, first] = real[part]
                        left[t, top : top + vectors, other] = imag[part]
                        left[t, turned : turned + vectors, first] = -imag[part]
                        left[t, turned : turned + vectors, other] = real[part]


NT_DIMS = (((1,), (1,)), ((), ()))


def last_kernel(
    times, depth, vectors,
    far_ref, dacc, near_ref, fatf, longf, weights, left,
    dirac16, *pieces,
):
    fat_l, long_l = Links(fatf, times, depth), Links(longf, times, depth)
    near = Field(near_ref, times, depth, vectors)
    far = Field(far_ref, times, depth, vectors)
    even = lax.axis_index("ta") % 2 == 0

    def pick(first, second, t, z):
        return [
            [jnp.where(even, f, s) for f, s in zip(x, y)]
            for x, y in zip(first.raw(t, z), second.raw(t, z))
        ]

    rows = 2 * vectors
    left_rows = left.shape[1] // 2
    count = weights.shape[1]
    half = count * vectors // 2
    for t in range(times):
        main = jnp.zeros((2 * left_rows, count * vectors), F32)
        rest = jnp.zeros((left_rows, count * vectors), F32)
        for z in range(depth):
            acc = read(dacc, t, z)
            add_hop(acc, long_l, 0, 0, t, z, widen(pick(near, far, t, z)), False)
            add_hop(acc, long_l, 1, 0, t, z, widen(pick(far, near, t, z)), True)
            if t + 1 == times:
                add_hop(acc, fat_l, 0, 0, t, z, widen(pick(near, far, 0, z)), False)
            if t == 0:
                add_hop(acc, fat_l, 1, 0, t, z, widen(pick(far, near, times - 1, z)), True)
            write(dirac16, t, z, acc)
            for a in range(3):
                high, low = [], []
                for ri in range(2):
                    parts = [
                        turn_split(acc[a][ri] * weights[t * depth + z, w : w + 1, :])
                        for w in range(count)
                    ]
                    high.append(jnp.concatenate([h for h, _ in parts], axis=0))
                    low.append(jnp.concatenate([l for _, l in parts], axis=0))
                high = jnp.concatenate(high, axis=1)
                low = jnp.concatenate(low, axis=1)
                col = (z * 3 + a) * 2 * LANES
                lefts = left[t, :, col : col + 2 * LANES]
                main = main + lax.dot_general(lefts, high, NT_DIMS, preferred_element_type=F32)
                rest = rest + lax.dot_general(
                    lefts[:left_rows], low, NT_DIMS, preferred_element_type=F32
                )
        total = main[:left_rows] + main[left_rows:] + rest
        for slot, piece in enumerate(pieces):
            plain = total[slot * rows : slot * rows + vectors]
            turned = total[slot * rows + vectors : (slot + 1) * rows]
            piece[t, 0] = plain[:, :half] + turned[:, half:]
            piece[t, 1] = turned[:, :half] - plain[:, half:]


def spread_kernel(dirac16, out, wide):
    rows, vectors = dirac16.shape[0], dirac16.shape[1]
    for r in range(rows):
        wide[pl.ds(r, vectors, stride=rows), :] = dirac16[r].astype(F32)
    out[...] = wide[...].astype(BF16)


def final_kernel(kept, arrived, other, out):
    times = kept.shape[0]
    for t in range(times):
        for ri in range(2):
            total = kept[t, ri] + arrived[t, ri] + other[t, ri]
            for p in range(out.shape[0]):
                width = out.shape[4]
                out[p, t, ri] = total[:, p * width : (p + 1) * width]


def exchange(value, axis):
    size = lax.axis_size(axis)
    up = [(i, (i + 1) % size) for i in range(size)]
    down = [(j, i) for i, j in up]
    before = lax.ppermute(value, axis, up)
    if size == 2:
        return before, before
    return before, lax.ppermute(value, axis, down)


def on_device(eigen_store, fat_links, long_links, chosen, momenta, current_dirs, taste_masks):
    stored, _, _, times, depth, _ = eigen_store.shape
    vectors = chosen.shape[0]
    per_vector = 6 * times * depth
    n_ta, n_gz, n_gy = (lax.axis_size(a) for a in ("ta", "gz", "gy"))
    total_y = (LANES // HALF) * n_gy
    total_z = depth * n_gz

    store = eigen_store.transpose(0, 1, 3, 4, 2, 5).reshape(stored * per_vector, LANES)
    fat = fat_links.transpose(0, 1, 2, 3, 5, 6, 4, 7).reshape(-1, LANES)
    long = long_links.transpose(0, 1, 2, 3, 5, 6, 4, 7).reshape(-1, LANES)
    link_rows = fat.shape[0]
    shape6 = (3, times, depth, 2, vectors, LANES)
    size = per_vector * vectors

    def rows_of(n, dtype=BF16):
        return jax.ShapeDtypeStruct((n, LANES), dtype)

    far_out, side_out, packed, fat_v, long_v = call(
        functools.partial(gather_kernel, vectors),
        [rows_of(size + 32), rows_of(size + 16), rows_of(size), rows_of(link_rows), rows_of(link_rows)],
        [HB] * 4,
        [
            pltpu.SMEM(chosen.shape, jnp.int32),
            pltpu.VMEM(store.shape, BF16),
            pltpu.VMEM(store.shape, F32),
            pltpu.VMEM((size, LANES), F32),
            pltpu.SemaphoreType.DMA((4,)),
        ],
        1000,
    )(chosen, store, fat, long)
    near = [(i, i ^ 1) for i in range(n_ta)]
    far = [((i + 1) % n_ta, ((i ^ 1) + 1) % n_ta) for i in range(n_ta)]
    far_field = lax.ppermute(far_out, "ta", far)
    before_z, after_z = exchange(side_out, "gz")
    near_field = lax.ppermute(packed, "ta", near)
    y_field, _ = exchange(packed, "gy")

    slots = current_dirs.shape[0]
    count = momenta.shape[0]
    width = depth * 6 * LANES
    left_rows = slots * 2 * vectors
    rotate = n_gz == 2 and n_gy == 2
    scale = 1.0 / math.sqrt(NX * total_y * total_z / 2)
    dacc, back_xy, weights, fatf, longf = call(
        functools.partial(local_kernel, times, depth, vectors, (total_y, total_z, scale)),
        [
            jax.ShapeDtypeStruct(shape6, F32),
            jax.ShapeDtypeStruct((2,) + shape6, F32),
            jax.ShapeDtypeStruct((times * depth, 2 * count, LANES), F32),
            rows_of(link_rows, F32),
            rows_of(link_rows, F32),
        ],
        [HB] + [VM] * 4,
        [
            pltpu.SMEM((3, count), jnp.int32),
            pltpu.VMEM((2, LANES, 4 * LANES), BF16),
            pltpu.VMEM((2 * LANES, 4 * LANES), BF16),
            pltpu.SemaphoreType.DMA,
        ],
        1000,
    )(momenta.T, packed, y_field, fat_v, long_v)
    dacc, left = call(
        functools.partial(side_kernel, times, depth, vectors, rotate),
        [
            jax.ShapeDtypeStruct(shape6, F32),
            jax.ShapeDtypeStruct((times, 2 * left_rows, width), BF16),
        ],
        [HB] * 2 + [VM] * 7,
        [
            pltpu.SMEM((slots,), jnp.int32),
            pltpu.SMEM((slots,), jnp.int32),
            pltpu.VMEM((3,) + shape6, F32),
            pltpu.SemaphoreType.DMA((2,)),
        ],
        1000,
    )(current_dirs, taste_masks, packed, before_z, after_z, fatf, longf, dacc, back_xy)
    piece = jax.ShapeDtypeStruct((times, 2, vectors, count * vectors), F32)
    dirac16, *pieces = call(
        functools.partial(last_kernel, times, depth, vectors),
        [jax.ShapeDtypeStruct(shape6, BF16)] + [piece] * slots,
        [VM] * 7,
        [],
        1000,
    )(far_field, dacc, near_field, fatf, longf, weights, left)

    (odd_rows,) = call(
        spread_kernel,
        [jax.ShapeDtypeStruct((vectors * per_vector, LANES), BF16)],
        [VM],
        [pltpu.VMEM((vectors * per_vector, LANES), F32)],
        1000,
    )(dirac16.reshape(per_vector, vectors, LANES))
    odd_vectors = odd_rows.reshape(vectors, 3, times, depth, 2, LANES).transpose(0, 1, 4, 2, 3, 5)

    if rotate:
        swap = [(0, 1), (1, 0)]
        got = lax.ppermute(jnp.stack([pieces[1], pieces[3]]), "gy", swap)
        other = lax.ppermute(pieces[2] + got[1], "gz", swap)
        (meson_fields,) = call(
            final_kernel,
            [jax.ShapeDtypeStruct((count, times, 2, vectors, vectors), F32)],
            [VM] * 3,
            [],
            1000,
        )(pieces[0], got[0], other)
    else:
        whole = jnp.stack(pieces).reshape(slots, times, 2, vectors, count, vectors)
        whole = whole.transpose(0, 4, 1, 2, 3, 5).reshape(
            slots * count, times, 2, vectors, vectors
        )
        meson_fields = lax.psum_scatter(whole, ("gz", "gy"), scatter_dimension=0, tiled=True)
    return odd_vectors, meson_fields


def solution(mesh):
    in_specs = (
        P(None, None, None, ("cfg", "ta"), "gz", "gy"),
        P(None, None, None, None, None, ("cfg", "ta"), "gz", "gy"),
        P(None, None, None, None, None, ("cfg", "ta"), "gz", "gy"),
        P("cfg"),
        P(),
        P(),
        P(),
    )
    out_specs = (
        P(None, None, None, ("cfg", "ta"), "gz", "gy"),
        P(("gz", "gy"), ("cfg", "ta"), None, None, None),
    )
    return jax.shard_map(
        on_device, mesh=mesh, in_specs=in_specs, out_specs=out_specs, check_vma=False
    )
```

```python
import functools
import math

import jax
import jax.numpy as jnp
from jax import lax
from jax.experimental import pallas as pl
from jax.experimental.pallas import tpu as pltpu
from jax.sharding import PartitionSpec as P

NX = 64
HALF = NX // 2
LANES = 128
F32 = jnp.float32
BF16 = jnp.bfloat16
VM = pl.BlockSpec(memory_space=pltpu.VMEM)
SM = pl.BlockSpec(memory_space=pltpu.SMEM)
HB = pl.BlockSpec(memory_space=pltpu.HBM)


def pinned(value):
    return pltpu.with_memory_space_constraint(value, pltpu.HBM)


def call(body, outs, ins, scratch, cost):
    return pl.pallas_call(
        body,
        out_shape=outs,
        in_specs=ins,
        out_specs=[VM] * len(outs),
        scratch_shapes=scratch,
        compiler_params=pltpu.CompilerParams(vmem_limit_bytes=40 * 1024 * 1024),
        cost_estimate=pl.CostEstimate(flops=cost, bytes_accessed=cost, transcendentals=0),
    )


def gather_kernel(
    vectors, chosen_hbm, store_hbm, fat_hbm, long_hbm,
    far, side, out, fat, long,
    chosen, store, wide, turned, sems,
):
    first = [
        pltpu.make_async_copy(chosen_hbm, chosen, sems.at[0]),
        pltpu.make_async_copy(store_hbm, store, sems.at[1]),
    ]
    later = [
        pltpu.make_async_copy(fat_hbm, fat, sems.at[2]),
        pltpu.make_async_copy(long_hbm, long, sems.at[3]),
    ]
    for copy in first + later:
        copy.start()
    for copy in first:
        copy.wait()
    size = out.shape[0]
    rows = size // vectors
    wide[...] = store[...].astype(F32)
    full = rows // 8
    rest = rows - 8 * full
    for n in range(vectors):
        start = chosen[n] * rows
        for q in range(full):
            turned[pl.ds(q * 8 * vectors + n, 8, stride=vectors), :] = wide[
                pl.ds(start + 8 * q, 8), :
            ]
        if rest:
            turned[pl.ds(full * 8 * vectors + n, rest, stride=vectors), :] = wide[
                pl.ds(start + 8 * full, rest), :
            ]
    for r in range(0, size, 16):
        block = turned[r : r + 16, :].astype(BF16)
        out[r : r + 16, :] = block
        far[r : r + 16, :] = block
        side[r : r + 16, :] = block
    for ref in (far, side):
        ref[size:, :] = jnp.zeros((ref.shape[0] - size, LANES), BF16)
    for copy in later:
        copy.wait()


class Links:
    def __init__(self, ref, times, depth):
        self.ref, self.times, self.depth = ref, times, depth

    def row(self, w, mu, a, b, t, z, ri):
        at = (((((w * 4 + mu) * 3 + a) * 3 + b) * self.times + t) * self.depth + z) * 2 + ri
        return self.ref[at : at + 1, :]


def add_hop(acc, links, w, mu, t, z, vec, minus):
    for a in range(3):
        for b in range(3):
            lr = links.row(w, mu, a, b, t, z, 0)
            li = links.row(w, mu, a, b, t, z, 1)
            vr, vi = vec[b]
            if minus:
                acc[a][0] = (acc[a][0] - lr * vr) + li * vi
                acc[a][1] = (acc[a][1] - lr * vi) - li * vr
            else:
                acc[a][0] = (acc[a][0] + lr * vr) - li * vi
                acc[a][1] = (acc[a][1] + lr * vi) + li * vr


class Field:
    def __init__(self, ref, times, depth, vectors):
        self.ref, self.times, self.depth, self.vectors = ref, times, depth, vectors

    def raw(self, t, z):
        out = []
        for a in range(3):
            pair = []
            for ri in range(2):
                at = (((a * self.times + t) * self.depth + z) * 2 + ri) * self.vectors
                pair.append(self.ref[at : at + self.vectors, :])
            out.append(pair)
        return out

    def read(self, t, z):
        return widen(self.raw(t, z))

    def stacked(self, t, z):
        return jnp.concatenate([v for pair in self.raw(t, z) for v in pair], axis=0)


def widen(parts):
    return [[v.astype(F32) for v in pair] for pair in parts]


def zeros(vectors):
    return [[jnp.zeros((vectors, LANES), F32) for _ in range(2)] for _ in range(3)]


def read(ref, t, z):
    return [[ref[a, t, z, ri] for ri in range(2)] for a in range(3)]


def write(ref, t, z, acc):
    for a in range(3):
        for ri in range(2):
            ref[a, t, z, ri] = acc[a][ri].astype(ref.dtype)


def subtract(acc, other):
    for a in range(3):
        for ri in range(2):
            acc[a][ri] = acc[a][ri] - other[a][ri]


def split_hops(product, vectors, count):
    out = []
    for h in range(count):
        cols = product[:, h * LANES : (h + 1) * LANES]
        out.append(
            [
                [cols[(a * 2 + ri) * vectors : (a * 2 + ri + 1) * vectors] for ri in range(2)]
                for a in range(3)
            ]
        )
    return out


def x_permutation(e):
    src = lax.broadcasted_iota(jnp.int32, (LANES, 4 * LANES), 0)
    col = lax.broadcasted_iota(jnp.int32, (LANES, 4 * LANES), 1)
    h = col // LANES
    dst = col % LANES
    y = dst // HALF
    k = dst % HALF
    s = (e + y) % 2
    lead = jnp.where(h == 0, 1, jnp.where(h == 1, 0, jnp.where(h == 2, 2, -1)))
    want = y * HALF + (k + lead - s + HALF) % HALF
    return jnp.where(src == want, 1.0, 0.0).astype(BF16)


def y_permutation():
    rows = LANES // HALF
    src = lax.broadcasted_iota(jnp.int32, (2 * LANES, 4 * LANES), 0)
    col = lax.broadcasted_iota(jnp.int32, (2 * LANES, 4 * LANES), 1)
    h = col // LANES
    dst = col % LANES
    y = dst // HALF
    k = dst % HALF
    d = jnp.where(h == 0, 1, jnp.where(h == 1, -1, jnp.where(h == 2, 3, -3)))
    want = ((y + d + 2 * rows) % (2 * rows)) * HALF + k
    return jnp.where(src == want, 1.0, 0.0).astype(BF16)


def local_kernel(
    times, depth, vectors, sizes,
    momenta_hbm, field_ref, y_ref, fat, long,
    dacc, back_xy, weights, fatf, longf,
    momenta, x_perm, y_perm, sem,
):
    total_y, total_z, scale = sizes
    copy = pltpu.make_async_copy(momenta_hbm, momenta, sem)
    copy.start()
    fatf[...] = fat[...].astype(F32)
    longf[...] = long[...].astype(F32)
    fat_l, long_l = Links(fatf, times, depth), Links(longf, times, depth)
    field = Field(field_ref, times, depth, vectors)
    y_field = Field(y_ref, times, depth, vectors)
    origin = lax.axis_index("ta") * times + lax.axis_index("gz") * depth
    for e in range(2):
        x_perm[e] = x_permutation(origin + e)
    y_perm[...] = y_permutation()
    for t in range(times):
        for z in range(depth):
            here = field.stacked(t, z)
            moved = jnp.dot(here, x_perm[(t + z) % 2], preferred_element_type=F32)
            plus1, minus1, plus3, minus3 = split_hops(moved, vectors, 4)
            back = zeros(vectors)
            add_hop(back, fat_l, 1, 3, t, z, minus1, False)
            write(back_xy.at[1], t, z, back)
            acc = [[-v for v in pair] for pair in back]
            add_hop(acc, fat_l, 0, 3, t, z, plus1, False)
            add_hop(acc, long_l, 0, 3, t, z, plus3, False)
            add_hop(acc, long_l, 1, 3, t, z, minus3, True)
            both = jnp.concatenate([here, y_field.stacked(t, z)], axis=1)
            moved = jnp.dot(both, y_perm[...], preferred_element_type=F32)
            plus1, minus1, plus3, minus3 = split_hops(moved, vectors, 4)
            back = zeros(vectors)
            add_hop(back, fat_l, 1, 2, t, z, minus1, False)
            write(back_xy.at[0], t, z, back)
            subtract(acc, back)
            add_hop(acc, fat_l, 0, 2, t, z, plus1, False)
            add_hop(acc, long_l, 0, 2, t, z, plus3, False)
            add_hop(acc, long_l, 1, 2, t, z, minus3, True)
            if t + 1 < times:
                add_hop(acc, fat_l, 0, 0, t, z, field.read(t + 1, z), False)
            if t >= 1:
                add_hop(acc, fat_l, 1, 0, t, z, field.read(t - 1, z), True)
            if z + 1 < depth:
                add_hop(acc, fat_l, 0, 1, t, z, field.read(t, z + 1), False)
            write(dacc, t, z, acc)
    copy.wait()
    count = momenta.shape[1]
    lane = lax.broadcasted_iota(jnp.int32, (count, LANES), 1)
    sub = lax.broadcasted_iota(jnp.int32, (count, LANES), 0)
    y_glob = lax.axis_index("gy") * (LANES // HALF) + lane // HALF
    q = [jnp.zeros((count, LANES), F32) for _ in range(3)]
    for p in range(count):
        for axis in range(3):
            q[axis] = jnp.where(sub == p, momenta[axis, p].astype(F32), q[axis])
    for t in range(times):
        for z in range(depth):
            z_glob = lax.axis_index("gz") * depth + z
            x_glob = 2 * (lane % HALF) + 1 - (origin + t + z + y_glob) % 2
            turns = (
                q[0] * (x_glob.astype(F32) * (1.0 / NX))
                + q[1] * (y_glob.astype(F32) * (1.0 / total_y))
                + q[2] * (z_glob.astype(F32) * (1.0 / total_z))
            )
            cosine, sine = sincos_turns(turns)
            weights[t * depth + z, 0:count] = cosine * scale
            weights[t * depth + z, count : 2 * count] = sine * scale


def turn_split(value):
    high = value.astype(BF16)
    low = (value - high.astype(F32)).astype(BF16)
    return high, low


def sincos_turns(turns):
    quarters = 4.0 * (turns - jnp.floor(turns + 0.5))
    near = jnp.floor(quarters + 0.5)
    x = (quarters - near) * (0.5 * math.pi)
    x2 = x * x
    s = x * (1.0 + x2 * (-1.0 / 6 + x2 * (1.0 / 120 + x2 * (-1.0 / 5040 + x2 / 362880))))
    c = 1.0 + x2 * (-0.5 + x2 * (1.0 / 24 + x2 * (-1.0 / 720 + x2 * (1.0 / 40320))))
    which = near.astype(jnp.int32) & 3
    odd = (which & 1) == 1
    cosine = jnp.where(odd, s, c)
    sine = jnp.where(odd, c, s)
    cosine = jnp.where((which == 1) | (which == 2), -cosine, cosine)
    sine = jnp.where(which >= 2, -sine, sine)
    return cosine, sine


def side_kernel(
    times, depth, vectors, rotate,
    dirs_hbm, masks_hbm, field_ref, before_ref, after_ref, fatf, longf, dacc_in, back_xy,
    dacc, left,
    dirs, masks, back, sems,
):
    copies = [
        pltpu.make_async_copy(dirs_hbm, dirs, sems.at[0]),
        pltpu.make_async_copy(masks_hbm, masks, sems.at[1]),
    ]
    for copy in copies:
        copy.start()
    fat_l, long_l = Links(fatf, times, depth), Links(longf, times, depth)
    field = Field(field_ref, times, depth, vectors)
    before = Field(before_ref, times, depth, vectors)
    after = Field(after_ref, times, depth, vectors)
    for t in range(times):
        for z in range(depth):
            acc = read(dacc_in, t, z)
            back_z = zeros(vectors)
            source = field.read(t, z - 1) if z >= 1 else before.read(t, depth - 1)
            add_hop(back_z, fat_l, 1, 1, t, z, source, False)
            write(back.at[0], t, z, back_z)
            for d in range(2):
                write(back.at[1 + d], t, z, read(back_xy.at[d], t, z))
            subtract(acc, back_z)
            if z + 1 == depth:
                add_hop(acc, fat_l, 0, 1, t, z, after.read(t, 0), False)
            add_hop(acc, long_l, 0, 1, t, z, after.read(t, z), False)
            add_hop(acc, long_l, 1, 1, t, z, before.read(t, z), True)
            write(dacc, t, z, acc)
    for copy in copies:
        copy.wait()
    slots = dirs.shape[0]
    if rotate:
        gz, gy = lax.axis_index("gz"), lax.axis_index("gy")
        current_of = [((gz + d // 2) % 2) * 2 + (gy + d % 2) % 2 for d in range(slots)]
    else:
        current_of = list(range(slots))
    lane = lax.broadcasted_iota(jnp.int32, (1, LANES), 1)
    y_glob = lax.axis_index("gy") * (LANES // HALF) + lane // HALF
    origin = lax.axis_index("ta") * times + lax.axis_index("gz") * depth
    low_part = slots * 2 * vectors
    for slot in range(slots):
        direction = dirs[current_of[slot]] - 1
        mask = masks[current_of[slot]]
        for t in range(times):
            for z in range(depth):
                z_glob = lax.axis_index("gz") * depth + z
                x_glob = 2 * (lane % HALF) + 1 - (origin + t + z + y_glob) % 2
                exponent = (
                    (mask & 1) * x_glob + ((mask >> 1) & 1) * y_glob + ((mask >> 2) & 1) * z_glob
                )
                sign = (1 - 2 * (exponent & 1)).astype(F32)
                for a in range(3):
                    col = (z * 3 + a) * 2 * LANES
                    first = slice(col, col + LANES)
                    other = slice(col + LANES, col + 2 * LANES)
                    real = turn_split(back[direction, a, t, z, 0] * sign)
                    imag = turn_split(back[direction, a, t, z, 1] * sign)
                    for part in range(2):
                        top = part * low_part + slot * 2 * vectors
                        turned = top + vectors
                        left[t, top : top + vectors, first] = real[part]
                        left[t, top : top + vectors, other] = imag[part]
                        left[t, turned : turned + vectors, first] = -imag[part]
                        left[t, turned : turned + vectors, other] = real[part]


NT_DIMS = (((1,), (1,)), ((), ()))


def last_kernel(
    times, depth, vectors,
    far_ref, dacc, near_ref, fatf, longf, weights, left,
    dirac16, *pieces,
):
    fat_l, long_l = Links(fatf, times, depth), Links(longf, times, depth)
    near = Field(near_ref, times, depth, vectors)
    far = Field(far_ref, times, depth, vectors)
    even = lax.axis_index("ta") % 2 == 0

    def pick(first, second, t, z):
        return [
            [jnp.where(even, f, s) for f, s in zip(x, y)]
            for x, y in zip(first.raw(t, z), second.raw(t, z))
        ]

    rows = 2 * vectors
    left_rows = left.shape[1] // 2
    count = weights.shape[1]
    half = count * vectors // 2
    for t in range(times):
        main = jnp.zeros((2 * left_rows, count * vectors), F32)
        rest = jnp.zeros((left_rows, count * vectors), F32)
        for z in range(depth):
            acc = read(dacc, t, z)
            add_hop(acc, long_l, 0, 0, t, z, widen(pick(near, far, t, z)), False)
            add_hop(acc, long_l, 1, 0, t, z, widen(pick(far, near, t, z)), True)
            if t + 1 == times:
                add_hop(acc, fat_l, 0, 0, t, z, widen(pick(near, far, 0, z)), False)
            if t == 0:
                add_hop(acc, fat_l, 1, 0, t, z, widen(pick(far, near, times - 1, z)), True)
            write(dirac16, t, z, acc)
            for a in range(3):
                high, low = [], []
                for ri in range(2):
                    parts = [
                        turn_split(acc[a][ri] * weights[t * depth + z, w : w + 1, :])
                        for w in range(count)
                    ]
                    high.append(jnp.concatenate([h for h, _ in parts], axis=0))
                    low.append(jnp.concatenate([l for _, l in parts], axis=0))
                high = jnp.concatenate(high, axis=1)
                low = jnp.concatenate(low, axis=1)
                col = (z * 3 + a) * 2 * LANES
                lefts = left[t, :, col : col + 2 * LANES]
                main = main + lax.dot_general(lefts, high, NT_DIMS, preferred_element_type=F32)
                rest = rest + lax.dot_general(
                    lefts[:left_rows], low, NT_DIMS, preferred_element_type=F32
                )
        total = main[:left_rows] + main[left_rows:] + rest
        for slot, piece in enumerate(pieces):
            plain = total[slot * rows : slot * rows + vectors]
            turned = total[slot * rows + vectors : (slot + 1) * rows]
            piece[t, 0] = plain[:, :half] + turned[:, half:]
            piece[t, 1] = turned[:, :half] - plain[:, half:]


def spread_kernel(dirac16, kept, arrived, out, partial, wide):
    rows, vectors = dirac16.shape[0], dirac16.shape[1]
    if partial is not None:
        partial[...] = kept[...] + arrived[...]
    for r in range(rows):
        wide[pl.ds(r, vectors, stride=rows), :] = dirac16[r].astype(F32)
    out[...] = wide[...].astype(BF16)


def turn_kernel(dirac16, out, wide):
    spread_kernel(dirac16, None, None, out, None, wide)


def final_kernel(partial, other, out):
    times = partial.shape[0]
    width = out.shape[4]
    for t in range(times):
        for ri in range(2):
            total = partial[t, ri] + other[t, ri]
            for p in range(out.shape[0]):
                out[p, t, ri] = total[:, p * width : (p + 1) * width]


def exchange(value, axis):
    size = lax.axis_size(axis)
    up = [(i, (i + 1) % size) for i in range(size)]
    down = [(j, i) for i, j in up]
    before = lax.ppermute(value, axis, up)
    if size == 2:
        return before, before
    return before, lax.ppermute(value, axis, down)


def on_device(eigen_store, fat_links, long_links, chosen, momenta, current_dirs, taste_masks):
    stored, _, _, times, depth, _ = eigen_store.shape
    vectors = chosen.shape[0]
    per_vector = 6 * times * depth
    n_ta, n_gz, n_gy = (lax.axis_size(a) for a in ("ta", "gz", "gy"))
    total_y = (LANES // HALF) * n_gy
    total_z = depth * n_gz

    store = eigen_store.transpose(0, 1, 3, 4, 2, 5).reshape(stored * per_vector, LANES)
    fat = fat_links.transpose(0, 1, 2, 3, 5, 6, 4, 7).reshape(-1, LANES)
    long = long_links.transpose(0, 1, 2, 3, 5, 6, 4, 7).reshape(-1, LANES)
    link_rows = fat.shape[0]
    shape6 = (3, times, depth, 2, vectors, LANES)
    size = per_vector * vectors

    def rows_of(n, dtype=BF16):
        return jax.ShapeDtypeStruct((n, LANES), dtype)

    far_out, side_out, packed, fat_v, long_v = call(
        functools.partial(gather_kernel, vectors),
        [rows_of(size + 32), rows_of(size + 16), rows_of(size), rows_of(link_rows), rows_of(link_rows)],
        [HB] * 4,
        [
            pltpu.SMEM(chosen.shape, jnp.int32),
            pltpu.VMEM(store.shape, BF16),
            pltpu.VMEM(store.shape, F32),
            pltpu.VMEM((size, LANES), F32),
            pltpu.SemaphoreType.DMA((4,)),
        ],
        1000,
    )(*map(pinned, (chosen, store, fat, long)))
    near = [(i, i ^ 1) for i in range(n_ta)]
    far = [((i + 1) % n_ta, ((i ^ 1) + 1) % n_ta) for i in range(n_ta)]
    far_field = lax.ppermute(far_out, "ta", far)
    before_z, after_z = exchange(side_out, "gz")
    near_field = lax.ppermute(packed, "ta", near)
    y_field, _ = exchange(packed, "gy")

    slots = current_dirs.shape[0]
    count = momenta.shape[0]
    width = depth * 6 * LANES
    left_rows = slots * 2 * vectors
    rotate = n_gz == 2 and n_gy == 2
    scale = 1.0 / math.sqrt(NX * total_y * total_z / 2)
    dacc, back_xy, weights, fatf, longf = call(
        functools.partial(local_kernel, times, depth, vectors, (total_y, total_z, scale)),
        [
            jax.ShapeDtypeStruct(shape6, F32),
            jax.ShapeDtypeStruct((2,) + shape6, F32),
            jax.ShapeDtypeStruct((times * depth, 2 * count, LANES), F32),
            rows_of(link_rows, F32),
            rows_of(link_rows, F32),
        ],
        [HB] + [VM] * 4,
        [
            pltpu.SMEM((3, count), jnp.int32),
            pltpu.VMEM((2, LANES, 4 * LANES), BF16),
            pltpu.VMEM((2 * LANES, 4 * LANES), BF16),
            pltpu.SemaphoreType.DMA,
        ],
        1000,
    )(pinned(momenta.T), packed, y_field, fat_v, long_v)
    dacc, left = call(
        functools.partial(side_kernel, times, depth, vectors, rotate),
        [
            jax.ShapeDtypeStruct(shape6, F32),
            jax.ShapeDtypeStruct((times, 2 * left_rows, width), BF16),
        ],
        [HB] * 2 + [VM] * 7,
        [
            pltpu.SMEM((slots,), jnp.int32),
            pltpu.SMEM((slots,), jnp.int32),
            pltpu.VMEM((3,) + shape6, F32),
            pltpu.SemaphoreType.DMA((2,)),
        ],
        1000,
    )(
        pinned(current_dirs), pinned(taste_masks), packed, before_z, after_z, fatf, longf, dacc, back_xy
    )
    piece = jax.ShapeDtypeStruct((times, 2, vectors, count * vectors), F32)
    dirac16, *pieces = call(
        functools.partial(last_kernel, times, depth, vectors),
        [jax.ShapeDtypeStruct(shape6, BF16)] + [piece] * slots,
        [VM] * 7,
        [],
        1000,
    )(far_field, dacc, near_field, fatf, longf, weights, left)

    odd_shape = rows_of(size)
    turned = dirac16.reshape(per_vector, vectors, LANES)
    scratch = [pltpu.VMEM((size, LANES), F32)]
    if rotate:
        swap = [(0, 1), (1, 0)]
        got = lax.ppermute(jnp.stack([pieces[1], pieces[3]]), "gy", swap)
        other = lax.ppermute(pieces[2] + got[1], "gz", swap)
        odd_rows, partial = call(
            spread_kernel, [odd_shape, piece], [VM] * 3, scratch, 1000
        )(turned, pieces[0], got[0])
        meson_shape = jax.ShapeDtypeStruct((count, times, 2, vectors, vectors), F32)
        (meson_fields,) = call(final_kernel, [meson_shape], [VM] * 2, [], 1000)(partial, other)
    else:
        (odd_rows,) = call(turn_kernel, [odd_shape], [VM], scratch, 1000)(turned)
        whole = jnp.stack(pieces).reshape(slots, times, 2, vectors, count, vectors)
        whole = whole.transpose(0, 4, 1, 2, 3, 5).reshape(
            slots * count, times, 2, vectors, vectors
        )
        meson_fields = lax.psum_scatter(whole, ("gz", "gy"), scatter_dimension=0, tiled=True)
    odd_vectors = odd_rows.reshape(vectors, 3, times, depth, 2, LANES).transpose(0, 1, 4, 2, 3, 5)
    return odd_vectors, meson_fields


def solution(mesh):
    in_specs = (
        P(None, None, None, ("cfg", "ta"), "gz", "gy"),
        P(None, None, None, None, None, ("cfg", "ta"), "gz", "gy"),
        P(None, None, None, None, None, ("cfg", "ta"), "gz", "gy"),
        P("cfg"),
        P(),
        P(),
        P(),
    )
    out_specs = (
        P(None, None, None, ("cfg", "ta"), "gz", "gy"),
        P(("gz", "gy"), ("cfg", "ta"), None, None, None),
    )
    return jax.shard_map(
        on_device, mesh=mesh, in_specs=in_specs, out_specs=out_specs, check_vma=False
    )
```

```python
import functools
import math

import jax
import jax.numpy as jnp
from jax import lax
from jax.experimental import pallas as pl
from jax.experimental.pallas import tpu as pltpu
from jax.sharding import PartitionSpec as P

NX = 64
HALF = NX // 2
LANES = 128
F32 = jnp.float32
BF16 = jnp.bfloat16
VM = pl.BlockSpec(memory_space=pltpu.VMEM)
SM = pl.BlockSpec(memory_space=pltpu.SMEM)
HB = pl.BlockSpec(memory_space=pltpu.HBM)


def pinned(value):
    return pltpu.with_memory_space_constraint(value, pltpu.HBM)


def call(body, outs, ins, scratch, cost):
    return pl.pallas_call(
        body,
        out_shape=outs,
        in_specs=ins,
        out_specs=[VM] * len(outs),
        scratch_shapes=scratch,
        compiler_params=pltpu.CompilerParams(vmem_limit_bytes=40 * 1024 * 1024),
        cost_estimate=pl.CostEstimate(flops=cost, bytes_accessed=cost, transcendentals=0),
    )


def gather_kernel(vectors, chosen_hbm, store_hbm, far, out, chosen, store, wide, turned, sems):
    copies = [
        pltpu.make_async_copy(chosen_hbm, chosen, sems.at[0]),
        pltpu.make_async_copy(store_hbm, store, sems.at[1]),
    ]
    for copy in copies:
        copy.start()
    for copy in copies:
        copy.wait()
    size = out.shape[0]
    rows = size // vectors
    wide[...] = store[...].astype(F32)
    full = rows // 8
    rest = rows - 8 * full
    for n in range(vectors):
        start = chosen[n] * rows
        for q in range(full):
            turned[pl.ds(q * 8 * vectors + n, 8, stride=vectors), :] = wide[
                pl.ds(start + 8 * q, 8), :
            ]
        if rest:
            turned[pl.ds(full * 8 * vectors + n, rest, stride=vectors), :] = wide[
                pl.ds(start + 8 * full, rest), :
            ]
    for r in range(0, size, 16):
        block = turned[r : r + 16, :].astype(BF16)
        out[r : r + 16, :] = block
        far[r : r + 16, :] = block
    far[size:, :] = jnp.zeros((far.shape[0] - size, LANES), BF16)


class Links:
    def __init__(self, ref, times, depth):
        self.ref, self.times, self.depth = ref, times, depth

    def row(self, w, mu, a, b, t, z, ri):
        at = (((((w * 4 + mu) * 3 + a) * 3 + b) * self.times + t) * self.depth + z) * 2 + ri
        return self.ref[at : at + 1, :]


def add_hop(acc, links, w, mu, t, z, vec, minus):
    for a in range(3):
        for b in range(3):
            lr = links.row(w, mu, a, b, t, z, 0)
            li = links.row(w, mu, a, b, t, z, 1)
            vr, vi = vec[b]
            if minus:
                acc[a][0] = (acc[a][0] - lr * vr) + li * vi
                acc[a][1] = (acc[a][1] - lr * vi) - li * vr
            else:
                acc[a][0] = (acc[a][0] + lr * vr) - li * vi
                acc[a][1] = (acc[a][1] + lr * vi) + li * vr


class Field:
    def __init__(self, ref, times, depth, vectors):
        self.ref, self.times, self.depth, self.vectors = ref, times, depth, vectors

    def raw(self, t, z):
        out = []
        for a in range(3):
            pair = []
            for ri in range(2):
                at = (((a * self.times + t) * self.depth + z) * 2 + ri) * self.vectors
                pair.append(self.ref[at : at + self.vectors, :])
            out.append(pair)
        return out

    def read(self, t, z):
        return widen(self.raw(t, z))

    def stacked(self, t, z):
        return jnp.concatenate([v for pair in self.raw(t, z) for v in pair], axis=0)


def widen(parts):
    return [[v.astype(F32) for v in pair] for pair in parts]


def zeros(vectors):
    return [[jnp.zeros((vectors, LANES), F32) for _ in range(2)] for _ in range(3)]


def read(ref, t, z):
    return [[ref[a, t, z, ri] for ri in range(2)] for a in range(3)]


def write(ref, t, z, acc):
    for a in range(3):
        for ri in range(2):
            ref[a, t, z, ri] = acc[a][ri].astype(ref.dtype)


def subtract(acc, other):
    for a in range(3):
        for ri in range(2):
            acc[a][ri] = acc[a][ri] - other[a][ri]


def split_hops(product, vectors, count):
    out = []
    for h in range(count):
        cols = product[:, h * LANES : (h + 1) * LANES]
        out.append(
            [
                [cols[(a * 2 + ri) * vectors : (a * 2 + ri + 1) * vectors] for ri in range(2)]
                for a in range(3)
            ]
        )
    return out


def x_permutation(e):
    src = lax.broadcasted_iota(jnp.int32, (LANES, 4 * LANES), 0)
    col = lax.broadcasted_iota(jnp.int32, (LANES, 4 * LANES), 1)
    h = col // LANES
    dst = col % LANES
    y = dst // HALF
    k = dst % HALF
    s = (e + y) % 2
    lead = jnp.where(h == 0, 1, jnp.where(h == 1, 0, jnp.where(h == 2, 2, -1)))
    want = y * HALF + (k + lead - s + HALF) % HALF
    return jnp.where(src == want, 1.0, 0.0).astype(BF16)


def y_permutation():
    rows = LANES // HALF
    src = lax.broadcasted_iota(jnp.int32, (2 * LANES, 4 * LANES), 0)
    col = lax.broadcasted_iota(jnp.int32, (2 * LANES, 4 * LANES), 1)
    h = col // LANES
    dst = col % LANES
    y = dst // HALF
    k = dst % HALF
    d = jnp.where(h == 0, 1, jnp.where(h == 1, -1, jnp.where(h == 2, 3, -3)))
    want = ((y + d + 2 * rows) % (2 * rows)) * HALF + k
    return jnp.where(src == want, 1.0, 0.0).astype(BF16)


def local_kernel(
    times, depth, vectors, sizes,
    momenta_hbm, fat_hbm, long_hbm, field_ref, y_ref,
    dacc, back_xy, weights, fatf, longf,
    momenta, fat, long, x_perm, y_perm, sems,
):
    total_y, total_z, scale = sizes
    copies = [
        pltpu.make_async_copy(fat_hbm, fat, sems.at[0]),
        pltpu.make_async_copy(long_hbm, long, sems.at[1]),
        pltpu.make_async_copy(momenta_hbm, momenta, sems.at[2]),
    ]
    for copy in copies:
        copy.start()
    fat_l, long_l = Links(fatf, times, depth), Links(longf, times, depth)
    field = Field(field_ref, times, depth, vectors)
    y_field = Field(y_ref, times, depth, vectors)
    origin = lax.axis_index("ta") * times + lax.axis_index("gz") * depth
    for e in range(2):
        x_perm[e] = x_permutation(origin + e)
    y_perm[...] = y_permutation()
    for copy in copies:
        copy.wait()
    fatf[...] = fat[...].astype(F32)
    longf[...] = long[...].astype(F32)
    for t in range(times):
        for z in range(depth):
            here = field.stacked(t, z)
            moved = jnp.dot(here, x_perm[(t + z) % 2], preferred_element_type=F32)
            plus1, minus1, plus3, minus3 = split_hops(moved, vectors, 4)
            back = zeros(vectors)
            add_hop(back, fat_l, 1, 3, t, z, minus1, False)
            write(back_xy.at[1], t, z, back)
            acc = [[-v for v in pair] for pair in back]
            add_hop(acc, fat_l, 0, 3, t, z, plus1, False)
            add_hop(acc, long_l, 0, 3, t, z, plus3, False)
            add_hop(acc, long_l, 1, 3, t, z, minus3, True)
            both = jnp.concatenate([here, y_field.stacked(t, z)], axis=1)
            moved = jnp.dot(both, y_perm[...], preferred_element_type=F32)
            plus1, minus1, plus3, minus3 = split_hops(moved, vectors, 4)
            back = zeros(vectors)
            add_hop(back, fat_l, 1, 2, t, z, minus1, False)
            write(back_xy.at[0], t, z, back)
            subtract(acc, back)
            add_hop(acc, fat_l, 0, 2, t, z, plus1, False)
            add_hop(acc, long_l, 0, 2, t, z, plus3, False)
            add_hop(acc, long_l, 1, 2, t, z, minus3, True)
            if t + 1 < times:
                add_hop(acc, fat_l, 0, 0, t, z, field.read(t + 1, z), False)
            if t >= 1:
                add_hop(acc, fat_l, 1, 0, t, z, field.read(t - 1, z), True)
            if z + 1 < depth:
                add_hop(acc, fat_l, 0, 1, t, z, field.read(t, z + 1), False)
            write(dacc, t, z, acc)
    count = momenta.shape[1]
    lane = lax.broadcasted_iota(jnp.int32, (count, LANES), 1)
    sub = lax.broadcasted_iota(jnp.int32, (count, LANES), 0)
    y_glob = lax.axis_index("gy") * (LANES // HALF) + lane // HALF
    q = [jnp.zeros((count, LANES), F32) for _ in range(3)]
    for p in range(count):
        for axis in range(3):
            q[axis] = jnp.where(sub == p, momenta[axis, p].astype(F32), q[axis])
    for t in range(times):
        for z in range(depth):
            z_glob = lax.axis_index("gz") * depth + z
            x_glob = 2 * (lane % HALF) + 1 - (origin + t + z + y_glob) % 2
            turns = (
                q[0] * (x_glob.astype(F32) * (1.0 / NX))
                + q[1] * (y_glob.astype(F32) * (1.0 / total_y))
                + q[2] * (z_glob.astype(F32) * (1.0 / total_z))
            )
            cosine, sine = sincos_turns(turns)
            weights[t * depth + z, 0:count] = cosine * scale
            weights[t * depth + z, count : 2 * count] = sine * scale


def halves(value):
    high = value.astype(BF16)
    low = (value - high.astype(F32)).astype(BF16)
    return high, low


def sincos_turns(turns):
    quarters = 4.0 * (turns - jnp.floor(turns + 0.5))
    near = jnp.floor(quarters + 0.5)
    x = (quarters - near) * (0.5 * math.pi)
    x2 = x * x
    s = x * (1.0 + x2 * (-1.0 / 6 + x2 * (1.0 / 120 + x2 * (-1.0 / 5040 + x2 / 362880))))
    c = 1.0 + x2 * (-0.5 + x2 * (1.0 / 24 + x2 * (-1.0 / 720 + x2 * (1.0 / 40320))))
    which = near.astype(jnp.int32) & 3
    odd = (which & 1) == 1
    cosine = jnp.where(odd, s, c)
    sine = jnp.where(odd, c, s)
    cosine = jnp.where((which == 1) | (which == 2), -cosine, cosine)
    sine = jnp.where(which >= 2, -sine, sine)
    return cosine, sine


def side_kernel(
    times, depth, vectors, rotate,
    dirs_hbm, masks_hbm, field_ref, before_ref, after_ref, fatf, longf, dacc_in, back_xy,
    dacc, left,
    dirs, masks, back, sems,
):
    copies = [
        pltpu.make_async_copy(dirs_hbm, dirs, sems.at[0]),
        pltpu.make_async_copy(masks_hbm, masks, sems.at[1]),
    ]
    for copy in copies:
        copy.start()
    fat_l, long_l = Links(fatf, times, depth), Links(longf, times, depth)
    field = Field(field_ref, times, depth, vectors)
    before = Field(before_ref, times, depth, vectors)
    after = Field(after_ref, times, depth, vectors)
    for t in range(times):
        for z in range(depth):
            acc = read(dacc_in, t, z)
            back_z = zeros(vectors)
            source = field.read(t, z - 1) if z >= 1 else before.read(t, depth - 1)
            add_hop(back_z, fat_l, 1, 1, t, z, source, False)
            write(back.at[0], t, z, back_z)
            for d in range(2):
                write(back.at[1 + d], t, z, read(back_xy.at[d], t, z))
            subtract(acc, back_z)
            if z + 1 == depth:
                add_hop(acc, fat_l, 0, 1, t, z, after.read(t, 0), False)
            add_hop(acc, long_l, 0, 1, t, z, after.read(t, z), False)
            add_hop(acc, long_l, 1, 1, t, z, before.read(t, z), True)
            write(dacc, t, z, acc)
    for copy in copies:
        copy.wait()
    slots = dirs.shape[0]
    if rotate:
        gz, gy = lax.axis_index("gz"), lax.axis_index("gy")
        current_of = [((gz + d // 2) % 2) * 2 + (gy + d % 2) % 2 for d in range(slots)]
    else:
        current_of = list(range(slots))
    lane = lax.broadcasted_iota(jnp.int32, (1, LANES), 1)
    y_glob = lax.axis_index("gy") * (LANES // HALF) + lane // HALF
    origin = lax.axis_index("ta") * times + lax.axis_index("gz") * depth
    low_part = slots * 2 * vectors
    for slot in range(slots):
        direction = dirs[current_of[slot]] - 1
        mask = masks[current_of[slot]]
        for t in range(times):
            for z in range(depth):
                z_glob = lax.axis_index("gz") * depth + z
                x_glob = 2 * (lane % HALF) + 1 - (origin + t + z + y_glob) % 2
                exponent = (
                    (mask & 1) * x_glob + ((mask >> 1) & 1) * y_glob + ((mask >> 2) & 1) * z_glob
                )
                sign = (1 - 2 * (exponent & 1)).astype(F32)
                for a in range(3):
                    col = (z * 3 + a) * 2 * LANES
                    first = slice(col, col + LANES)
                    other = slice(col + LANES, col + 2 * LANES)
                    real = halves(back[direction, a, t, z, 0] * sign)
                    imag = halves(back[direction, a, t, z, 1] * sign)
                    for part in range(2):
                        top = part * low_part + slot * 2 * vectors
                        turned = top + vectors
                        left[t, top : top + vectors, first] = real[part]
                        left[t, top : top + vectors, other] = imag[part]
                        left[t, turned : turned + vectors, first] = -imag[part]
                        left[t, turned : turned + vectors, other] = real[part]


NT_DIMS = (((1,), (1,)), ((), ()))


def last_kernel(
    times, depth, vectors,
    far_ref, dacc, near_ref, fatf, longf, weights, left,
    dirac16, *pieces,
):
    fat_l, long_l = Links(fatf, times, depth), Links(longf, times, depth)
    near = Field(near_ref, times, depth, vectors)
    far = Field(far_ref, times, depth, vectors)
    even = lax.axis_index("ta") % 2 == 0

    def pick(first, second, t, z):
        return [
            [jnp.where(even, f, s) for f, s in zip(x, y)]
            for x, y in zip(first.raw(t, z), second.raw(t, z))
        ]

    rows = 2 * vectors
    left_rows = left.shape[1] // 2
    count = weights.shape[1] // 2
    columns = count * vectors
    for t in range(times):
        parts = jnp.zeros((2 * left_rows, 2 * columns), F32)
        for z in range(depth):
            acc = read(dacc, t, z)
            add_hop(acc, long_l, 0, 0, t, z, widen(pick(near, far, t, z)), False)
            add_hop(acc, long_l, 1, 0, t, z, widen(pick(far, near, t, z)), True)
            if t + 1 == times:
                add_hop(acc, fat_l, 0, 0, t, z, widen(pick(near, far, 0, z)), False)
            if t == 0:
                add_hop(acc, fat_l, 1, 0, t, z, widen(pick(far, near, times - 1, z)), True)
            write(dirac16, t, z, acc)
            at = t * depth + z
            for a in range(3):
                real, imag = acc[a]
                right = [[], []]
                for p in range(count):
                    cosine = weights[at, p : p + 1, :]
                    sine = weights[at, count + p : count + p + 1, :]
                    right[0].append(halves(cosine * real + sine * imag))
                    right[1].append(halves(cosine * imag - sine * real))
                right = jnp.concatenate(
                    [
                        jnp.concatenate([h for h, _ in r] + [l for _, l in r], axis=0)
                        for r in right
                    ],
                    axis=1,
                )
                col = (z * 3 + a) * 2 * LANES
                parts = parts + lax.dot_general(
                    left[t, :, col : col + 2 * LANES],
                    right,
                    NT_DIMS,
                    preferred_element_type=F32,
                )
        total = (parts[:left_rows, :columns] + parts[left_rows:, columns:]) + (
            parts[left_rows:, :columns] + parts[:left_rows, columns:]
        )
        for slot, piece in enumerate(pieces):
            for ri in range(2):
                top = slot * rows + ri * vectors
                piece[t, ri] = total[top : top + vectors]


def spread_kernel(dirac16, kept, arrived, out, partial, wide):
    rows, vectors = dirac16.shape[0], dirac16.shape[1]
    if partial is not None:
        partial[...] = kept[...] + arrived[...]
    for r in range(rows):
        wide[pl.ds(r, vectors, stride=rows), :] = dirac16[r].astype(F32)
    out[...] = wide[...].astype(BF16)


def turn_kernel(dirac16, out, wide):
    spread_kernel(dirac16, None, None, out, None, wide)


def final_kernel(partial, other, out):
    times = partial.shape[0]
    width = out.shape[4]
    for t in range(times):
        for ri in range(2):
            total = partial[t, ri] + other[t, ri]
            for p in range(out.shape[0]):
                out[p, t, ri] = total[:, p * width : (p + 1) * width]


def exchange(value, axis):
    size = lax.axis_size(axis)
    up = [(i, (i + 1) % size) for i in range(size)]
    down = [(j, i) for i, j in up]
    before = lax.ppermute(value, axis, up)
    if size == 2:
        return before, before
    return before, lax.ppermute(value, axis, down)


def on_device(eigen_store, fat_links, long_links, chosen, momenta, current_dirs, taste_masks):
    stored, _, _, times, depth, _ = eigen_store.shape
    vectors = chosen.shape[0]
    per_vector = 6 * times * depth
    n_ta, n_gz, n_gy = (lax.axis_size(a) for a in ("ta", "gz", "gy"))
    total_y = (LANES // HALF) * n_gy
    total_z = depth * n_gz

    store = eigen_store.transpose(0, 1, 3, 4, 2, 5).reshape(stored * per_vector, LANES)
    fat = fat_links.transpose(0, 1, 2, 3, 5, 6, 4, 7).reshape(-1, LANES)
    long = long_links.transpose(0, 1, 2, 3, 5, 6, 4, 7).reshape(-1, LANES)
    link_rows = fat.shape[0]
    shape6 = (3, times, depth, 2, vectors, LANES)
    size = per_vector * vectors

    def rows_of(n, dtype=BF16):
        return jax.ShapeDtypeStruct((n, LANES), dtype)

    far_out, packed = call(
        functools.partial(gather_kernel, vectors),
        [rows_of(size + 16), rows_of(size)],
        [HB] * 2,
        [
            pltpu.SMEM(chosen.shape, jnp.int32),
            pltpu.VMEM(store.shape, BF16),
            pltpu.VMEM(store.shape, F32),
            pltpu.VMEM((size, LANES), F32),
            pltpu.SemaphoreType.DMA((2,)),
        ],
        1000,
    )(pinned(chosen), pinned(store))
    near = [(i, i ^ 1) for i in range(n_ta)]
    far = [((i + 1) % n_ta, ((i ^ 1) + 1) % n_ta) for i in range(n_ta)]
    far_field = lax.ppermute(far_out, "ta", far)
    before_z, after_z = exchange(packed, "gz")
    near_field = lax.ppermute(packed, "ta", near)
    y_field, _ = exchange(packed, "gy")

    slots = current_dirs.shape[0]
    count = momenta.shape[0]
    width = depth * 6 * LANES
    left_rows = slots * 2 * vectors
    rotate = n_gz == 2 and n_gy == 2
    scale = 1.0 / math.sqrt(NX * total_y * total_z / 2)
    dacc, back_xy, weights, fatf, longf = call(
        functools.partial(local_kernel, times, depth, vectors, (total_y, total_z, scale)),
        [
            jax.ShapeDtypeStruct(shape6, F32),
            jax.ShapeDtypeStruct((2,) + shape6, F32),
            jax.ShapeDtypeStruct((times * depth, 2 * count, LANES), F32),
            rows_of(link_rows, F32),
            rows_of(link_rows, F32),
        ],
        [HB] * 3 + [VM] * 2,
        [
            pltpu.SMEM((3, count), jnp.int32),
            pltpu.VMEM((link_rows, LANES), BF16),
            pltpu.VMEM((link_rows, LANES), BF16),
            pltpu.VMEM((2, LANES, 4 * LANES), BF16),
            pltpu.VMEM((2 * LANES, 4 * LANES), BF16),
            pltpu.SemaphoreType.DMA((3,)),
        ],
        1000,
    )(pinned(momenta.T), pinned(fat), pinned(long), packed, y_field)
    dacc, left = call(
        functools.partial(side_kernel, times, depth, vectors, rotate),
        [
            jax.ShapeDtypeStruct(shape6, F32),
            jax.ShapeDtypeStruct((times, 2 * left_rows, width), BF16),
        ],
        [HB] * 2 + [VM] * 7,
        [
            pltpu.SMEM((slots,), jnp.int32),
            pltpu.SMEM((slots,), jnp.int32),
            pltpu.VMEM((3,) + shape6, F32),
            pltpu.SemaphoreType.DMA((2,)),
        ],
        1000,
    )(
        pinned(current_dirs), pinned(taste_masks), packed, before_z, after_z, fatf, longf, dacc, back_xy
    )
    piece = jax.ShapeDtypeStruct((times, 2, vectors, count * vectors), F32)
    dirac16, *pieces = call(
        functools.partial(last_kernel, times, depth, vectors),
        [jax.ShapeDtypeStruct(shape6, BF16)] + [piece] * slots,
        [VM] * 7,
        [],
        1000,
    )(far_field, dacc, near_field, fatf, longf, weights, left)

    odd_shape = rows_of(size)
    turned = dirac16.reshape(per_vector, vectors, LANES)
    scratch = [pltpu.VMEM((size, LANES), F32)]
    if rotate:
        swap = [(0, 1), (1, 0)]
        got = lax.ppermute(jnp.stack([pieces[1], pieces[3]]), "gy", swap)
        other = lax.ppermute(pieces[2] + got[1], "gz", swap)
        odd_rows, partial = call(
            spread_kernel, [odd_shape, piece], [VM] * 3, scratch, 1000
        )(turned, pieces[0], got[0])
        meson_shape = jax.ShapeDtypeStruct((count, times, 2, vectors, vectors), F32)
        (meson_fields,) = call(final_kernel, [meson_shape], [VM] * 2, [], 1000)(partial, other)
    else:
        (odd_rows,) = call(turn_kernel, [odd_shape], [VM], scratch, 1000)(turned)
        whole = jnp.stack(pieces).reshape(slots, times, 2, vectors, count, vectors)
        whole = whole.transpose(0, 4, 1, 2, 3, 5).reshape(
            slots * count, times, 2, vectors, vectors
        )
        meson_fields = lax.psum_scatter(whole, ("gz", "gy"), scatter_dimension=0, tiled=True)
    odd_vectors = odd_rows.reshape(vectors, 3, times, depth, 2, LANES).transpose(0, 1, 4, 2, 3, 5)
    return odd_vectors, meson_fields


def solution(mesh):
    in_specs = (
        P(None, None, None, ("cfg", "ta"), "gz", "gy"),
        P(None, None, None, None, None, ("cfg", "ta"), "gz", "gy"),
        P(None, None, None, None, None, ("cfg", "ta"), "gz", "gy"),
        P("cfg"),
        P(),
        P(),
        P(),
    )
    out_specs = (
        P(None, None, None, ("cfg", "ta"), "gz", "gy"),
        P(("gz", "gy"), ("cfg", "ta"), None, None, None),
    )
    return jax.shard_map(
        on_device, mesh=mesh, in_specs=in_specs, out_specs=out_specs, check_vma=False
    )
```

```python
import functools
import math

import jax
import jax.numpy as jnp
from jax import lax
from jax.experimental import pallas as pl
from jax.experimental.pallas import tpu as pltpu
from jax.sharding import PartitionSpec as P

NX = 64
HALF = NX // 2
LANES = 128
F32 = jnp.float32
BF16 = jnp.bfloat16
VM = pl.BlockSpec(memory_space=pltpu.VMEM)
SM = pl.BlockSpec(memory_space=pltpu.SMEM)
HB = pl.BlockSpec(memory_space=pltpu.HBM)


def pinned(value):
    return pltpu.with_memory_space_constraint(value, pltpu.HBM)


def call(body, outs, ins, scratch, cost):
    return pl.pallas_call(
        body,
        out_shape=outs,
        in_specs=ins,
        out_specs=[VM] * len(outs),
        scratch_shapes=scratch,
        compiler_params=pltpu.CompilerParams(vmem_limit_bytes=40 * 1024 * 1024),
        cost_estimate=pl.CostEstimate(flops=cost, bytes_accessed=cost, transcendentals=0),
    )


PIECES = 5


def gather_kernel(
    vectors, chosen_hbm, store_hbm, fat_hbm, long_hbm,
    far, out, fat, long,
    chosen, store, wide, turned, sems,
):
    piece = store.shape[0] // PIECES
    first = pltpu.make_async_copy(chosen_hbm, chosen, sems.at[PIECES])
    first.start()
    copies = []
    for i in range(PIECES):
        part = pl.ds(i * piece, piece)
        copies.append(pltpu.make_async_copy(store_hbm.at[part], store.at[part], sems.at[i]))
    later = [
        pltpu.make_async_copy(fat_hbm, fat, sems.at[PIECES + 1]),
        pltpu.make_async_copy(long_hbm, long, sems.at[PIECES + 2]),
    ]
    for copy in copies + later:
        copy.start()
    for i, copy in enumerate(copies):
        copy.wait()
        wide[i * piece : (i + 1) * piece, :] = store[i * piece : (i + 1) * piece, :].astype(F32)
    first.wait()
    size = out.shape[0]
    rows = size // vectors
    full = rows // 8
    rest = rows - 8 * full
    for n in range(vectors):
        start = chosen[n] * rows
        for q in range(full):
            turned[pl.ds(q * 8 * vectors + n, 8, stride=vectors), :] = wide[
                pl.ds(start + 8 * q, 8), :
            ]
        if rest:
            turned[pl.ds(full * 8 * vectors + n, rest, stride=vectors), :] = wide[
                pl.ds(start + 8 * full, rest), :
            ]
    for r in range(0, size, 16):
        block = turned[r : r + 16, :].astype(BF16)
        out[r : r + 16, :] = block
        far[r : r + 16, :] = block
    far[size:, :] = jnp.zeros((far.shape[0] - size, LANES), BF16)
    for copy in later:
        copy.wait()


class Links:
    def __init__(self, ref, times, depth):
        self.ref, self.times, self.depth = ref, times, depth

    def row(self, w, mu, a, b, t, z, ri):
        at = (((((w * 4 + mu) * 3 + a) * 3 + b) * self.times + t) * self.depth + z) * 2 + ri
        return self.ref[at : at + 1, :]


def add_hop(acc, links, w, mu, t, z, vec, minus):
    for a in range(3):
        for b in range(3):
            lr = links.row(w, mu, a, b, t, z, 0)
            li = links.row(w, mu, a, b, t, z, 1)
            vr, vi = vec[b]
            if minus:
                acc[a][0] = (acc[a][0] - lr * vr) + li * vi
                acc[a][1] = (acc[a][1] - lr * vi) - li * vr
            else:
                acc[a][0] = (acc[a][0] + lr * vr) - li * vi
                acc[a][1] = (acc[a][1] + lr * vi) + li * vr


class Field:
    def __init__(self, ref, times, depth, vectors):
        self.ref, self.times, self.depth, self.vectors = ref, times, depth, vectors

    def raw(self, t, z):
        out = []
        for a in range(3):
            pair = []
            for ri in range(2):
                at = (((a * self.times + t) * self.depth + z) * 2 + ri) * self.vectors
                pair.append(self.ref[at : at + self.vectors, :])
            out.append(pair)
        return out

    def read(self, t, z):
        return widen(self.raw(t, z))

    def stacked(self, t, z):
        return jnp.concatenate([v for pair in self.raw(t, z) for v in pair], axis=0)


def widen(parts):
    return [[v.astype(F32) for v in pair] for pair in parts]


def zeros(vectors):
    return [[jnp.zeros((vectors, LANES), F32) for _ in range(2)] for _ in range(3)]


def read(ref, t, z):
    return [[ref[a, t, z, ri] for ri in range(2)] for a in range(3)]


def write(ref, t, z, acc):
    for a in range(3):
        for ri in range(2):
            ref[a, t, z, ri] = acc[a][ri].astype(ref.dtype)


def subtract(acc, other):
    for a in range(3):
        for ri in range(2):
            acc[a][ri] = acc[a][ri] - other[a][ri]


def split_hops(product, vectors, count):
    out = []
    for h in range(count):
        cols = product[:, h * LANES : (h + 1) * LANES]
        out.append(
            [
                [cols[(a * 2 + ri) * vectors : (a * 2 + ri + 1) * vectors] for ri in range(2)]
                for a in range(3)
            ]
        )
    return out


def x_permutation(e):
    src = lax.broadcasted_iota(jnp.int32, (LANES, 4 * LANES), 0)
    col = lax.broadcasted_iota(jnp.int32, (LANES, 4 * LANES), 1)
    h = col // LANES
    dst = col % LANES
    y = dst // HALF
    k = dst % HALF
    s = (e + y) % 2
    lead = jnp.where(h == 0, 1, jnp.where(h == 1, 0, jnp.where(h == 2, 2, -1)))
    want = y * HALF + (k + lead - s + HALF) % HALF
    return jnp.where(src == want, 1.0, 0.0).astype(BF16)


def y_permutation():
    rows = LANES // HALF
    src = lax.broadcasted_iota(jnp.int32, (2 * LANES, 4 * LANES), 0)
    col = lax.broadcasted_iota(jnp.int32, (2 * LANES, 4 * LANES), 1)
    h = col // LANES
    dst = col % LANES
    y = dst // HALF
    k = dst % HALF
    d = jnp.where(h == 0, 1, jnp.where(h == 1, -1, jnp.where(h == 2, 3, -3)))
    want = ((y + d + 2 * rows) % (2 * rows)) * HALF + k
    return jnp.where(src == want, 1.0, 0.0).astype(BF16)


def local_kernel(
    times, depth, vectors, sizes,
    momenta_hbm, fat, long, field_ref, y_ref,
    dacc, back_xy, weights, fatf, longf,
    momenta, x_perm, y_perm, sem,
):
    total_y, total_z, scale = sizes
    copy = pltpu.make_async_copy(momenta_hbm, momenta, sem)
    copy.start()
    fat_l, long_l = Links(fatf, times, depth), Links(longf, times, depth)
    field = Field(field_ref, times, depth, vectors)
    y_field = Field(y_ref, times, depth, vectors)
    origin = lax.axis_index("ta") * times + lax.axis_index("gz") * depth
    for e in range(2):
        x_perm[e] = x_permutation(origin + e)
    y_perm[...] = y_permutation()
    fatf[...] = fat[...].astype(F32)
    longf[...] = long[...].astype(F32)
    for t in range(times):
        for z in range(depth):
            here = field.stacked(t, z)
            moved = jnp.dot(here, x_perm[(t + z) % 2], preferred_element_type=F32)
            plus1, minus1, plus3, minus3 = split_hops(moved, vectors, 4)
            back = zeros(vectors)
            add_hop(back, fat_l, 1, 3, t, z, minus1, False)
            write(back_xy.at[1], t, z, back)
            acc = [[-v for v in pair] for pair in back]
            add_hop(acc, fat_l, 0, 3, t, z, plus1, False)
            add_hop(acc, long_l, 0, 3, t, z, plus3, False)
            add_hop(acc, long_l, 1, 3, t, z, minus3, True)
            both = jnp.concatenate([here, y_field.stacked(t, z)], axis=1)
            moved = jnp.dot(both, y_perm[...], preferred_element_type=F32)
            plus1, minus1, plus3, minus3 = split_hops(moved, vectors, 4)
            back = zeros(vectors)
            add_hop(back, fat_l, 1, 2, t, z, minus1, False)
            write(back_xy.at[0], t, z, back)
            subtract(acc, back)
            add_hop(acc, fat_l, 0, 2, t, z, plus1, False)
            add_hop(acc, long_l, 0, 2, t, z, plus3, False)
            add_hop(acc, long_l, 1, 2, t, z, minus3, True)
            if t + 1 < times:
                add_hop(acc, fat_l, 0, 0, t, z, field.read(t + 1, z), False)
            if t >= 1:
                add_hop(acc, fat_l, 1, 0, t, z, field.read(t - 1, z), True)
            if z + 1 < depth:
                add_hop(acc, fat_l, 0, 1, t, z, field.read(t, z + 1), False)
            write(dacc, t, z, acc)
    copy.wait()
    count = momenta.shape[1]
    lane = lax.broadcasted_iota(jnp.int32, (count, LANES), 1)
    sub = lax.broadcasted_iota(jnp.int32, (count, LANES), 0)
    y_glob = lax.axis_index("gy") * (LANES // HALF) + lane // HALF
    q = [jnp.zeros((count, LANES), F32) for _ in range(3)]
    for p in range(count):
        for axis in range(3):
            q[axis] = jnp.where(sub == p, momenta[axis, p].astype(F32), q[axis])
    for t in range(times):
        for z in range(depth):
            z_glob = lax.axis_index("gz") * depth + z
            x_glob = 2 * (lane % HALF) + 1 - (origin + t + z + y_glob) % 2
            turns = (
                q[0] * (x_glob.astype(F32) * (1.0 / NX))
                + q[1] * (y_glob.astype(F32) * (1.0 / total_y))
                + q[2] * (z_glob.astype(F32) * (1.0 / total_z))
            )
            cosine, sine = sincos_turns(turns)
            weights[t * depth + z, 0:count] = cosine * scale
            weights[t * depth + z, count : 2 * count] = sine * scale


def halves(value):
    high = value.astype(BF16)
    low = (value - high.astype(F32)).astype(BF16)
    return high, low


def sincos_turns(turns):
    quarters = 4.0 * (turns - jnp.floor(turns + 0.5))
    near = jnp.floor(quarters + 0.5)
    x = (quarters - near) * (0.5 * math.pi)
    x2 = x * x
    s = x * (1.0 + x2 * (-1.0 / 6 + x2 * (1.0 / 120 + x2 * (-1.0 / 5040 + x2 / 362880))))
    c = 1.0 + x2 * (-0.5 + x2 * (1.0 / 24 + x2 * (-1.0 / 720 + x2 * (1.0 / 40320))))
    which = near.astype(jnp.int32) & 3
    odd = (which & 1) == 1
    cosine = jnp.where(odd, s, c)
    sine = jnp.where(odd, c, s)
    cosine = jnp.where((which == 1) | (which == 2), -cosine, cosine)
    sine = jnp.where(which >= 2, -sine, sine)
    return cosine, sine


def side_kernel(
    times, depth, vectors, rotate,
    dirs_hbm, masks_hbm, field_ref, before_ref, after_ref, fatf, longf, dacc_in, back_xy,
    dacc, left,
    dirs, masks, back, sems,
):
    copies = [
        pltpu.make_async_copy(dirs_hbm, dirs, sems.at[0]),
        pltpu.make_async_copy(masks_hbm, masks, sems.at[1]),
    ]
    for copy in copies:
        copy.start()
    fat_l, long_l = Links(fatf, times, depth), Links(longf, times, depth)
    field = Field(field_ref, times, depth, vectors)
    before = Field(before_ref, times, depth, vectors)
    after = Field(after_ref, times, depth, vectors)
    for t in range(times):
        for z in range(depth):
            acc = read(dacc_in, t, z)
            back_z = zeros(vectors)
            source = field.read(t, z - 1) if z >= 1 else before.read(t, depth - 1)
            add_hop(back_z, fat_l, 1, 1, t, z, source, False)
            write(back.at[0], t, z, back_z)
            for d in range(2):
                write(back.at[1 + d], t, z, read(back_xy.at[d], t, z))
            subtract(acc, back_z)
            if z + 1 == depth:
                add_hop(acc, fat_l, 0, 1, t, z, after.read(t, 0), False)
            add_hop(acc, long_l, 0, 1, t, z, after.read(t, z), False)
            add_hop(acc, long_l, 1, 1, t, z, before.read(t, z), True)
            write(dacc, t, z, acc)
    for copy in copies:
        copy.wait()
    slots = dirs.shape[0]
    if rotate:
        gz, gy = lax.axis_index("gz"), lax.axis_index("gy")
        current_of = [((gz + d // 2) % 2) * 2 + (gy + d % 2) % 2 for d in range(slots)]
    else:
        current_of = list(range(slots))
    lane = lax.broadcasted_iota(jnp.int32, (1, LANES), 1)
    y_glob = lax.axis_index("gy") * (LANES // HALF) + lane // HALF
    origin = lax.axis_index("ta") * times + lax.axis_index("gz") * depth
    low_part = slots * 2 * vectors
    for slot in range(slots):
        direction = dirs[current_of[slot]] - 1
        mask = masks[current_of[slot]]
        for t in range(times):
            for z in range(depth):
                z_glob = lax.axis_index("gz") * depth + z
                x_glob = 2 * (lane % HALF) + 1 - (origin + t + z + y_glob) % 2
                exponent = (
                    (mask & 1) * x_glob + ((mask >> 1) & 1) * y_glob + ((mask >> 2) & 1) * z_glob
                )
                sign = (1 - 2 * (exponent & 1)).astype(F32)
                for a in range(3):
                    col = (z * 3 + a) * 2 * LANES
                    first = slice(col, col + LANES)
                    other = slice(col + LANES, col + 2 * LANES)
                    real = halves(back[direction, a, t, z, 0] * sign)
                    imag = halves(back[direction, a, t, z, 1] * sign)
                    for part in range(2):
                        top = part * low_part + slot * 2 * vectors
                        turned = top + vectors
                        left[t, top : top + vectors, first] = real[part]
                        left[t, top : top + vectors, other] = imag[part]
                        left[t, turned : turned + vectors, first] = -imag[part]
                        left[t, turned : turned + vectors, other] = real[part]


NT_DIMS = (((1,), (1,)), ((), ()))


def block_hops(acc, links, field, times, t, z, ahead):
    fat_l, long_l = links
    w = 0 if ahead else 1
    add_hop(acc, long_l, w, 0, t, z, field.read(t, z), not ahead)
    if ahead and t + 1 == times:
        add_hop(acc, fat_l, 0, 0, t, z, field.read(0, z), False)
    if not ahead and t == 0:
        add_hop(acc, fat_l, 1, 0, t, z, field.read(times - 1, z), True)


def time_kernel(times, depth, vectors, near, block_ref, fatf, longf, dacc_in, dacc):
    links = Links(fatf, times, depth), Links(longf, times, depth)
    block = Field(block_ref, times, depth, vectors)
    even = lax.axis_index("ta") % 2 == 0
    for ahead in (True, False):

        @pl.when(even if ahead == near else jnp.logical_not(even))
        def _(ahead=ahead):
            for t in range(times):
                for z in range(depth):
                    acc = read(dacc_in, t, z)
                    block_hops(acc, links, block, times, t, z, ahead)
                    write(dacc, t, z, acc)


def meson_kernel(times, depth, vectors, dacc, weights, left, dirac16, *pieces):
    rows = 2 * vectors
    left_rows = left.shape[1] // 2
    count = weights.shape[1] // 2
    columns = count * vectors
    for t in range(times):
        parts = jnp.zeros((2 * left_rows, 2 * columns), F32)
        for z in range(depth):
            acc = read(dacc, t, z)
            write(dirac16, t, z, acc)
            at = t * depth + z
            for a in range(3):
                real, imag = acc[a]
                right = [[], []]
                for p in range(count):
                    cosine = weights[at, p : p + 1, :]
                    sine = weights[at, count + p : count + p + 1, :]
                    right[0].append(halves(cosine * real + sine * imag))
                    right[1].append(halves(cosine * imag - sine * real))
                right = jnp.concatenate(
                    [
                        jnp.concatenate([h for h, _ in r] + [l for _, l in r], axis=0)
                        for r in right
                    ],
                    axis=1,
                )
                col = (z * 3 + a) * 2 * LANES
                parts = parts + lax.dot_general(
                    left[t, :, col : col + 2 * LANES],
                    right,
                    NT_DIMS,
                    preferred_element_type=F32,
                )
        total = (parts[:left_rows, :columns] + parts[left_rows:, columns:]) + (
            parts[left_rows:, :columns] + parts[:left_rows, columns:]
        )
        for slot, piece in enumerate(pieces):
            for ri in range(2):
                top = slot * rows + ri * vectors
                piece[t, ri] = total[top : top + vectors]


def spread_kernel(dirac16, kept, arrived, out, partial, wide):
    rows, vectors = dirac16.shape[0], dirac16.shape[1]
    if partial is not None:
        partial[...] = kept[...] + arrived[...]
    for r in range(rows):
        wide[pl.ds(r, vectors, stride=rows), :] = dirac16[r].astype(F32)
    out[...] = wide[...].astype(BF16)


def turn_kernel(dirac16, out, wide):
    spread_kernel(dirac16, None, None, out, None, wide)


def final_kernel(partial, other, out):
    times = partial.shape[0]
    width = out.shape[4]
    for t in range(times):
        for ri in range(2):
            total = partial[t, ri] + other[t, ri]
            for p in range(out.shape[0]):
                out[p, t, ri] = total[:, p * width : (p + 1) * width]


def exchange(value, axis):
    size = lax.axis_size(axis)
    up = [(i, (i + 1) % size) for i in range(size)]
    down = [(j, i) for i, j in up]
    before = lax.ppermute(value, axis, up)
    if size == 2:
        return before, before
    return before, lax.ppermute(value, axis, down)


def on_device(eigen_store, fat_links, long_links, chosen, momenta, current_dirs, taste_masks):
    stored, _, _, times, depth, _ = eigen_store.shape
    vectors = chosen.shape[0]
    per_vector = 6 * times * depth
    n_ta, n_gz, n_gy = (lax.axis_size(a) for a in ("ta", "gz", "gy"))
    total_y = (LANES // HALF) * n_gy
    total_z = depth * n_gz

    store = eigen_store.transpose(0, 1, 3, 4, 2, 5).reshape(stored * per_vector, LANES)
    fat = fat_links.transpose(0, 1, 2, 3, 5, 6, 4, 7).reshape(-1, LANES)
    long = long_links.transpose(0, 1, 2, 3, 5, 6, 4, 7).reshape(-1, LANES)
    link_rows = fat.shape[0]
    shape6 = (3, times, depth, 2, vectors, LANES)
    size = per_vector * vectors

    def rows_of(n, dtype=BF16):
        return jax.ShapeDtypeStruct((n, LANES), dtype)

    far_out, packed, fat_v, long_v = call(
        functools.partial(gather_kernel, vectors),
        [rows_of(size + 8), rows_of(size), rows_of(link_rows), rows_of(link_rows)],
        [HB] * 4,
        [
            pltpu.SMEM(chosen.shape, jnp.int32),
            pltpu.VMEM(store.shape, BF16),
            pltpu.VMEM(store.shape, F32),
            pltpu.VMEM((size, LANES), F32),
            pltpu.SemaphoreType.DMA((PIECES + 3,)),
        ],
        1,
    )(*map(pinned, (chosen, store, fat, long)))
    near = [(i, i ^ 1) for i in range(n_ta)]
    far = [((i + 1) % n_ta, ((i ^ 1) + 1) % n_ta) for i in range(n_ta)]
    far_field = lax.ppermute(far_out, "ta", far)
    before_z, after_z = exchange(packed, "gz")
    near_field = lax.ppermute(packed, "ta", near)
    y_field, _ = exchange(packed, "gy")

    slots = current_dirs.shape[0]
    count = momenta.shape[0]
    width = depth * 6 * LANES
    left_rows = slots * 2 * vectors
    rotate = n_gz == 2 and n_gy == 2
    scale = 1.0 / math.sqrt(NX * total_y * total_z / 2)
    dacc, back_xy, weights, fatf, longf = call(
        functools.partial(local_kernel, times, depth, vectors, (total_y, total_z, scale)),
        [
            jax.ShapeDtypeStruct(shape6, F32),
            jax.ShapeDtypeStruct((2,) + shape6, F32),
            jax.ShapeDtypeStruct((times * depth, 2 * count, LANES), F32),
            rows_of(link_rows, F32),
            rows_of(link_rows, F32),
        ],
        [HB] + [VM] * 4,
        [
            pltpu.SMEM((3, count), jnp.int32),
            pltpu.VMEM((2, LANES, 4 * LANES), BF16),
            pltpu.VMEM((2 * LANES, 4 * LANES), BF16),
            pltpu.SemaphoreType.DMA,
        ],
        1,
    )(pinned(momenta.T), fat_v, long_v, packed, y_field)
    dacc, left = call(
        functools.partial(side_kernel, times, depth, vectors, rotate),
        [
            jax.ShapeDtypeStruct(shape6, F32),
            jax.ShapeDtypeStruct((times, 2 * left_rows, width), BF16),
        ],
        [HB] * 2 + [VM] * 7,
        [
            pltpu.SMEM((slots,), jnp.int32),
            pltpu.SMEM((slots,), jnp.int32),
            pltpu.VMEM((3,) + shape6, F32),
            pltpu.SemaphoreType.DMA((2,)),
        ],
        1,
    )(
        pinned(current_dirs), pinned(taste_masks), packed, before_z, after_z, fatf, longf, dacc, back_xy
    )
    piece = jax.ShapeDtypeStruct((times, 2, vectors, count * vectors), F32)
    for block, is_near in ((near_field, True), (far_field, False)):
        (dacc,) = call(
            functools.partial(time_kernel, times, depth, vectors, is_near),
            [jax.ShapeDtypeStruct(shape6, F32)],
            [VM] * 4,
            [],
            1000,
        )(block, fatf, longf, dacc)
    dirac16, *pieces = call(
        functools.partial(meson_kernel, times, depth, vectors),
        [jax.ShapeDtypeStruct(shape6, BF16)] + [piece] * slots,
        [VM] * 3,
        [],
        1,
    )(dacc, weights, left)

    odd_shape = rows_of(size)
    turned = dirac16.reshape(per_vector, vectors, LANES)
    scratch = [pltpu.VMEM((size, LANES), F32)]
    if rotate:
        swap = [(0, 1), (1, 0)]
        got = lax.ppermute(jnp.stack([pieces[1], pieces[3]]), "gy", swap)
        other = lax.ppermute(pieces[2] + got[1], "gz", swap)
        odd_rows, partial = call(
            spread_kernel, [odd_shape, piece], [VM] * 3, scratch, 1
        )(turned, pieces[0], got[0])
        meson_shape = jax.ShapeDtypeStruct((count, times, 2, vectors, vectors), F32)
        (meson_fields,) = call(final_kernel, [meson_shape], [VM] * 2, [], 1)(partial, other)
    else:
        (odd_rows,) = call(turn_kernel, [odd_shape], [VM], scratch, 1)(turned)
        whole = jnp.stack(pieces).reshape(slots, times, 2, vectors, count, vectors)
        whole = whole.transpose(0, 4, 1, 2, 3, 5).reshape(
            slots * count, times, 2, vectors, vectors
        )
        meson_fields = lax.psum_scatter(whole, ("gz", "gy"), scatter_dimension=0, tiled=True)
    odd_vectors = odd_rows.reshape(vectors, 3, times, depth, 2, LANES).transpose(0, 1, 4, 2, 3, 5)
    return odd_vectors, meson_fields


def solution(mesh):
    in_specs = (
        P(None, None, None, ("cfg", "ta"), "gz", "gy"),
        P(None, None, None, None, None, ("cfg", "ta"), "gz", "gy"),
        P(None, None, None, None, None, ("cfg", "ta"), "gz", "gy"),
        P("cfg"),
        P(),
        P(),
        P(),
    )
    out_specs = (
        P(None, None, None, ("cfg", "ta"), "gz", "gy"),
        P(("gz", "gy"), ("cfg", "ta"), None, None, None),
    )
    return jax.shard_map(
        on_device, mesh=mesh, in_specs=in_specs, out_specs=out_specs, check_vma=False
    )
```

```python
import functools
import math

import jax
import jax.numpy as jnp
from jax import lax
from jax.experimental import pallas as pl
from jax.experimental.pallas import tpu as pltpu
from jax.sharding import PartitionSpec as P

NX = 64
HALF = NX // 2
LANES = 128
F32 = jnp.float32
BF16 = jnp.bfloat16
VM = pl.BlockSpec(memory_space=pltpu.VMEM)
SM = pl.BlockSpec(memory_space=pltpu.SMEM)
HB = pl.BlockSpec(memory_space=pltpu.HBM)


def pinned(value):
    return pltpu.with_memory_space_constraint(value, pltpu.HBM)


def call(body, outs, ins, scratch, cost):
    return pl.pallas_call(
        body,
        out_shape=outs,
        in_specs=ins,
        out_specs=[VM] * len(outs),
        scratch_shapes=scratch,
        compiler_params=pltpu.CompilerParams(vmem_limit_bytes=40 * 1024 * 1024),
        cost_estimate=pl.CostEstimate(flops=cost, bytes_accessed=cost, transcendentals=0),
    )


PIECES = 5


def gather_kernel(
    vectors, chosen_hbm, store_hbm, fat_hbm, long_hbm,
    up, down, out, fat, long,
    chosen, store, wide, turned, sems,
):
    piece = store.shape[0] // PIECES
    first = pltpu.make_async_copy(chosen_hbm, chosen, sems.at[PIECES])
    first.start()
    copies = []
    for i in range(PIECES):
        part = pl.ds(i * piece, piece)
        copies.append(pltpu.make_async_copy(store_hbm.at[part], store.at[part], sems.at[i]))
    later = [
        pltpu.make_async_copy(fat_hbm, fat, sems.at[PIECES + 1]),
        pltpu.make_async_copy(long_hbm, long, sems.at[PIECES + 2]),
    ]
    for copy in copies + later:
        copy.start()
    for i, copy in enumerate(copies):
        copy.wait()
        wide[i * piece : (i + 1) * piece, :] = store[i * piece : (i + 1) * piece, :].astype(F32)
    first.wait()
    size = out.shape[0]
    rows = size // vectors
    full = rows // 8
    rest = rows - 8 * full
    for n in range(vectors):
        start = chosen[n] * rows
        for q in range(full):
            turned[pl.ds(q * 8 * vectors + n, 8, stride=vectors), :] = wide[
                pl.ds(start + 8 * q, 8), :
            ]
        if rest:
            turned[pl.ds(full * 8 * vectors + n, rest, stride=vectors), :] = wide[
                pl.ds(start + 8 * full, rest), :
            ]
    for r in range(0, size, 16):
        block = turned[r : r + 16, :].astype(BF16)
        out[r : r + 16, :] = block
        up[r : r + 16, :] = block
        down[r : r + 16, :] = block
    for ref in (up, down):
        ref[size:, :] = jnp.zeros((ref.shape[0] - size, LANES), BF16)
    for copy in later:
        copy.wait()


class Links:
    def __init__(self, ref, times, depth):
        self.ref, self.times, self.depth = ref, times, depth

    def row(self, w, mu, a, b, t, z, ri):
        at = (((((w * 4 + mu) * 3 + a) * 3 + b) * self.times + t) * self.depth + z) * 2 + ri
        return self.ref[at : at + 1, :]


def add_hop(acc, links, w, mu, t, z, vec, minus):
    for a in range(3):
        for b in range(3):
            lr = links.row(w, mu, a, b, t, z, 0)
            li = links.row(w, mu, a, b, t, z, 1)
            vr, vi = vec[b]
            if minus:
                acc[a][0] = (acc[a][0] - lr * vr) + li * vi
                acc[a][1] = (acc[a][1] - lr * vi) - li * vr
            else:
                acc[a][0] = (acc[a][0] + lr * vr) - li * vi
                acc[a][1] = (acc[a][1] + lr * vi) + li * vr


class Field:
    def __init__(self, ref, times, depth, vectors):
        self.ref, self.times, self.depth, self.vectors = ref, times, depth, vectors

    def raw(self, t, z):
        out = []
        for a in range(3):
            pair = []
            for ri in range(2):
                at = (((a * self.times + t) * self.depth + z) * 2 + ri) * self.vectors
                pair.append(self.ref[at : at + self.vectors, :])
            out.append(pair)
        return out

    def read(self, t, z):
        return widen(self.raw(t, z))

    def stacked(self, t, z):
        return jnp.concatenate([v for pair in self.raw(t, z) for v in pair], axis=0)


def widen(parts):
    return [[v.astype(F32) for v in pair] for pair in parts]


def zeros(vectors):
    return [[jnp.zeros((vectors, LANES), F32) for _ in range(2)] for _ in range(3)]


def read(ref, t, z):
    return [[ref[a, t, z, ri] for ri in range(2)] for a in range(3)]


def write(ref, t, z, acc):
    for a in range(3):
        for ri in range(2):
            ref[a, t, z, ri] = acc[a][ri].astype(ref.dtype)


def subtract(acc, other):
    for a in range(3):
        for ri in range(2):
            acc[a][ri] = acc[a][ri] - other[a][ri]


def split_hops(product, vectors, count):
    out = []
    for h in range(count):
        cols = product[:, h * LANES : (h + 1) * LANES]
        out.append(
            [
                [cols[(a * 2 + ri) * vectors : (a * 2 + ri + 1) * vectors] for ri in range(2)]
                for a in range(3)
            ]
        )
    return out


def x_permutation(e):
    src = lax.broadcasted_iota(jnp.int32, (LANES, 4 * LANES), 0)
    col = lax.broadcasted_iota(jnp.int32, (LANES, 4 * LANES), 1)
    h = col // LANES
    dst = col % LANES
    y = dst // HALF
    k = dst % HALF
    s = (e + y) % 2
    lead = jnp.where(h == 0, 1, jnp.where(h == 1, 0, jnp.where(h == 2, 2, -1)))
    want = y * HALF + (k + lead - s + HALF) % HALF
    return jnp.where(src == want, 1.0, 0.0).astype(BF16)


def y_permutation():
    rows = LANES // HALF
    src = lax.broadcasted_iota(jnp.int32, (2 * LANES, 4 * LANES), 0)
    col = lax.broadcasted_iota(jnp.int32, (2 * LANES, 4 * LANES), 1)
    h = col // LANES
    dst = col % LANES
    y = dst // HALF
    k = dst % HALF
    d = jnp.where(h == 0, 1, jnp.where(h == 1, -1, jnp.where(h == 2, 3, -3)))
    want = ((y + d + 2 * rows) % (2 * rows)) * HALF + k
    return jnp.where(src == want, 1.0, 0.0).astype(BF16)


def local_kernel(
    times, depth, vectors, sizes,
    momenta_hbm, fat, long, field_ref, y_ref,
    dacc, back_xy, weights, fatf, longf,
    momenta, x_perm, y_perm, sem,
):
    total_y, total_z, scale = sizes
    copy = pltpu.make_async_copy(momenta_hbm, momenta, sem)
    copy.start()
    fat_l, long_l = Links(fatf, times, depth), Links(longf, times, depth)
    field = Field(field_ref, times, depth, vectors)
    y_field = Field(y_ref, times, depth, vectors)
    origin = lax.axis_index("ta") * times + lax.axis_index("gz") * depth
    for e in range(2):
        x_perm[e] = x_permutation(origin + e)
    y_perm[...] = y_permutation()
    fatf[...] = fat[...].astype(F32)
    longf[...] = long[...].astype(F32)
    for t in range(times):
        for z in range(depth):
            here = field.stacked(t, z)
            moved = jnp.dot(here, x_perm[(t + z) % 2], preferred_element_type=F32)
            plus1, minus1, plus3, minus3 = split_hops(moved, vectors, 4)
            back = zeros(vectors)
            add_hop(back, fat_l, 1, 3, t, z, minus1, False)
            write(back_xy.at[1], t, z, back)
            acc = [[-v for v in pair] for pair in back]
            add_hop(acc, fat_l, 0, 3, t, z, plus1, False)
            add_hop(acc, long_l, 0, 3, t, z, plus3, False)
            add_hop(acc, long_l, 1, 3, t, z, minus3, True)
            both = jnp.concatenate([here, y_field.stacked(t, z)], axis=1)
            moved = jnp.dot(both, y_perm[...], preferred_element_type=F32)
            plus1, minus1, plus3, minus3 = split_hops(moved, vectors, 4)
            back = zeros(vectors)
            add_hop(back, fat_l, 1, 2, t, z, minus1, False)
            write(back_xy.at[0], t, z, back)
            subtract(acc, back)
            add_hop(acc, fat_l, 0, 2, t, z, plus1, False)
            add_hop(acc, long_l, 0, 2, t, z, plus3, False)
            add_hop(acc, long_l, 1, 2, t, z, minus3, True)
            if t + 1 < times:
                add_hop(acc, fat_l, 0, 0, t, z, field.read(t + 1, z), False)
            if t >= 1:
                add_hop(acc, fat_l, 1, 0, t, z, field.read(t - 1, z), True)
            if z + 1 < depth:
                add_hop(acc, fat_l, 0, 1, t, z, field.read(t, z + 1), False)
            write(dacc, t, z, acc)
    copy.wait()
    count = momenta.shape[1]
    lane = lax.broadcasted_iota(jnp.int32, (count, LANES), 1)
    sub = lax.broadcasted_iota(jnp.int32, (count, LANES), 0)
    y_glob = lax.axis_index("gy") * (LANES // HALF) + lane // HALF
    q = [jnp.zeros((count, LANES), F32) for _ in range(3)]
    for p in range(count):
        for axis in range(3):
            q[axis] = jnp.where(sub == p, momenta[axis, p].astype(F32), q[axis])
    for t in range(times):
        for z in range(depth):
            z_glob = lax.axis_index("gz") * depth + z
            x_glob = 2 * (lane % HALF) + 1 - (origin + t + z + y_glob) % 2
            turns = (
                q[0] * (x_glob.astype(F32) * (1.0 / NX))
                + q[1] * (y_glob.astype(F32) * (1.0 / total_y))
                + q[2] * (z_glob.astype(F32) * (1.0 / total_z))
            )
            cosine, sine = sincos_turns(turns)
            weights[t * depth + z, 0:count] = cosine * scale
            weights[t * depth + z, count : 2 * count] = sine * scale


def halves(value):
    high = value.astype(BF16)
    low = (value - high.astype(F32)).astype(BF16)
    return high, low


def sincos_turns(turns):
    quarters = 4.0 * (turns - jnp.floor(turns + 0.5))
    near = jnp.floor(quarters + 0.5)
    x = (quarters - near) * (0.5 * math.pi)
    x2 = x * x
    s = x * (1.0 + x2 * (-1.0 / 6 + x2 * (1.0 / 120 + x2 * (-1.0 / 5040 + x2 / 362880))))
    c = 1.0 + x2 * (-0.5 + x2 * (1.0 / 24 + x2 * (-1.0 / 720 + x2 * (1.0 / 40320))))
    which = near.astype(jnp.int32) & 3
    odd = (which & 1) == 1
    cosine = jnp.where(odd, s, c)
    sine = jnp.where(odd, c, s)
    cosine = jnp.where((which == 1) | (which == 2), -cosine, cosine)
    sine = jnp.where(which >= 2, -sine, sine)
    return cosine, sine


def side_kernel(
    times, depth, vectors, rotate,
    dirs_hbm, masks_hbm, field_ref, before_ref, after_ref, fatf, longf, dacc_in, back_xy,
    dacc, left,
    dirs, masks, back, sems,
):
    copies = [
        pltpu.make_async_copy(dirs_hbm, dirs, sems.at[0]),
        pltpu.make_async_copy(masks_hbm, masks, sems.at[1]),
    ]
    for copy in copies:
        copy.start()
    fat_l, long_l = Links(fatf, times, depth), Links(longf, times, depth)
    field = Field(field_ref, times, depth, vectors)
    before = Field(before_ref, times, depth, vectors)
    after = Field(after_ref, times, depth, vectors)
    for t in range(times):
        for z in range(depth):
            acc = read(dacc_in, t, z)
            back_z = zeros(vectors)
            source = field.read(t, z - 1) if z >= 1 else before.read(t, depth - 1)
            add_hop(back_z, fat_l, 1, 1, t, z, source, False)
            write(back.at[0], t, z, back_z)
            for d in range(2):
                write(back.at[1 + d], t, z, read(back_xy.at[d], t, z))
            subtract(acc, back_z)
            if z + 1 == depth:
                add_hop(acc, fat_l, 0, 1, t, z, after.read(t, 0), False)
            add_hop(acc, long_l, 0, 1, t, z, after.read(t, z), False)
            add_hop(acc, long_l, 1, 1, t, z, before.read(t, z), True)
            write(dacc, t, z, acc)
    for copy in copies:
        copy.wait()
    slots = dirs.shape[0]
    if rotate:
        gz, gy = lax.axis_index("gz"), lax.axis_index("gy")
        current_of = [((gz + d // 2) % 2) * 2 + (gy + d % 2) % 2 for d in range(slots)]
    else:
        current_of = list(range(slots))
    lane = lax.broadcasted_iota(jnp.int32, (1, LANES), 1)
    y_glob = lax.axis_index("gy") * (LANES // HALF) + lane // HALF
    origin = lax.axis_index("ta") * times + lax.axis_index("gz") * depth
    low_part = slots * 2 * vectors
    for slot in range(slots):
        direction = dirs[current_of[slot]] - 1
        mask = masks[current_of[slot]]
        for t in range(times):
            for z in range(depth):
                z_glob = lax.axis_index("gz") * depth + z
                x_glob = 2 * (lane % HALF) + 1 - (origin + t + z + y_glob) % 2
                exponent = (
                    (mask & 1) * x_glob + ((mask >> 1) & 1) * y_glob + ((mask >> 2) & 1) * z_glob
                )
                sign = (1 - 2 * (exponent & 1)).astype(F32)
                for a in range(3):
                    col = (z * 3 + a) * 2 * LANES
                    first = slice(col, col + LANES)
                    other = slice(col + LANES, col + 2 * LANES)
                    real = halves(back[direction, a, t, z, 0] * sign)
                    imag = halves(back[direction, a, t, z, 1] * sign)
                    for part in range(2):
                        top = part * low_part + slot * 2 * vectors
                        turned = top + vectors
                        left[t, top : top + vectors, first] = real[part]
                        left[t, top : top + vectors, other] = imag[part]
                        left[t, turned : turned + vectors, first] = -imag[part]
                        left[t, turned : turned + vectors, other] = real[part]


NT_DIMS = (((1,), (1,)), ((), ()))


def block_hops(acc, links, field, times, t, z, ahead):
    fat_l, long_l = links
    w = 0 if ahead else 1
    add_hop(acc, long_l, w, 0, t, z, field.read(t, z), not ahead)
    if ahead and t + 1 == times:
        add_hop(acc, fat_l, 0, 0, t, z, field.read(0, z), False)
    if not ahead and t == 0:
        add_hop(acc, fat_l, 1, 0, t, z, field.read(times - 1, z), True)


def time_kernel(times, depth, vectors, ahead, block_ref, fatf, longf, dacc_in, dacc):
    links = Links(fatf, times, depth), Links(longf, times, depth)
    block = Field(block_ref, times, depth, vectors)
    for t in range(times):
        for z in range(depth):
            acc = read(dacc_in, t, z)
            block_hops(acc, links, block, times, t, z, ahead)
            write(dacc, t, z, acc)


def meson_kernel(times, depth, vectors, dacc, weights, left, dirac16, *pieces):
    rows = 2 * vectors
    left_rows = left.shape[1] // 2
    count = weights.shape[1] // 2
    columns = count * vectors
    for t in range(times):
        parts = jnp.zeros((2 * left_rows, 2 * columns), F32)
        for z in range(depth):
            acc = read(dacc, t, z)
            write(dirac16, t, z, acc)
            at = t * depth + z
            for a in range(3):
                real, imag = acc[a]
                right = [[], []]
                for p in range(count):
                    cosine = weights[at, p : p + 1, :]
                    sine = weights[at, count + p : count + p + 1, :]
                    right[0].append(halves(cosine * real + sine * imag))
                    right[1].append(halves(cosine * imag - sine * real))
                right = jnp.concatenate(
                    [
                        jnp.concatenate([h for h, _ in r] + [l for _, l in r], axis=0)
                        for r in right
                    ],
                    axis=1,
                )
                col = (z * 3 + a) * 2 * LANES
                parts = parts + lax.dot_general(
                    left[t, :, col : col + 2 * LANES],
                    right,
                    NT_DIMS,
                    preferred_element_type=F32,
                )
        total = (parts[:left_rows, :columns] + parts[left_rows:, columns:]) + (
            parts[left_rows:, :columns] + parts[:left_rows, columns:]
        )
        for slot, piece in enumerate(pieces):
            for ri in range(2):
                top = slot * rows + ri * vectors
                piece[t, ri] = total[top : top + vectors]


def spread_kernel(dirac16, kept, arrived, out, partial, wide):
    rows, vectors = dirac16.shape[0], dirac16.shape[1]
    if partial is not None:
        partial[...] = kept[...] + arrived[...]
    for r in range(rows):
        wide[pl.ds(r, vectors, stride=rows), :] = dirac16[r].astype(F32)
    out[...] = wide[...].astype(BF16)


def turn_kernel(dirac16, out, wide):
    spread_kernel(dirac16, None, None, out, None, wide)


def final_kernel(partial, other, out):
    times = partial.shape[0]
    width = out.shape[4]
    for t in range(times):
        for ri in range(2):
            total = partial[t, ri] + other[t, ri]
            for p in range(out.shape[0]):
                out[p, t, ri] = total[:, p * width : (p + 1) * width]


def exchange(value, axis):
    size = lax.axis_size(axis)
    up = [(i, (i + 1) % size) for i in range(size)]
    down = [(j, i) for i, j in up]
    before = lax.ppermute(value, axis, up)
    if size == 2:
        return before, before
    return before, lax.ppermute(value, axis, down)


def on_device(eigen_store, fat_links, long_links, chosen, momenta, current_dirs, taste_masks):
    stored, _, _, times, depth, _ = eigen_store.shape
    vectors = chosen.shape[0]
    per_vector = 6 * times * depth
    n_ta, n_gz, n_gy = (lax.axis_size(a) for a in ("ta", "gz", "gy"))
    total_y = (LANES // HALF) * n_gy
    total_z = depth * n_gz

    store = eigen_store.transpose(0, 1, 3, 4, 2, 5).reshape(stored * per_vector, LANES)
    fat = fat_links.transpose(0, 1, 2, 3, 5, 6, 4, 7).reshape(-1, LANES)
    long = long_links.transpose(0, 1, 2, 3, 5, 6, 4, 7).reshape(-1, LANES)
    link_rows = fat.shape[0]
    shape6 = (3, times, depth, 2, vectors, LANES)
    size = per_vector * vectors

    def rows_of(n, dtype=BF16):
        return jax.ShapeDtypeStruct((n, LANES), dtype)

    up_out, down_out, packed, fat_v, long_v = call(
        functools.partial(gather_kernel, vectors),
        [
            rows_of(size + 16), rows_of(size + 8), rows_of(size),
            rows_of(link_rows), rows_of(link_rows),
        ],
        [HB] * 4,
        [
            pltpu.SMEM(chosen.shape, jnp.int32),
            pltpu.VMEM(store.shape, BF16),
            pltpu.VMEM(store.shape, F32),
            pltpu.VMEM((size, LANES), F32),
            pltpu.SemaphoreType.DMA((PIECES + 3,)),
        ],
        1,
    )(*map(pinned, (chosen, store, fat, long)))
    up = [(i, (i + 1) % n_ta) for i in range(n_ta)]
    down = [(j, i) for i, j in up]
    before_t = lax.ppermute(up_out, "ta", up)
    after_t = lax.ppermute(down_out, "ta", down)
    before_z, after_z = exchange(packed, "gz")
    y_field, _ = exchange(packed, "gy")

    slots = current_dirs.shape[0]
    count = momenta.shape[0]
    width = depth * 6 * LANES
    left_rows = slots * 2 * vectors
    rotate = n_gz == 2 and n_gy == 2
    scale = 1.0 / math.sqrt(NX * total_y * total_z / 2)
    dacc, back_xy, weights, fatf, longf = call(
        functools.partial(local_kernel, times, depth, vectors, (total_y, total_z, scale)),
        [
            jax.ShapeDtypeStruct(shape6, F32),
            jax.ShapeDtypeStruct((2,) + shape6, F32),
            jax.ShapeDtypeStruct((times * depth, 2 * count, LANES), F32),
            rows_of(link_rows, F32),
            rows_of(link_rows, F32),
        ],
        [HB] + [VM] * 4,
        [
            pltpu.SMEM((3, count), jnp.int32),
            pltpu.VMEM((2, LANES, 4 * LANES), BF16),
            pltpu.VMEM((2 * LANES, 4 * LANES), BF16),
            pltpu.SemaphoreType.DMA,
        ],
        1,
    )(pinned(momenta.T), fat_v, long_v, packed, y_field)
    dacc, left = call(
        functools.partial(side_kernel, times, depth, vectors, rotate),
        [
            jax.ShapeDtypeStruct(shape6, F32),
            jax.ShapeDtypeStruct((times, 2 * left_rows, width), BF16),
        ],
        [HB] * 2 + [VM] * 7,
        [
            pltpu.SMEM((slots,), jnp.int32),
            pltpu.SMEM((slots,), jnp.int32),
            pltpu.VMEM((3,) + shape6, F32),
            pltpu.SemaphoreType.DMA((2,)),
        ],
        1,
    )(
        pinned(current_dirs), pinned(taste_masks), packed, before_z, after_z, fatf, longf, dacc, back_xy
    )
    piece = jax.ShapeDtypeStruct((times, 2, vectors, count * vectors), F32)
    for block, ahead in ((before_t, False), (after_t, True)):
        (dacc,) = call(
            functools.partial(time_kernel, times, depth, vectors, ahead),
            [jax.ShapeDtypeStruct(shape6, F32)],
            [VM] * 4,
            [],
            1000,
        )(block, fatf, longf, dacc)
    dirac16, *pieces = call(
        functools.partial(meson_kernel, times, depth, vectors),
        [jax.ShapeDtypeStruct(shape6, BF16)] + [piece] * slots,
        [VM] * 3,
        [],
        1,
    )(dacc, weights, left)

    odd_shape = rows_of(size)
    turned = dirac16.reshape(per_vector, vectors, LANES)
    scratch = [pltpu.VMEM((size, LANES), F32)]
    if rotate:
        swap = [(0, 1), (1, 0)]
        got = lax.ppermute(jnp.stack([pieces[1], pieces[3]]), "gy", swap)
        other = lax.ppermute(pieces[2] + got[1], "gz", swap)
        odd_rows, partial = call(
            spread_kernel, [odd_shape, piece], [VM] * 3, scratch, 1
        )(turned, pieces[0], got[0])
        meson_shape = jax.ShapeDtypeStruct((count, times, 2, vectors, vectors), F32)
        (meson_fields,) = call(final_kernel, [meson_shape], [VM] * 2, [], 1)(partial, other)
    else:
        (odd_rows,) = call(turn_kernel, [odd_shape], [VM], scratch, 1)(turned)
        whole = jnp.stack(pieces).reshape(slots, times, 2, vectors, count, vectors)
        whole = whole.transpose(0, 4, 1, 2, 3, 5).reshape(
            slots * count, times, 2, vectors, vectors
        )
        meson_fields = lax.psum_scatter(whole, ("gz", "gy"), scatter_dimension=0, tiled=True)
    odd_vectors = odd_rows.reshape(vectors, 3, times, depth, 2, LANES).transpose(0, 1, 4, 2, 3, 5)
    return odd_vectors, meson_fields


def solution(mesh):
    in_specs = (
        P(None, None, None, ("cfg", "ta"), "gz", "gy"),
        P(None, None, None, None, None, ("cfg", "ta"), "gz", "gy"),
        P(None, None, None, None, None, ("cfg", "ta"), "gz", "gy"),
        P("cfg"),
        P(),
        P(),
        P(),
    )
    out_specs = (
        P(None, None, None, ("cfg", "ta"), "gz", "gy"),
        P(("gz", "gy"), ("cfg", "ta"), None, None, None),
    )
    return jax.shard_map(
        on_device, mesh=mesh, in_specs=in_specs, out_specs=out_specs, check_vma=False
    )
```

```python
import functools
import math

import jax
import jax.numpy as jnp
from jax import lax
from jax.experimental import pallas as pl
from jax.experimental.pallas import tpu as pltpu
from jax.sharding import PartitionSpec as P

NX = 64
HALF = NX // 2
LANES = 128
F32 = jnp.float32
BF16 = jnp.bfloat16
VM = pl.BlockSpec(memory_space=pltpu.VMEM)
SM = pl.BlockSpec(memory_space=pltpu.SMEM)
HB = pl.BlockSpec(memory_space=pltpu.HBM)


def pinned(value):
    return pltpu.with_memory_space_constraint(value, pltpu.HBM)


def call(body, outs, ins, scratch, cost):
    return pl.pallas_call(
        body,
        out_shape=outs,
        in_specs=ins,
        out_specs=[VM] * len(outs),
        scratch_shapes=scratch,
        compiler_params=pltpu.CompilerParams(vmem_limit_bytes=40 * 1024 * 1024),
        cost_estimate=pl.CostEstimate(flops=cost, bytes_accessed=cost, transcendentals=0),
    )


PIECES = 5


def gather_kernel(
    times, depth, vectors, chosen_hbm, store_hbm, fat_hbm, long_hbm,
    up, down, last, out, fat, long,
    chosen, store, wide, turned, sems,
):
    piece = store.shape[0] // PIECES
    first = pltpu.make_async_copy(chosen_hbm, chosen, sems.at[PIECES])
    first.start()
    copies = []
    for i in range(PIECES):
        part = pl.ds(i * piece, piece)
        copies.append(pltpu.make_async_copy(store_hbm.at[part], store.at[part], sems.at[i]))
    later = [
        pltpu.make_async_copy(fat_hbm, fat, sems.at[PIECES + 1]),
        pltpu.make_async_copy(long_hbm, long, sems.at[PIECES + 2]),
    ]
    for copy in copies + later:
        copy.start()
    for i, copy in enumerate(copies):
        copy.wait()
        wide[i * piece : (i + 1) * piece, :] = store[i * piece : (i + 1) * piece, :].astype(F32)
    first.wait()
    size = out.shape[0]
    rows = size // vectors
    full = rows // 8
    rest = rows - 8 * full
    for n in range(vectors):
        start = chosen[n] * rows
        for q in range(full):
            turned[pl.ds(q * 8 * vectors + n, 8, stride=vectors), :] = wide[
                pl.ds(start + 8 * q, 8), :
            ]
        if rest:
            turned[pl.ds(full * 8 * vectors + n, rest, stride=vectors), :] = wide[
                pl.ds(start + 8 * full, rest), :
            ]
    layer = depth * 2 * vectors
    for a in range(3):
        for t in range(times):
            source = (a * times + t) * layer
            block = turned[source : source + layer, :].astype(BF16)
            out[source : source + layer, :] = block
            up[source : source + layer, :] = block
            if t + 1 < times:
                target = (a * (times - 1) + t) * layer
                down[target : target + layer, :] = block
            else:
                last[a * layer : (a + 1) * layer, :] = block
    up[size:, :] = jnp.zeros((up.shape[0] - size, LANES), BF16)
    for copy in later:
        copy.wait()


class Links:
    def __init__(self, ref, times, depth):
        self.ref, self.times, self.depth = ref, times, depth

    def row(self, w, mu, a, b, t, z, ri):
        at = (((((w * 4 + mu) * 3 + a) * 3 + b) * self.times + t) * self.depth + z) * 2 + ri
        return self.ref[at : at + 1, :]


def add_hop(acc, links, w, mu, t, z, vec, minus):
    for a in range(3):
        for b in range(3):
            lr = links.row(w, mu, a, b, t, z, 0)
            li = links.row(w, mu, a, b, t, z, 1)
            vr, vi = vec[b]
            if minus:
                acc[a][0] = (acc[a][0] - lr * vr) + li * vi
                acc[a][1] = (acc[a][1] - lr * vi) - li * vr
            else:
                acc[a][0] = (acc[a][0] + lr * vr) - li * vi
                acc[a][1] = (acc[a][1] + lr * vi) + li * vr


class Field:
    def __init__(self, ref, times, depth, vectors):
        self.ref, self.times, self.depth, self.vectors = ref, times, depth, vectors

    def raw(self, t, z):
        out = []
        for a in range(3):
            pair = []
            for ri in range(2):
                at = (((a * self.times + t) * self.depth + z) * 2 + ri) * self.vectors
                pair.append(self.ref[at : at + self.vectors, :])
            out.append(pair)
        return out

    def read(self, t, z):
        return widen(self.raw(t, z))

    def stacked(self, t, z):
        return jnp.concatenate([v for pair in self.raw(t, z) for v in pair], axis=0)


def widen(parts):
    return [[v.astype(F32) for v in pair] for pair in parts]


def zeros(vectors):
    return [[jnp.zeros((vectors, LANES), F32) for _ in range(2)] for _ in range(3)]


def read(ref, t, z):
    return [[ref[a, t, z, ri] for ri in range(2)] for a in range(3)]


def write(ref, t, z, acc):
    for a in range(3):
        for ri in range(2):
            ref[a, t, z, ri] = acc[a][ri].astype(ref.dtype)


def subtract(acc, other):
    for a in range(3):
        for ri in range(2):
            acc[a][ri] = acc[a][ri] - other[a][ri]


def split_hops(product, vectors, count):
    out = []
    for h in range(count):
        cols = product[:, h * LANES : (h + 1) * LANES]
        out.append(
            [
                [cols[(a * 2 + ri) * vectors : (a * 2 + ri + 1) * vectors] for ri in range(2)]
                for a in range(3)
            ]
        )
    return out


def x_permutation(e):
    src = lax.broadcasted_iota(jnp.int32, (LANES, 4 * LANES), 0)
    col = lax.broadcasted_iota(jnp.int32, (LANES, 4 * LANES), 1)
    h = col // LANES
    dst = col % LANES
    y = dst // HALF
    k = dst % HALF
    s = (e + y) % 2
    lead = jnp.where(h == 0, 1, jnp.where(h == 1, 0, jnp.where(h == 2, 2, -1)))
    want = y * HALF + (k + lead - s + HALF) % HALF
    return jnp.where(src == want, 1.0, 0.0).astype(BF16)


def y_permutation():
    rows = LANES // HALF
    src = lax.broadcasted_iota(jnp.int32, (2 * LANES, 4 * LANES), 0)
    col = lax.broadcasted_iota(jnp.int32, (2 * LANES, 4 * LANES), 1)
    h = col // LANES
    dst = col % LANES
    y = dst // HALF
    k = dst % HALF
    d = jnp.where(h == 0, 1, jnp.where(h == 1, -1, jnp.where(h == 2, 3, -3)))
    want = ((y + d + 2 * rows) % (2 * rows)) * HALF + k
    return jnp.where(src == want, 1.0, 0.0).astype(BF16)


def local_kernel(
    times, depth, vectors, sizes,
    momenta_hbm, fat, long, field_ref, y_ref,
    dacc, back_xy, weights, fatf, longf,
    momenta, x_perm, y_perm, sem,
):
    total_y, total_z, scale = sizes
    copy = pltpu.make_async_copy(momenta_hbm, momenta, sem)
    copy.start()
    fat_l, long_l = Links(fatf, times, depth), Links(longf, times, depth)
    field = Field(field_ref, times, depth, vectors)
    y_field = Field(y_ref, times, depth, vectors)
    origin = lax.axis_index("ta") * times + lax.axis_index("gz") * depth
    for e in range(2):
        x_perm[e] = x_permutation(origin + e)
    y_perm[...] = y_permutation()
    fatf[...] = fat[...].astype(F32)
    longf[...] = long[...].astype(F32)
    for t in range(times):
        for z in range(depth):
            here = field.stacked(t, z)
            moved = jnp.dot(here, x_perm[(t + z) % 2], preferred_element_type=F32)
            plus1, minus1, plus3, minus3 = split_hops(moved, vectors, 4)
            back = zeros(vectors)
            add_hop(back, fat_l, 1, 3, t, z, minus1, False)
            write(back_xy.at[1], t, z, back)
            acc = [[-v for v in pair] for pair in back]
            add_hop(acc, fat_l, 0, 3, t, z, plus1, False)
            add_hop(acc, long_l, 0, 3, t, z, plus3, False)
            add_hop(acc, long_l, 1, 3, t, z, minus3, True)
            both = jnp.concatenate([here, y_field.stacked(t, z)], axis=1)
            moved = jnp.dot(both, y_perm[...], preferred_element_type=F32)
            plus1, minus1, plus3, minus3 = split_hops(moved, vectors, 4)
            back = zeros(vectors)
            add_hop(back, fat_l, 1, 2, t, z, minus1, False)
            write(back_xy.at[0], t, z, back)
            subtract(acc, back)
            add_hop(acc, fat_l, 0, 2, t, z, plus1, False)
            add_hop(acc, long_l, 0, 2, t, z, plus3, False)
            add_hop(acc, long_l, 1, 2, t, z, minus3, True)
            if t + 1 < times:
                add_hop(acc, fat_l, 0, 0, t, z, field.read(t + 1, z), False)
            if t >= 1:
                add_hop(acc, fat_l, 1, 0, t, z, field.read(t - 1, z), True)
            if z + 1 < depth:
                add_hop(acc, fat_l, 0, 1, t, z, field.read(t, z + 1), False)
            write(dacc, t, z, acc)
    copy.wait()
    count = momenta.shape[1]
    lane = lax.broadcasted_iota(jnp.int32, (count, LANES), 1)
    sub = lax.broadcasted_iota(jnp.int32, (count, LANES), 0)
    y_glob = lax.axis_index("gy") * (LANES // HALF) + lane // HALF
    q = [jnp.zeros((count, LANES), F32) for _ in range(3)]
    for p in range(count):
        for axis in range(3):
            q[axis] = jnp.where(sub == p, momenta[axis, p].astype(F32), q[axis])
    for t in range(times):
        for z in range(depth):
            z_glob = lax.axis_index("gz") * depth + z
            x_glob = 2 * (lane % HALF) + 1 - (origin + t + z + y_glob) % 2
            turns = (
                q[0] * (x_glob.astype(F32) * (1.0 / NX))
                + q[1] * (y_glob.astype(F32) * (1.0 / total_y))
                + q[2] * (z_glob.astype(F32) * (1.0 / total_z))
            )
            cosine, sine = sincos_turns(turns)
            weights[t * depth + z, 0:count] = cosine * scale
            weights[t * depth + z, count : 2 * count] = sine * scale


def halves(value):
    high = value.astype(BF16)
    low = (value - high.astype(F32)).astype(BF16)
    return high, low


def sincos_turns(turns):
    quarters = 4.0 * (turns - jnp.floor(turns + 0.5))
    near = jnp.floor(quarters + 0.5)
    x = (quarters - near) * (0.5 * math.pi)
    x2 = x * x
    s = x * (1.0 + x2 * (-1.0 / 6 + x2 * (1.0 / 120 + x2 * (-1.0 / 5040 + x2 / 362880))))
    c = 1.0 + x2 * (-0.5 + x2 * (1.0 / 24 + x2 * (-1.0 / 720 + x2 * (1.0 / 40320))))
    which = near.astype(jnp.int32) & 3
    odd = (which & 1) == 1
    cosine = jnp.where(odd, s, c)
    sine = jnp.where(odd, c, s)
    cosine = jnp.where((which == 1) | (which == 2), -cosine, cosine)
    sine = jnp.where(which >= 2, -sine, sine)
    return cosine, sine


def side_kernel(
    times, depth, vectors, rotate,
    dirs_hbm, masks_hbm, field_ref, before_ref, after_ref, fatf, longf, dacc_in, back_xy,
    dacc, left,
    dirs, masks, back, sems,
):
    copies = [
        pltpu.make_async_copy(dirs_hbm, dirs, sems.at[0]),
        pltpu.make_async_copy(masks_hbm, masks, sems.at[1]),
    ]
    for copy in copies:
        copy.start()
    fat_l, long_l = Links(fatf, times, depth), Links(longf, times, depth)
    field = Field(field_ref, times, depth, vectors)
    before = Field(before_ref, times, depth, vectors)
    after = Field(after_ref, times, depth, vectors)
    for t in range(times):
        for z in range(depth):
            acc = read(dacc_in, t, z)
            back_z = zeros(vectors)
            source = field.read(t, z - 1) if z >= 1 else before.read(t, depth - 1)
            add_hop(back_z, fat_l, 1, 1, t, z, source, False)
            write(back.at[0], t, z, back_z)
            for d in range(2):
                write(back.at[1 + d], t, z, read(back_xy.at[d], t, z))
            subtract(acc, back_z)
            if z + 1 == depth:
                add_hop(acc, fat_l, 0, 1, t, z, after.read(t, 0), False)
            add_hop(acc, long_l, 0, 1, t, z, after.read(t, z), False)
            add_hop(acc, long_l, 1, 1, t, z, before.read(t, z), True)
            write(dacc, t, z, acc)
    for copy in copies:
        copy.wait()
    slots = dirs.shape[0]
    if rotate:
        gz, gy = lax.axis_index("gz"), lax.axis_index("gy")
        current_of = [((gz + d // 2) % 2) * 2 + (gy + d % 2) % 2 for d in range(slots)]
    else:
        current_of = list(range(slots))
    lane = lax.broadcasted_iota(jnp.int32, (1, LANES), 1)
    y_glob = lax.axis_index("gy") * (LANES // HALF) + lane // HALF
    origin = lax.axis_index("ta") * times + lax.axis_index("gz") * depth
    low_part = slots * 2 * vectors
    for slot in range(slots):
        direction = dirs[current_of[slot]] - 1
        mask = masks[current_of[slot]]
        for t in range(times):
            for z in range(depth):
                z_glob = lax.axis_index("gz") * depth + z
                x_glob = 2 * (lane % HALF) + 1 - (origin + t + z + y_glob) % 2
                exponent = (
                    (mask & 1) * x_glob + ((mask >> 1) & 1) * y_glob + ((mask >> 2) & 1) * z_glob
                )
                sign = (1 - 2 * (exponent & 1)).astype(F32)
                for a in range(3):
                    col = (z * 3 + a) * 2 * LANES
                    first = slice(col, col + LANES)
                    other = slice(col + LANES, col + 2 * LANES)
                    real = halves(back[direction, a, t, z, 0] * sign)
                    imag = halves(back[direction, a, t, z, 1] * sign)
                    for part in range(2):
                        top = part * low_part + slot * 2 * vectors
                        turned = top + vectors
                        left[t, top : top + vectors, first] = real[part]
                        left[t, top : top + vectors, other] = imag[part]
                        left[t, turned : turned + vectors, first] = -imag[part]
                        left[t, turned : turned + vectors, other] = real[part]


NT_DIMS = (((1,), (1,)), ((), ()))


def before_kernel(times, depth, vectors, block_ref, fatf, longf, dacc_in, dacc):
    fat_l, long_l = Links(fatf, times, depth), Links(longf, times, depth)
    block = Field(block_ref, times, depth, vectors)
    for t in range(times):
        for z in range(depth):
            acc = read(dacc_in, t, z)
            add_hop(acc, long_l, 1, 0, t, z, block.read(t, z), True)
            if t == 0:
                add_hop(acc, fat_l, 1, 0, t, z, block.read(times - 1, z), True)
            write(dacc, t, z, acc)


def meson_slice(t, layers, weights, left, pieces, vectors):
    rows = 2 * vectors
    left_rows = left.shape[1] // 2
    count = weights.shape[1] // 2
    columns = count * vectors
    parts = jnp.zeros((2 * left_rows, 2 * columns), F32)
    depth = len(layers)
    for z, acc in enumerate(layers):
        at = t * depth + z
        for a in range(3):
            real, imag = acc[a]
            right = [[], []]
            for p in range(count):
                cosine = weights[at, p : p + 1, :]
                sine = weights[at, count + p : count + p + 1, :]
                right[0].append(halves(cosine * real + sine * imag))
                right[1].append(halves(cosine * imag - sine * real))
            right = jnp.concatenate(
                [jnp.concatenate([h for h, _ in r] + [l for _, l in r], axis=0) for r in right],
                axis=1,
            )
            col = (z * 3 + a) * 2 * LANES
            parts = parts + lax.dot_general(
                left[t, :, col : col + 2 * LANES], right, NT_DIMS, preferred_element_type=F32
            )
    total = (parts[:left_rows, :columns] + parts[left_rows:, columns:]) + (
        parts[left_rows:, :columns] + parts[:left_rows, columns:]
    )
    for slot, piece in enumerate(pieces):
        for ri in range(2):
            top = slot * rows + ri * vectors
            piece[t, ri] = total[top : top + vectors]


def early_kernel(
    times, depth, vectors,
    block_ref, fatf, longf, dacc, weights, left,
    edge, dirac16, *pieces,
):
    fat_l, long_l = Links(fatf, times, depth), Links(longf, times, depth)
    block = Field(block_ref, times - 1, depth, vectors)
    for z in range(depth):
        acc = read(dacc, times - 1, z)
        add_hop(acc, fat_l, 0, 0, times - 1, z, block.read(0, z), False)
        write(edge, 0, z, acc)
    for t in range(times - 1):
        layers = []
        for z in range(depth):
            acc = read(dacc, t, z)
            add_hop(acc, long_l, 0, 0, t, z, block.read(t, z), False)
            write(dirac16, t, z, acc)
            layers.append(acc)
        meson_slice(t, layers, weights, left, pieces, vectors)


def late_kernel(
    times, depth, vectors,
    block_ref, longf, edge, weights, left, dirac16_in, *rest,
):
    slots = len(rest) // 2
    pieces_in, dirac16, pieces = rest[:slots], rest[slots], rest[slots + 1 :]
    long_l = Links(longf, times, depth)
    block = Field(block_ref, 1, depth, vectors)
    layers = []
    for z in range(depth):
        acc = read(edge, 0, z)
        add_hop(acc, long_l, 0, 0, times - 1, z, block.read(0, z), False)
        write(dirac16, times - 1, z, acc)
        layers.append(acc)
    meson_slice(times - 1, layers, weights, left, pieces, vectors)
    for t in range(times - 1):
        dirac16[:, t] = dirac16_in[:, t]
        for source, piece in zip(pieces_in, pieces):
            piece[t] = source[t]


def spread_kernel(dirac16, kept, arrived, out, partial, wide):
    rows, vectors = dirac16.shape[0], dirac16.shape[1]
    if partial is not None:
        partial[...] = kept[...] + arrived[...]
    for r in range(rows):
        wide[pl.ds(r, vectors, stride=rows), :] = dirac16[r].astype(F32)
    out[...] = wide[...].astype(BF16)


def turn_kernel(dirac16, out, wide):
    spread_kernel(dirac16, None, None, out, None, wide)


def final_kernel(partial, other, out):
    times = partial.shape[0]
    width = out.shape[4]
    for t in range(times):
        for ri in range(2):
            total = partial[t, ri] + other[t, ri]
            for p in range(out.shape[0]):
                out[p, t, ri] = total[:, p * width : (p + 1) * width]


def exchange(value, axis):
    size = lax.axis_size(axis)
    up = [(i, (i + 1) % size) for i in range(size)]
    down = [(j, i) for i, j in up]
    before = lax.ppermute(value, axis, up)
    if size == 2:
        return before, before
    return before, lax.ppermute(value, axis, down)


def on_device(eigen_store, fat_links, long_links, chosen, momenta, current_dirs, taste_masks):
    stored, _, _, times, depth, _ = eigen_store.shape
    vectors = chosen.shape[0]
    per_vector = 6 * times * depth
    n_ta, n_gz, n_gy = (lax.axis_size(a) for a in ("ta", "gz", "gy"))
    total_y = (LANES // HALF) * n_gy
    total_z = depth * n_gz

    store = eigen_store.transpose(0, 1, 3, 4, 2, 5).reshape(stored * per_vector, LANES)
    fat = fat_links.transpose(0, 1, 2, 3, 5, 6, 4, 7).reshape(-1, LANES)
    long = long_links.transpose(0, 1, 2, 3, 5, 6, 4, 7).reshape(-1, LANES)
    link_rows = fat.shape[0]
    shape6 = (3, times, depth, 2, vectors, LANES)
    size = per_vector * vectors

    def rows_of(n, dtype=BF16):
        return jax.ShapeDtypeStruct((n, LANES), dtype)

    last_size = size // times
    up_out, down_out, last_out, packed, fat_v, long_v = call(
        functools.partial(gather_kernel, times, depth, vectors),
        [
            rows_of(size + 16), rows_of(size - last_size), rows_of(last_size), rows_of(size),
            rows_of(link_rows), rows_of(link_rows),
        ],
        [HB] * 4,
        [
            pltpu.SMEM(chosen.shape, jnp.int32),
            pltpu.VMEM(store.shape, BF16),
            pltpu.VMEM(store.shape, F32),
            pltpu.VMEM((size, LANES), F32),
            pltpu.SemaphoreType.DMA((PIECES + 3,)),
        ],
        1,
    )(*map(pinned, (chosen, store, fat, long)))
    up = [(i, (i + 1) % n_ta) for i in range(n_ta)]
    down = [(j, i) for i, j in up]
    before_t = lax.ppermute(up_out, "ta", up)
    after_t = lax.ppermute(down_out, "ta", down)
    after_last = lax.ppermute(last_out, "ta", down)
    before_z, after_z = exchange(packed, "gz")
    y_field, _ = exchange(packed, "gy")

    slots = current_dirs.shape[0]
    count = momenta.shape[0]
    width = depth * 6 * LANES
    left_rows = slots * 2 * vectors
    rotate = n_gz == 2 and n_gy == 2
    scale = 1.0 / math.sqrt(NX * total_y * total_z / 2)
    dacc, back_xy, weights, fatf, longf = call(
        functools.partial(local_kernel, times, depth, vectors, (total_y, total_z, scale)),
        [
            jax.ShapeDtypeStruct(shape6, F32),
            jax.ShapeDtypeStruct((2,) + shape6, F32),
            jax.ShapeDtypeStruct((times * depth, 2 * count, LANES), F32),
            rows_of(link_rows, F32),
            rows_of(link_rows, F32),
        ],
        [HB] + [VM] * 4,
        [
            pltpu.SMEM((3, count), jnp.int32),
            pltpu.VMEM((2, LANES, 4 * LANES), BF16),
            pltpu.VMEM((2 * LANES, 4 * LANES), BF16),
            pltpu.SemaphoreType.DMA,
        ],
        1,
    )(pinned(momenta.T), fat_v, long_v, packed, y_field)
    dacc, left = call(
        functools.partial(side_kernel, times, depth, vectors, rotate),
        [
            jax.ShapeDtypeStruct(shape6, F32),
            jax.ShapeDtypeStruct((times, 2 * left_rows, width), BF16),
        ],
        [HB] * 2 + [VM] * 7,
        [
            pltpu.SMEM((slots,), jnp.int32),
            pltpu.SMEM((slots,), jnp.int32),
            pltpu.VMEM((3,) + shape6, F32),
            pltpu.SemaphoreType.DMA((2,)),
        ],
        1,
    )(
        pinned(current_dirs), pinned(taste_masks), packed, before_z, after_z, fatf, longf, dacc, back_xy
    )
    piece = jax.ShapeDtypeStruct((times, 2, vectors, count * vectors), F32)
    (dacc,) = call(
        functools.partial(before_kernel, times, depth, vectors),
        [jax.ShapeDtypeStruct(shape6, F32)],
        [VM] * 4,
        [],
        1,
    )(before_t, fatf, longf, dacc)
    finished = [jax.ShapeDtypeStruct(shape6, BF16)] + [piece] * slots
    edge, *early = call(
        functools.partial(early_kernel, times, depth, vectors),
        [jax.ShapeDtypeStruct((3, 1) + shape6[2:], F32)] + finished,
        [VM] * 6,
        [],
        1,
    )(after_t, fatf, longf, dacc, weights, left)
    dirac16, *pieces = call(
        functools.partial(late_kernel, times, depth, vectors),
        finished,
        [VM] * (6 + slots),
        [],
        1,
    )(after_last, longf, edge, weights, left, *early)

    odd_shape = rows_of(size)
    turned = dirac16.reshape(per_vector, vectors, LANES)
    scratch = [pltpu.VMEM((size, LANES), F32)]
    if rotate:
        swap = [(0, 1), (1, 0)]
        got = lax.ppermute(jnp.stack([pieces[1], pieces[3]]), "gy", swap)
        other = lax.ppermute(pieces[2] + got[1], "gz", swap)
        odd_rows, partial = call(
            spread_kernel, [odd_shape, piece], [VM] * 3, scratch, 1
        )(turned, pieces[0], got[0])
        meson_shape = jax.ShapeDtypeStruct((count, times, 2, vectors, vectors), F32)
        (meson_fields,) = call(final_kernel, [meson_shape], [VM] * 2, [], 1)(partial, other)
    else:
        (odd_rows,) = call(turn_kernel, [odd_shape], [VM], scratch, 1)(turned)
        whole = jnp.stack(pieces).reshape(slots, times, 2, vectors, count, vectors)
        whole = whole.transpose(0, 4, 1, 2, 3, 5).reshape(
            slots * count, times, 2, vectors, vectors
        )
        meson_fields = lax.psum_scatter(whole, ("gz", "gy"), scatter_dimension=0, tiled=True)
    odd_vectors = odd_rows.reshape(vectors, 3, times, depth, 2, LANES).transpose(0, 1, 4, 2, 3, 5)
    return odd_vectors, meson_fields


def solution(mesh):
    in_specs = (
        P(None, None, None, ("cfg", "ta"), "gz", "gy"),
        P(None, None, None, None, None, ("cfg", "ta"), "gz", "gy"),
        P(None, None, None, None, None, ("cfg", "ta"), "gz", "gy"),
        P("cfg"),
        P(),
        P(),
        P(),
    )
    out_specs = (
        P(None, None, None, ("cfg", "ta"), "gz", "gy"),
        P(("gz", "gy"), ("cfg", "ta"), None, None, None),
    )
    return jax.shard_map(
        on_device, mesh=mesh, in_specs=in_specs, out_specs=out_specs, check_vma=False
    )
```

```python
import functools
import math

import jax
import jax.numpy as jnp
from jax import lax
from jax.experimental import pallas as pl
from jax.experimental.pallas import tpu as pltpu
from jax.sharding import PartitionSpec as P

NX = 64
HALF = NX // 2
LANES = 128
F32 = jnp.float32
BF16 = jnp.bfloat16
VM = pl.BlockSpec(memory_space=pltpu.VMEM)
SM = pl.BlockSpec(memory_space=pltpu.SMEM)
HB = pl.BlockSpec(memory_space=pltpu.HBM)


def pinned(value):
    return pltpu.with_memory_space_constraint(value, pltpu.HBM)


def call(body, outs, ins, scratch, cost):
    return pl.pallas_call(
        body,
        out_shape=outs,
        in_specs=ins,
        out_specs=[VM] * len(outs),
        scratch_shapes=scratch,
        compiler_params=pltpu.CompilerParams(vmem_limit_bytes=40 * 1024 * 1024),
        cost_estimate=pl.CostEstimate(flops=cost, bytes_accessed=cost, transcendentals=0),
    )


PIECES = 5


def gather_kernel(
    times, depth, vectors, chosen_hbm, store_hbm, fat_hbm, long_hbm,
    up, down, last, out, fat, long,
    chosen, store, wide, turned, sems,
):
    piece = store.shape[0] // PIECES
    first = pltpu.make_async_copy(chosen_hbm, chosen, sems.at[PIECES])
    first.start()
    copies = []
    for i in range(PIECES):
        part = pl.ds(i * piece, piece)
        copies.append(pltpu.make_async_copy(store_hbm.at[part], store.at[part], sems.at[i]))
    later = [
        pltpu.make_async_copy(fat_hbm, fat, sems.at[PIECES + 1]),
        pltpu.make_async_copy(long_hbm, long, sems.at[PIECES + 2]),
    ]
    for copy in copies + later:
        copy.start()
    for i, copy in enumerate(copies):
        copy.wait()
        wide[i * piece : (i + 1) * piece, :] = store[i * piece : (i + 1) * piece, :].astype(F32)
    first.wait()
    size = out.shape[0]
    rows = size // vectors
    full = rows // 8
    rest = rows - 8 * full
    for n in range(vectors):
        start = chosen[n] * rows
        for q in range(full):
            turned[pl.ds(q * 8 * vectors + n, 8, stride=vectors), :] = wide[
                pl.ds(start + 8 * q, 8), :
            ]
        if rest:
            turned[pl.ds(full * 8 * vectors + n, rest, stride=vectors), :] = wide[
                pl.ds(start + 8 * full, rest), :
            ]
    layer = depth * 2 * vectors
    for a in range(3):
        for t in range(times):
            source = (a * times + t) * layer
            block = turned[source : source + layer, :].astype(BF16)
            out[source : source + layer, :] = block
            up[source : source + layer, :] = block
            if t + 1 < times:
                target = (a * (times - 1) + t) * layer
                down[target : target + layer, :] = block
            else:
                last[a * layer : (a + 1) * layer, :] = block
    up[size:, :] = jnp.zeros((up.shape[0] - size, LANES), BF16)
    for copy in later:
        copy.wait()


class Links:
    def __init__(self, ref, times, depth):
        self.ref, self.times, self.depth = ref, times, depth

    def row(self, w, mu, a, b, t, z, ri):
        at = (((((w * 4 + mu) * 3 + a) * 3 + b) * self.times + t) * self.depth + z) * 2 + ri
        return self.ref[at : at + 1, :]


def add_hop(acc, links, w, mu, t, z, vec, minus):
    for a in range(3):
        for b in range(3):
            lr = links.row(w, mu, a, b, t, z, 0)
            li = links.row(w, mu, a, b, t, z, 1)
            vr, vi = vec[b]
            if minus:
                acc[a][0] = (acc[a][0] - lr * vr) + li * vi
                acc[a][1] = (acc[a][1] - lr * vi) - li * vr
            else:
                acc[a][0] = (acc[a][0] + lr * vr) - li * vi
                acc[a][1] = (acc[a][1] + lr * vi) + li * vr


class Field:
    def __init__(self, ref, times, depth, vectors):
        self.ref, self.times, self.depth, self.vectors = ref, times, depth, vectors

    def raw(self, t, z):
        out = []
        for a in range(3):
            pair = []
            for ri in range(2):
                at = (((a * self.times + t) * self.depth + z) * 2 + ri) * self.vectors
                pair.append(self.ref[at : at + self.vectors, :])
            out.append(pair)
        return out

    def read(self, t, z):
        return widen(self.raw(t, z))

    def stacked(self, t, z):
        return jnp.concatenate([v for pair in self.raw(t, z) for v in pair], axis=0)


def widen(parts):
    return [[v.astype(F32) for v in pair] for pair in parts]


def zeros(vectors):
    return [[jnp.zeros((vectors, LANES), F32) for _ in range(2)] for _ in range(3)]


def read(ref, t, z):
    return [[ref[a, t, z, ri] for ri in range(2)] for a in range(3)]


def write(ref, t, z, acc):
    for a in range(3):
        for ri in range(2):
            ref[a, t, z, ri] = acc[a][ri].astype(ref.dtype)


def subtract(acc, other):
    for a in range(3):
        for ri in range(2):
            acc[a][ri] = acc[a][ri] - other[a][ri]


def split_hops(product, vectors, count):
    out = []
    for h in range(count):
        cols = product[:, h * LANES : (h + 1) * LANES]
        out.append(
            [
                [cols[(a * 2 + ri) * vectors : (a * 2 + ri + 1) * vectors] for ri in range(2)]
                for a in range(3)
            ]
        )
    return out


def x_permutation(e):
    src = lax.broadcasted_iota(jnp.int32, (LANES, 4 * LANES), 0)
    col = lax.broadcasted_iota(jnp.int32, (LANES, 4 * LANES), 1)
    h = col // LANES
    dst = col % LANES
    y = dst // HALF
    k = dst % HALF
    s = (e + y) % 2
    lead = jnp.where(h == 0, 1, jnp.where(h == 1, 0, jnp.where(h == 2, 2, -1)))
    want = y * HALF + (k + lead - s + HALF) % HALF
    return jnp.where(src == want, 1.0, 0.0).astype(BF16)


def y_permutation():
    rows = LANES // HALF
    src = lax.broadcasted_iota(jnp.int32, (2 * LANES, 4 * LANES), 0)
    col = lax.broadcasted_iota(jnp.int32, (2 * LANES, 4 * LANES), 1)
    h = col // LANES
    dst = col % LANES
    y = dst // HALF
    k = dst % HALF
    d = jnp.where(h == 0, 1, jnp.where(h == 1, -1, jnp.where(h == 2, 3, -3)))
    want = ((y + d + 2 * rows) % (2 * rows)) * HALF + k
    return jnp.where(src == want, 1.0, 0.0).astype(BF16)


def local_kernel(
    times, depth, vectors, sizes,
    momenta_hbm, fat, long, field_ref, y_ref,
    dacc, back_xy, weights, fatf, longf,
    momenta, x_perm, y_perm, sem,
):
    total_y, total_z, scale = sizes
    copy = pltpu.make_async_copy(momenta_hbm, momenta, sem)
    copy.start()
    fat_l, long_l = Links(fatf, times, depth), Links(longf, times, depth)
    field = Field(field_ref, times, depth, vectors)
    y_field = Field(y_ref, times, depth, vectors)
    origin = lax.axis_index("ta") * times + lax.axis_index("gz") * depth
    for e in range(2):
        x_perm[e] = x_permutation(origin + e)
    y_perm[...] = y_permutation()
    fatf[...] = fat[...].astype(F32)
    longf[...] = long[...].astype(F32)
    for t in range(times):
        for z in range(depth):
            here = field.stacked(t, z)
            moved = jnp.dot(here, x_perm[(t + z) % 2], preferred_element_type=F32)
            plus1, minus1, plus3, minus3 = split_hops(moved, vectors, 4)
            back = zeros(vectors)
            add_hop(back, fat_l, 1, 3, t, z, minus1, False)
            write(back_xy.at[1], t, z, back)
            acc = [[-v for v in pair] for pair in back]
            add_hop(acc, fat_l, 0, 3, t, z, plus1, False)
            add_hop(acc, long_l, 0, 3, t, z, plus3, False)
            add_hop(acc, long_l, 1, 3, t, z, minus3, True)
            both = jnp.concatenate([here, y_field.stacked(t, z)], axis=1)
            moved = jnp.dot(both, y_perm[...], preferred_element_type=F32)
            plus1, minus1, plus3, minus3 = split_hops(moved, vectors, 4)
            back = zeros(vectors)
            add_hop(back, fat_l, 1, 2, t, z, minus1, False)
            write(back_xy.at[0], t, z, back)
            subtract(acc, back)
            add_hop(acc, fat_l, 0, 2, t, z, plus1, False)
            add_hop(acc, long_l, 0, 2, t, z, plus3, False)
            add_hop(acc, long_l, 1, 2, t, z, minus3, True)
            if t + 1 < times:
                add_hop(acc, fat_l, 0, 0, t, z, field.read(t + 1, z), False)
            if t >= 1:
                add_hop(acc, fat_l, 1, 0, t, z, field.read(t - 1, z), True)
            if z + 1 < depth:
                add_hop(acc, fat_l, 0, 1, t, z, field.read(t, z + 1), False)
            write(dacc, t, z, acc)
    copy.wait()
    count = momenta.shape[1]
    lane = lax.broadcasted_iota(jnp.int32, (count, LANES), 1)
    sub = lax.broadcasted_iota(jnp.int32, (count, LANES), 0)
    y_glob = lax.axis_index("gy") * (LANES // HALF) + lane // HALF
    q = [jnp.zeros((count, LANES), F32) for _ in range(3)]
    for p in range(count):
        for axis in range(3):
            q[axis] = jnp.where(sub == p, momenta[axis, p].astype(F32), q[axis])
    for t in range(times):
        for z in range(depth):
            z_glob = lax.axis_index("gz") * depth + z
            x_glob = 2 * (lane % HALF) + 1 - (origin + t + z + y_glob) % 2
            turns = (
                q[0] * (x_glob.astype(F32) * (1.0 / NX))
                + q[1] * (y_glob.astype(F32) * (1.0 / total_y))
                + q[2] * (z_glob.astype(F32) * (1.0 / total_z))
            )
            cosine, sine = sincos_turns(turns)
            weights[t * depth + z, 0:count] = cosine * scale
            weights[t * depth + z, count : 2 * count] = sine * scale


def halves(value):
    high = value.astype(BF16)
    low = (value - high.astype(F32)).astype(BF16)
    return high, low


def sincos_turns(turns):
    quarters = 4.0 * (turns - jnp.floor(turns + 0.5))
    near = jnp.floor(quarters + 0.5)
    x = (quarters - near) * (0.5 * math.pi)
    x2 = x * x
    s = x * (1.0 + x2 * (-1.0 / 6 + x2 * (1.0 / 120 + x2 * (-1.0 / 5040 + x2 / 362880))))
    c = 1.0 + x2 * (-0.5 + x2 * (1.0 / 24 + x2 * (-1.0 / 720 + x2 * (1.0 / 40320))))
    which = near.astype(jnp.int32) & 3
    odd = (which & 1) == 1
    cosine = jnp.where(odd, s, c)
    sine = jnp.where(odd, c, s)
    cosine = jnp.where((which == 1) | (which == 2), -cosine, cosine)
    sine = jnp.where(which >= 2, -sine, sine)
    return cosine, sine


def side_kernel(
    times, depth, vectors, rotate,
    dirs_hbm, masks_hbm, field_ref, before_ref, after_ref, fatf, longf, dacc_in, back_xy,
    dacc, left,
    dirs, masks, back, sems,
):
    copies = [
        pltpu.make_async_copy(dirs_hbm, dirs, sems.at[0]),
        pltpu.make_async_copy(masks_hbm, masks, sems.at[1]),
    ]
    for copy in copies:
        copy.start()
    fat_l, long_l = Links(fatf, times, depth), Links(longf, times, depth)
    field = Field(field_ref, times, depth, vectors)
    before = Field(before_ref, times, depth, vectors)
    after = Field(after_ref, times, depth, vectors)
    for t in range(times):
        for z in range(depth):
            acc = read(dacc_in, t, z)
            back_z = zeros(vectors)
            source = field.read(t, z - 1) if z >= 1 else before.read(t, depth - 1)
            add_hop(back_z, fat_l, 1, 1, t, z, source, False)
            write(back.at[0], t, z, back_z)
            for d in range(2):
                write(back.at[1 + d], t, z, read(back_xy.at[d], t, z))
            subtract(acc, back_z)
            if z + 1 == depth:
                add_hop(acc, fat_l, 0, 1, t, z, after.read(t, 0), False)
            add_hop(acc, long_l, 0, 1, t, z, after.read(t, z), False)
            add_hop(acc, long_l, 1, 1, t, z, before.read(t, z), True)
            write(dacc, t, z, acc)
    for copy in copies:
        copy.wait()
    slots = dirs.shape[0]
    if rotate:
        gz, gy = lax.axis_index("gz"), lax.axis_index("gy")
        current_of = [((gz + d // 2) % 2) * 2 + (gy + d % 2) % 2 for d in range(slots)]
    else:
        current_of = list(range(slots))
    lane = lax.broadcasted_iota(jnp.int32, (1, LANES), 1)
    y_glob = lax.axis_index("gy") * (LANES // HALF) + lane // HALF
    origin = lax.axis_index("ta") * times + lax.axis_index("gz") * depth
    low_part = slots * 2 * vectors
    for slot in range(slots):
        direction = dirs[current_of[slot]] - 1
        mask = masks[current_of[slot]]
        for t in range(times):
            for z in range(depth):
                z_glob = lax.axis_index("gz") * depth + z
                x_glob = 2 * (lane % HALF) + 1 - (origin + t + z + y_glob) % 2
                exponent = (
                    (mask & 1) * x_glob + ((mask >> 1) & 1) * y_glob + ((mask >> 2) & 1) * z_glob
                )
                sign = (1 - 2 * (exponent & 1)).astype(F32)
                for a in range(3):
                    col = (z * 3 + a) * 2 * LANES
                    first = slice(col, col + LANES)
                    other = slice(col + LANES, col + 2 * LANES)
                    real = halves(back[direction, a, t, z, 0] * sign)
                    imag = halves(back[direction, a, t, z, 1] * sign)
                    for part in range(2):
                        top = part * low_part + slot * 2 * vectors
                        turned = top + vectors
                        left[t, top : top + vectors, first] = real[part]
                        left[t, top : top + vectors, other] = imag[part]
                        left[t, turned : turned + vectors, first] = -imag[part]
                        left[t, turned : turned + vectors, other] = real[part]


NT_DIMS = (((1,), (1,)), ((), ()))


def before_kernel(times, depth, vectors, block_ref, fatf, longf, dacc_in, dacc):
    fat_l, long_l = Links(fatf, times, depth), Links(longf, times, depth)
    block = Field(block_ref, times, depth, vectors)
    for t in range(times):
        for z in range(depth):
            acc = read(dacc_in, t, z)
            add_hop(acc, long_l, 1, 0, t, z, block.read(t, z), True)
            if t == 0:
                add_hop(acc, fat_l, 1, 0, t, z, block.read(times - 1, z), True)
            write(dacc, t, z, acc)


def meson_slice(t, layers, weights, left, pieces, vectors, first=0):
    rows = 2 * vectors
    left_rows = left.shape[1] // 2
    count = weights.shape[1] // 2
    columns = count * vectors
    parts = jnp.zeros((2 * left_rows, 2 * columns), F32)
    depth = len(layers)
    for z, acc in enumerate(layers):
        at = t * depth + z
        for a in range(3):
            real, imag = acc[a]
            right = [[], []]
            for p in range(count):
                cosine = weights[at, p : p + 1, :]
                sine = weights[at, count + p : count + p + 1, :]
                right[0].append(halves(cosine * real + sine * imag))
                right[1].append(halves(cosine * imag - sine * real))
            right = jnp.concatenate(
                [jnp.concatenate([h for h, _ in r] + [l for _, l in r], axis=0) for r in right],
                axis=1,
            )
            col = (z * 3 + a) * 2 * LANES
            parts = parts + lax.dot_general(
                left[t, :, col : col + 2 * LANES], right, NT_DIMS, preferred_element_type=F32
            )
    total = (parts[:left_rows, :columns] + parts[left_rows:, columns:]) + (
        parts[left_rows:, :columns] + parts[:left_rows, columns:]
    )
    for slot, piece in enumerate(pieces):
        for ri in range(2):
            top = slot * rows + ri * vectors
            piece[t - first, ri] = total[top : top + vectors]


def early_kernel(
    times, depth, vectors,
    block_ref, fatf, longf, dacc, weights, left,
    edge, dirac16, *pieces,
):
    fat_l, long_l = Links(fatf, times, depth), Links(longf, times, depth)
    block = Field(block_ref, times - 1, depth, vectors)
    for z in range(depth):
        acc = read(dacc, times - 1, z)
        add_hop(acc, fat_l, 0, 0, times - 1, z, block.read(0, z), False)
        write(edge, 0, z, acc)
    for t in range(times - 1):
        layers = []
        for z in range(depth):
            acc = read(dacc, t, z)
            add_hop(acc, long_l, 0, 0, t, z, block.read(t, z), False)
            write(dirac16, t, z, acc)
            layers.append(acc)
        meson_slice(t, layers, weights, left, pieces, vectors)


def late_kernel(
    times, depth, vectors,
    block_ref, longf, edge, weights, left, dirac16_in,
    dirac16, *pieces,
):
    long_l = Links(longf, times, depth)
    block = Field(block_ref, 1, depth, vectors)
    layers = []
    for z in range(depth):
        acc = read(edge, 0, z)
        add_hop(acc, long_l, 0, 0, times - 1, z, block.read(0, z), False)
        write(dirac16, times - 1, z, acc)
        layers.append(acc)
    meson_slice(times - 1, layers, weights, left, pieces, vectors, times - 1)
    for t in range(times - 1):
        dirac16[:, t] = dirac16_in[:, t]


def pair_kernel(*refs):
    give, give_got, keep, keep_got = refs[:4]
    send, partial = refs[-2:]
    send[...] = give[...] + give_got[...]
    partial[...] = keep[...] + keep_got[...]


def spread_kernel(dirac16, *refs):
    out, wide = refs[-2:]
    rows, vectors = dirac16.shape[0], dirac16.shape[1]
    for r in range(rows):
        wide[pl.ds(r, vectors, stride=rows), :] = dirac16[r].astype(F32)
    out[...] = wide[...].astype(BF16)


def final_kernel(partial, other, partial_last, other_last, out):
    early = partial.shape[0]
    width = out.shape[4]
    for t in range(out.shape[1]):
        for ri in range(2):
            if t < early:
                total = partial[t, ri] + other[t, ri]
            else:
                total = partial_last[t - early, ri] + other_last[t - early, ri]
            for p in range(out.shape[0]):
                out[p, t, ri] = total[:, p * width : (p + 1) * width]


def send_parts(pieces, after):
    swap = [(0, 1), (1, 0)]
    got = lax.ppermute(jnp.stack([pieces[1], pieces[3]]), "gy", swap)
    shape = jax.ShapeDtypeStruct(pieces[0].shape, F32)
    send, partial = call(pair_kernel, [shape] * 2, [VM] * (4 + len(after)), [], 1)(
        pieces[2], got[1], pieces[0], got[0], *after
    )
    return send, partial, lax.ppermute(send, "gz", swap)


def exchange(value, axis):
    size = lax.axis_size(axis)
    up = [(i, (i + 1) % size) for i in range(size)]
    down = [(j, i) for i, j in up]
    before = lax.ppermute(value, axis, up)
    if size == 2:
        return before, before
    return before, lax.ppermute(value, axis, down)


def on_device(eigen_store, fat_links, long_links, chosen, momenta, current_dirs, taste_masks):
    stored, _, _, times, depth, _ = eigen_store.shape
    vectors = chosen.shape[0]
    per_vector = 6 * times * depth
    n_ta, n_gz, n_gy = (lax.axis_size(a) for a in ("ta", "gz", "gy"))
    total_y = (LANES // HALF) * n_gy
    total_z = depth * n_gz

    store = eigen_store.transpose(0, 1, 3, 4, 2, 5).reshape(stored * per_vector, LANES)
    fat = fat_links.transpose(0, 1, 2, 3, 5, 6, 4, 7).reshape(-1, LANES)
    long = long_links.transpose(0, 1, 2, 3, 5, 6, 4, 7).reshape(-1, LANES)
    link_rows = fat.shape[0]
    shape6 = (3, times, depth, 2, vectors, LANES)
    size = per_vector * vectors

    def rows_of(n, dtype=BF16):
        return jax.ShapeDtypeStruct((n, LANES), dtype)

    last_size = size // times
    up_out, down_out, last_out, packed, fat_v, long_v = call(
        functools.partial(gather_kernel, times, depth, vectors),
        [
            rows_of(size + 16), rows_of(size - last_size), rows_of(last_size), rows_of(size),
            rows_of(link_rows), rows_of(link_rows),
        ],
        [HB] * 4,
        [
            pltpu.SMEM(chosen.shape, jnp.int32),
            pltpu.VMEM(store.shape, BF16),
            pltpu.VMEM(store.shape, F32),
            pltpu.VMEM((size, LANES), F32),
            pltpu.SemaphoreType.DMA((PIECES + 3,)),
        ],
        1,
    )(*map(pinned, (chosen, store, fat, long)))
    up = [(i, (i + 1) % n_ta) for i in range(n_ta)]
    down = [(j, i) for i, j in up]
    before_t = lax.ppermute(up_out, "ta", up)
    after_t = lax.ppermute(down_out, "ta", down)
    after_last = lax.ppermute(last_out, "ta", down)
    before_z, after_z = exchange(packed, "gz")
    y_field, _ = exchange(packed, "gy")

    slots = current_dirs.shape[0]
    count = momenta.shape[0]
    width = depth * 6 * LANES
    left_rows = slots * 2 * vectors
    rotate = n_gz == 2 and n_gy == 2
    scale = 1.0 / math.sqrt(NX * total_y * total_z / 2)
    dacc, back_xy, weights, fatf, longf = call(
        functools.partial(local_kernel, times, depth, vectors, (total_y, total_z, scale)),
        [
            jax.ShapeDtypeStruct(shape6, F32),
            jax.ShapeDtypeStruct((2,) + shape6, F32),
            jax.ShapeDtypeStruct((times * depth, 2 * count, LANES), F32),
            rows_of(link_rows, F32),
            rows_of(link_rows, F32),
        ],
        [HB] + [VM] * 4,
        [
            pltpu.SMEM((3, count), jnp.int32),
            pltpu.VMEM((2, LANES, 4 * LANES), BF16),
            pltpu.VMEM((2 * LANES, 4 * LANES), BF16),
            pltpu.SemaphoreType.DMA,
        ],
        1,
    )(pinned(momenta.T), fat_v, long_v, packed, y_field)
    dacc, left = call(
        functools.partial(side_kernel, times, depth, vectors, rotate),
        [
            jax.ShapeDtypeStruct(shape6, F32),
            jax.ShapeDtypeStruct((times, 2 * left_rows, width), BF16),
        ],
        [HB] * 2 + [VM] * 7,
        [
            pltpu.SMEM((slots,), jnp.int32),
            pltpu.SMEM((slots,), jnp.int32),
            pltpu.VMEM((3,) + shape6, F32),
            pltpu.SemaphoreType.DMA((2,)),
        ],
        1,
    )(
        pinned(current_dirs), pinned(taste_masks), packed, before_z, after_z, fatf, longf, dacc, back_xy
    )

    def piece_of(slices):
        return jax.ShapeDtypeStruct((slices, 2, vectors, count * vectors), F32)

    (dacc,) = call(
        functools.partial(before_kernel, times, depth, vectors),
        [jax.ShapeDtypeStruct(shape6, F32)],
        [VM] * 4,
        [],
        1,
    )(before_t, fatf, longf, dacc)
    odd16 = jax.ShapeDtypeStruct(shape6, BF16)
    edge, dirac16, *early = call(
        functools.partial(early_kernel, times, depth, vectors),
        [jax.ShapeDtypeStruct((3, 1) + shape6[2:], F32), odd16] + [piece_of(times - 1)] * slots,
        [VM] * 6,
        [],
        1,
    )(after_t, fatf, longf, dacc, weights, left)
    dirac16, *late = call(
        functools.partial(late_kernel, times, depth, vectors),
        [odd16] + [piece_of(1)] * slots,
        [VM] * 6,
        [],
        1,
    )(after_last, longf, edge, weights, left, dirac16)

    odd_shape = rows_of(size)
    turned = dirac16.reshape(per_vector, vectors, LANES)
    scratch = [pltpu.VMEM((size, LANES), F32)]
    if rotate:
        send, partial, other = send_parts(early, [])
        _, partial_last, other_last = send_parts(late, [send])
        (odd_rows,) = call(spread_kernel, [odd_shape], [VM] * 2, scratch, 1)(turned, partial_last)
        meson_shape = jax.ShapeDtypeStruct((count, times, 2, vectors, vectors), F32)
        (meson_fields,) = call(final_kernel, [meson_shape], [VM] * 4, [], 1)(
            partial, other, partial_last, other_last
        )
    else:
        (odd_rows,) = call(spread_kernel, [odd_shape], [VM], scratch, 1)(turned)
        pieces = [jnp.concatenate(pair, axis=0) for pair in zip(early, late)]
        whole = jnp.stack(pieces).reshape(slots, times, 2, vectors, count, vectors)
        whole = whole.transpose(0, 4, 1, 2, 3, 5).reshape(
            slots * count, times, 2, vectors, vectors
        )
        meson_fields = lax.psum_scatter(whole, ("gz", "gy"), scatter_dimension=0, tiled=True)
    odd_vectors = odd_rows.reshape(vectors, 3, times, depth, 2, LANES).transpose(0, 1, 4, 2, 3, 5)
    return odd_vectors, meson_fields


def solution(mesh):
    in_specs = (
        P(None, None, None, ("cfg", "ta"), "gz", "gy"),
        P(None, None, None, None, None, ("cfg", "ta"), "gz", "gy"),
        P(None, None, None, None, None, ("cfg", "ta"), "gz", "gy"),
        P("cfg"),
        P(),
        P(),
        P(),
    )
    out_specs = (
        P(None, None, None, ("cfg", "ta"), "gz", "gy"),
        P(("gz", "gy"), ("cfg", "ta"), None, None, None),
    )
    return jax.shard_map(
        on_device, mesh=mesh, in_specs=in_specs, out_specs=out_specs, check_vma=False
    )
```

```python
import functools
import math

import jax
import jax.numpy as jnp
from jax import lax
from jax.experimental import pallas as pl
from jax.experimental.pallas import tpu as pltpu
from jax.sharding import PartitionSpec as P

NX = 64
HALF = NX // 2
LANES = 128
F32 = jnp.float32
BF16 = jnp.bfloat16
VM = pl.BlockSpec(memory_space=pltpu.VMEM)
SM = pl.BlockSpec(memory_space=pltpu.SMEM)
HB = pl.BlockSpec(memory_space=pltpu.HBM)


def pinned(value):
    return pltpu.with_memory_space_constraint(value, pltpu.HBM)


def call(body, outs, ins, scratch, cost):
    return pl.pallas_call(
        body,
        out_shape=outs,
        in_specs=ins,
        out_specs=[VM] * len(outs),
        scratch_shapes=scratch,
        compiler_params=pltpu.CompilerParams(vmem_limit_bytes=40 * 1024 * 1024),
        cost_estimate=pl.CostEstimate(flops=cost, bytes_accessed=cost, transcendentals=0),
    )


PIECES = 5


def gather_kernel(
    times, depth, vectors, chosen_hbm, store_hbm, fat_hbm, long_hbm,
    up, down, last, out, fat, long,
    chosen, store, wide, turned, sems,
):
    piece = store.shape[0] // PIECES
    first = pltpu.make_async_copy(chosen_hbm, chosen, sems.at[PIECES])
    first.start()
    copies = []
    for i in range(PIECES):
        part = pl.ds(i * piece, piece)
        copies.append(pltpu.make_async_copy(store_hbm.at[part], store.at[part], sems.at[i]))
    later = [
        pltpu.make_async_copy(fat_hbm, fat, sems.at[PIECES + 1]),
        pltpu.make_async_copy(long_hbm, long, sems.at[PIECES + 2]),
    ]
    for copy in copies + later:
        copy.start()
    for i, copy in enumerate(copies):
        copy.wait()
        wide[i * piece : (i + 1) * piece, :] = store[i * piece : (i + 1) * piece, :].astype(F32)
    first.wait()
    size = out.shape[0]
    rows = size // vectors
    full = rows // 8
    rest = rows - 8 * full
    for n in range(vectors):
        start = chosen[n] * rows
        for q in range(full):
            turned[pl.ds(q * 8 * vectors + n, 8, stride=vectors), :] = wide[
                pl.ds(start + 8 * q, 8), :
            ]
        if rest:
            turned[pl.ds(full * 8 * vectors + n, rest, stride=vectors), :] = wide[
                pl.ds(start + 8 * full, rest), :
            ]
    layer = depth * 2 * vectors
    for a in range(3):
        for t in range(times):
            source = (a * times + t) * layer
            block = turned[source : source + layer, :].astype(BF16)
            out[source : source + layer, :] = block
            up[source : source + layer, :] = block
            if t + 1 < times:
                target = (a * (times - 1) + t) * layer
                down[target : target + layer, :] = block
            else:
                last[a * layer : (a + 1) * layer, :] = block
    up[size:, :] = jnp.zeros((up.shape[0] - size, LANES), BF16)
    for copy in later:
        copy.wait()


class Links:
    def __init__(self, ref, times, depth):
        self.ref, self.times, self.depth = ref, times, depth

    def row(self, w, mu, a, b, t, z, ri):
        at = (((((w * 4 + mu) * 3 + a) * 3 + b) * self.times + t) * self.depth + z) * 2 + ri
        return self.ref[at : at + 1, :]


def add_hop(acc, links, w, mu, t, z, vec, minus):
    for a in range(3):
        for b in range(3):
            lr = links.row(w, mu, a, b, t, z, 0)
            li = links.row(w, mu, a, b, t, z, 1)
            vr, vi = vec[b]
            if minus:
                acc[a][0] = (acc[a][0] - lr * vr) + li * vi
                acc[a][1] = (acc[a][1] - lr * vi) - li * vr
            else:
                acc[a][0] = (acc[a][0] + lr * vr) - li * vi
                acc[a][1] = (acc[a][1] + lr * vi) + li * vr


class Field:
    def __init__(self, ref, times, depth, vectors):
        self.ref, self.times, self.depth, self.vectors = ref, times, depth, vectors

    def raw(self, t, z):
        out = []
        for a in range(3):
            pair = []
            for ri in range(2):
                at = (((a * self.times + t) * self.depth + z) * 2 + ri) * self.vectors
                pair.append(self.ref[at : at + self.vectors, :])
            out.append(pair)
        return out

    def read(self, t, z):
        return widen(self.raw(t, z))

    def stacked(self, t, z):
        return jnp.concatenate([v for pair in self.raw(t, z) for v in pair], axis=0)


def widen(parts):
    return [[v.astype(F32) for v in pair] for pair in parts]


def zeros(vectors):
    return [[jnp.zeros((vectors, LANES), F32) for _ in range(2)] for _ in range(3)]


def read(ref, t, z):
    return [[ref[a, t, z, ri] for ri in range(2)] for a in range(3)]


def write(ref, t, z, acc):
    for a in range(3):
        for ri in range(2):
            ref[a, t, z, ri] = acc[a][ri].astype(ref.dtype)


def subtract(acc, other):
    for a in range(3):
        for ri in range(2):
            acc[a][ri] = acc[a][ri] - other[a][ri]


def split_hops(product, vectors, count):
    out = []
    for h in range(count):
        cols = product[:, h * LANES : (h + 1) * LANES]
        out.append(
            [
                [cols[(a * 2 + ri) * vectors : (a * 2 + ri + 1) * vectors] for ri in range(2)]
                for a in range(3)
            ]
        )
    return out


def x_permutation(e):
    src = lax.broadcasted_iota(jnp.int32, (LANES, 4 * LANES), 0)
    col = lax.broadcasted_iota(jnp.int32, (LANES, 4 * LANES), 1)
    h = col // LANES
    dst = col % LANES
    y = dst // HALF
    k = dst % HALF
    s = (e + y) % 2
    lead = jnp.where(h == 0, 1, jnp.where(h == 1, 0, jnp.where(h == 2, 2, -1)))
    want = y * HALF + (k + lead - s + HALF) % HALF
    return jnp.where(src == want, 1.0, 0.0).astype(BF16)


def y_permutation():
    rows = LANES // HALF
    src = lax.broadcasted_iota(jnp.int32, (2 * LANES, 4 * LANES), 0)
    col = lax.broadcasted_iota(jnp.int32, (2 * LANES, 4 * LANES), 1)
    h = col // LANES
    dst = col % LANES
    y = dst // HALF
    k = dst % HALF
    d = jnp.where(h == 0, 1, jnp.where(h == 1, -1, jnp.where(h == 2, 3, -3)))
    want = ((y + d + 2 * rows) % (2 * rows)) * HALF + k
    return jnp.where(src == want, 1.0, 0.0).astype(BF16)


def local_kernel(
    times, depth, vectors, sizes,
    momenta_hbm, fat, long, field_ref, y_ref,
    dacc, back_xy, weights, fatf, longf,
    momenta, x_perm, y_perm, sem,
):
    total_y, total_z, scale = sizes
    copy = pltpu.make_async_copy(momenta_hbm, momenta, sem)
    copy.start()
    fat_l, long_l = Links(fatf, times, depth), Links(longf, times, depth)
    field = Field(field_ref, times, depth, vectors)
    y_field = Field(y_ref, times, depth, vectors)
    origin = lax.axis_index("ta") * times + lax.axis_index("gz") * depth
    for e in range(2):
        x_perm[e] = x_permutation(origin + e)
    y_perm[...] = y_permutation()
    fatf[...] = fat[...].astype(F32)
    longf[...] = long[...].astype(F32)
    for t in range(times):
        for z in range(depth):
            here = field.stacked(t, z)
            moved = jnp.dot(here, x_perm[(t + z) % 2], preferred_element_type=F32)
            plus1, minus1, plus3, minus3 = split_hops(moved, vectors, 4)
            back = zeros(vectors)
            add_hop(back, fat_l, 1, 3, t, z, minus1, False)
            write(back_xy.at[1], t, z, back)
            acc = [[-v for v in pair] for pair in back]
            add_hop(acc, fat_l, 0, 3, t, z, plus1, False)
            add_hop(acc, long_l, 0, 3, t, z, plus3, False)
            add_hop(acc, long_l, 1, 3, t, z, minus3, True)
            both = jnp.concatenate([here, y_field.stacked(t, z)], axis=1)
            moved = jnp.dot(both, y_perm[...], preferred_element_type=F32)
            plus1, minus1, plus3, minus3 = split_hops(moved, vectors, 4)
            back = zeros(vectors)
            add_hop(back, fat_l, 1, 2, t, z, minus1, False)
            write(back_xy.at[0], t, z, back)
            subtract(acc, back)
            add_hop(acc, fat_l, 0, 2, t, z, plus1, False)
            add_hop(acc, long_l, 0, 2, t, z, plus3, False)
            add_hop(acc, long_l, 1, 2, t, z, minus3, True)
            if t + 1 < times:
                add_hop(acc, fat_l, 0, 0, t, z, field.read(t + 1, z), False)
            if t >= 1:
                add_hop(acc, fat_l, 1, 0, t, z, field.read(t - 1, z), True)
            if z + 1 < depth:
                add_hop(acc, fat_l, 0, 1, t, z, field.read(t, z + 1), False)
            write(dacc, t, z, acc)
    copy.wait()
    count = momenta.shape[1]
    lane = lax.broadcasted_iota(jnp.int32, (count, LANES), 1)
    sub = lax.broadcasted_iota(jnp.int32, (count, LANES), 0)
    y_glob = lax.axis_index("gy") * (LANES // HALF) + lane // HALF
    q = [jnp.zeros((count, LANES), F32) for _ in range(3)]
    for p in range(count):
        for axis in range(3):
            q[axis] = jnp.where(sub == p, momenta[axis, p].astype(F32), q[axis])
    for t in range(times):
        for z in range(depth):
            z_glob = lax.axis_index("gz") * depth + z
            x_glob = 2 * (lane % HALF) + 1 - (origin + t + z + y_glob) % 2
            turns = (
                q[0] * (x_glob.astype(F32) * (1.0 / NX))
                + q[1] * (y_glob.astype(F32) * (1.0 / total_y))
                + q[2] * (z_glob.astype(F32) * (1.0 / total_z))
            )
            cosine, sine = sincos_turns(turns)
            weights[t * depth + z, 0:count] = cosine * scale
            weights[t * depth + z, count : 2 * count] = sine * scale


def halves(value):
    high = value.astype(BF16)
    low = (value - high.astype(F32)).astype(BF16)
    return high, low


def sincos_turns(turns):
    quarters = 4.0 * (turns - jnp.floor(turns + 0.5))
    near = jnp.floor(quarters + 0.5)
    x = (quarters - near) * (0.5 * math.pi)
    x2 = x * x
    s = x * (1.0 + x2 * (-1.0 / 6 + x2 * (1.0 / 120 + x2 * (-1.0 / 5040 + x2 / 362880))))
    c = 1.0 + x2 * (-0.5 + x2 * (1.0 / 24 + x2 * (-1.0 / 720 + x2 * (1.0 / 40320))))
    which = near.astype(jnp.int32) & 3
    odd = (which & 1) == 1
    cosine = jnp.where(odd, s, c)
    sine = jnp.where(odd, c, s)
    cosine = jnp.where((which == 1) | (which == 2), -cosine, cosine)
    sine = jnp.where(which >= 2, -sine, sine)
    return cosine, sine


def side_kernel(
    times, depth, vectors, rotate,
    dirs_hbm, masks_hbm, field_ref, before_ref, after_ref, fatf, longf, dacc_in, back_xy,
    dacc, left,
    dirs, masks, back, sems,
):
    copies = [
        pltpu.make_async_copy(dirs_hbm, dirs, sems.at[0]),
        pltpu.make_async_copy(masks_hbm, masks, sems.at[1]),
    ]
    for copy in copies:
        copy.start()
    fat_l, long_l = Links(fatf, times, depth), Links(longf, times, depth)
    field = Field(field_ref, times, depth, vectors)
    before = Field(before_ref, times, depth, vectors)
    after = Field(after_ref, times, depth, vectors)
    for t in range(times):
        for z in range(depth):
            acc = read(dacc_in, t, z)
            back_z = zeros(vectors)
            source = field.read(t, z - 1) if z >= 1 else before.read(t, depth - 1)
            add_hop(back_z, fat_l, 1, 1, t, z, source, False)
            write(back.at[0], t, z, back_z)
            for d in range(2):
                write(back.at[1 + d], t, z, read(back_xy.at[d], t, z))
            subtract(acc, back_z)
            if z + 1 == depth:
                add_hop(acc, fat_l, 0, 1, t, z, after.read(t, 0), False)
            add_hop(acc, long_l, 0, 1, t, z, after.read(t, z), False)
            add_hop(acc, long_l, 1, 1, t, z, before.read(t, z), True)
            write(dacc, t, z, acc)
    for copy in copies:
        copy.wait()
    slots = dirs.shape[0]
    if rotate:
        gz, gy = lax.axis_index("gz"), lax.axis_index("gy")
        current_of = [((gz + d // 2) % 2) * 2 + (gy + d % 2) % 2 for d in range(slots)]
    else:
        current_of = list(range(slots))
    lane = lax.broadcasted_iota(jnp.int32, (1, LANES), 1)
    y_glob = lax.axis_index("gy") * (LANES // HALF) + lane // HALF
    origin = lax.axis_index("ta") * times + lax.axis_index("gz") * depth
    low_part = slots * 2 * vectors
    for slot in range(slots):
        direction = dirs[current_of[slot]] - 1
        mask = masks[current_of[slot]]
        for t in range(times):
            for z in range(depth):
                z_glob = lax.axis_index("gz") * depth + z
                x_glob = 2 * (lane % HALF) + 1 - (origin + t + z + y_glob) % 2
                exponent = (
                    (mask & 1) * x_glob + ((mask >> 1) & 1) * y_glob + ((mask >> 2) & 1) * z_glob
                )
                sign = (1 - 2 * (exponent & 1)).astype(F32)
                for a in range(3):
                    col = (z * 3 + a) * 2 * LANES
                    first = slice(col, col + LANES)
                    other = slice(col + LANES, col + 2 * LANES)
                    real = halves(back[direction, a, t, z, 0] * sign)
                    imag = halves(back[direction, a, t, z, 1] * sign)
                    for part in range(2):
                        top = part * low_part + slot * 2 * vectors
                        turned = top + vectors
                        left[t, top : top + vectors, first] = real[part]
                        left[t, top : top + vectors, other] = imag[part]
                        left[t, turned : turned + vectors, first] = -imag[part]
                        left[t, turned : turned + vectors, other] = real[part]


NT_DIMS = (((1,), (1,)), ((), ()))


def before_kernel(times, depth, vectors, block_ref, fatf, longf, dacc_in, dacc):
    fat_l, long_l = Links(fatf, times, depth), Links(longf, times, depth)
    block = Field(block_ref, times, depth, vectors)
    for t in range(times):
        for z in range(depth):
            acc = read(dacc_in, t, z)
            add_hop(acc, long_l, 1, 0, t, z, block.read(t, z), True)
            if t == 0:
                add_hop(acc, fat_l, 1, 0, t, z, block.read(times - 1, z), True)
            write(dacc, t, z, acc)


def meson_slice(t, layers, weights, left, pieces, vectors, first=0):
    rows = 2 * vectors
    left_rows = left.shape[1] // 2
    count = weights.shape[1] // 2
    columns = count * vectors
    parts = jnp.zeros((2 * left_rows, 2 * columns), F32)
    depth = len(layers)
    for z, acc in enumerate(layers):
        at = t * depth + z
        for a in range(3):
            real, imag = acc[a]
            right = [[], []]
            for p in range(count):
                cosine = weights[at, p : p + 1, :]
                sine = weights[at, count + p : count + p + 1, :]
                right[0].append(halves(cosine * real + sine * imag))
                right[1].append(halves(cosine * imag - sine * real))
            right = jnp.concatenate(
                [jnp.concatenate([h for h, _ in r] + [l for _, l in r], axis=0) for r in right],
                axis=1,
            )
            col = (z * 3 + a) * 2 * LANES
            parts = parts + lax.dot_general(
                left[t, :, col : col + 2 * LANES], right, NT_DIMS, preferred_element_type=F32
            )
    total = (parts[:left_rows, :columns] + parts[left_rows:, columns:]) + (
        parts[left_rows:, :columns] + parts[:left_rows, columns:]
    )
    for slot, piece in enumerate(pieces):
        for ri in range(2):
            top = slot * rows + ri * vectors
            piece[t - first, ri] = total[top : top + vectors]


def early_kernel(
    times, depth, vectors,
    block_ref, fatf, longf, dacc, weights, left,
    edge, dirac16, *pieces,
):
    fat_l, long_l = Links(fatf, times, depth), Links(longf, times, depth)
    block = Field(block_ref, times - 1, depth, vectors)
    for z in range(depth):
        acc = read(dacc, times - 1, z)
        add_hop(acc, fat_l, 0, 0, times - 1, z, block.read(0, z), False)
        write(edge, 0, z, acc)
    for t in range(times - 1):
        layers = []
        for z in range(depth):
            acc = read(dacc, t, z)
            add_hop(acc, long_l, 0, 0, t, z, block.read(t, z), False)
            write(dirac16, t, z, acc)
            layers.append(acc)
        meson_slice(t, layers, weights, left, pieces, vectors)


def late_kernel(
    times, depth, vectors,
    block_ref, longf, edge, weights, left, dirac16_in,
    dirac16, *pieces,
):
    long_l = Links(longf, times, depth)
    block = Field(block_ref, 1, depth, vectors)
    layers = []
    for z in range(depth):
        acc = read(edge, 0, z)
        add_hop(acc, long_l, 0, 0, times - 1, z, block.read(0, z), False)
        write(dirac16, times - 1, z, acc)
        layers.append(acc)
    meson_slice(times - 1, layers, weights, left, pieces, vectors, times - 1)
    for t in range(times - 1):
        dirac16[:, t] = dirac16_in[:, t]


def pair_kernel(*refs):
    give, give_got, keep, keep_got = refs[:4]
    send, partial = refs[-2:]
    send[...] = give[...] + give_got[...]
    partial[...] = keep[...] + keep_got[...]


def spread_kernel(dirac16, *refs):
    out, wide = refs[-2:]
    rows, vectors = dirac16.shape[0], dirac16.shape[1]
    for r in range(rows):
        wide[pl.ds(r, vectors, stride=rows), :] = dirac16[r].astype(F32)
    out[...] = wide[...].astype(BF16)


def final_kernel(first, partial, other, *refs):
    out, rows, sem = refs[-3:]
    slices = partial.shape[0]
    width = out.shape[4]
    for t in range(slices):
        for ri in range(2):
            total = partial[t, ri] + other[t, ri]
            for p in range(out.shape[0]):
                rows[p, t, ri] = total[:, p * width : (p + 1) * width]
    copy = pltpu.make_async_copy(rows, out.at[:, pl.ds(first, slices)], sem)
    copy.start()
    copy.wait()


def finish(shape, first, partial, other, so_far):
    rows = shape.shape[:1] + partial.shape[:1] + shape.shape[2:]
    return pl.pallas_call(
        functools.partial(final_kernel, first),
        out_shape=shape,
        in_specs=[VM] * 2 + [HB] * len(so_far),
        out_specs=HB,
        scratch_shapes=[pltpu.VMEM(rows, F32), pltpu.SemaphoreType.DMA],
        input_output_aliases={2: 0} if so_far else {},
        compiler_params=pltpu.CompilerParams(vmem_limit_bytes=40 * 1024 * 1024),
        cost_estimate=pl.CostEstimate(flops=1, bytes_accessed=1, transcendentals=0),
    )(partial, other, *so_far)


def send_parts(pieces, after):
    swap = [(0, 1), (1, 0)]
    got = lax.ppermute(jnp.stack([pieces[1], pieces[3]]), "gy", swap)
    shape = jax.ShapeDtypeStruct(pieces[0].shape, F32)
    send, partial = call(pair_kernel, [shape] * 2, [VM] * (4 + len(after)), [], 1)(
        pieces[2], got[1], pieces[0], got[0], *after
    )
    return send, partial, lax.ppermute(send, "gz", swap)


def exchange(value, axis):
    size = lax.axis_size(axis)
    up = [(i, (i + 1) % size) for i in range(size)]
    down = [(j, i) for i, j in up]
    before = lax.ppermute(value, axis, up)
    if size == 2:
        return before, before
    return before, lax.ppermute(value, axis, down)


def on_device(eigen_store, fat_links, long_links, chosen, momenta, current_dirs, taste_masks):
    stored, _, _, times, depth, _ = eigen_store.shape
    vectors = chosen.shape[0]
    per_vector = 6 * times * depth
    n_ta, n_gz, n_gy = (lax.axis_size(a) for a in ("ta", "gz", "gy"))
    total_y = (LANES // HALF) * n_gy
    total_z = depth * n_gz

    store = eigen_store.transpose(0, 1, 3, 4, 2, 5).reshape(stored * per_vector, LANES)
    fat = fat_links.transpose(0, 1, 2, 3, 5, 6, 4, 7).reshape(-1, LANES)
    long = long_links.transpose(0, 1, 2, 3, 5, 6, 4, 7).reshape(-1, LANES)
    link_rows = fat.shape[0]
    shape6 = (3, times, depth, 2, vectors, LANES)
    size = per_vector * vectors

    def rows_of(n, dtype=BF16):
        return jax.ShapeDtypeStruct((n, LANES), dtype)

    last_size = size // times
    up_out, down_out, last_out, packed, fat_v, long_v = call(
        functools.partial(gather_kernel, times, depth, vectors),
        [
            rows_of(size + 16), rows_of(size - last_size), rows_of(last_size), rows_of(size),
            rows_of(link_rows), rows_of(link_rows),
        ],
        [HB] * 4,
        [
            pltpu.SMEM(chosen.shape, jnp.int32),
            pltpu.VMEM(store.shape, BF16),
            pltpu.VMEM(store.shape, F32),
            pltpu.VMEM((size, LANES), F32),
            pltpu.SemaphoreType.DMA((PIECES + 3,)),
        ],
        1,
    )(*map(pinned, (chosen, store, fat, long)))
    up = [(i, (i + 1) % n_ta) for i in range(n_ta)]
    down = [(j, i) for i, j in up]
    before_t = lax.ppermute(up_out, "ta", up)
    after_t = lax.ppermute(down_out, "ta", down)
    after_last = lax.ppermute(last_out, "ta", down)
    before_z, after_z = exchange(packed, "gz")
    y_field, _ = exchange(packed, "gy")

    slots = current_dirs.shape[0]
    count = momenta.shape[0]
    width = depth * 6 * LANES
    left_rows = slots * 2 * vectors
    rotate = n_gz == 2 and n_gy == 2
    scale = 1.0 / math.sqrt(NX * total_y * total_z / 2)
    dacc, back_xy, weights, fatf, longf = call(
        functools.partial(local_kernel, times, depth, vectors, (total_y, total_z, scale)),
        [
            jax.ShapeDtypeStruct(shape6, F32),
            jax.ShapeDtypeStruct((2,) + shape6, F32),
            jax.ShapeDtypeStruct((times * depth, 2 * count, LANES), F32),
            rows_of(link_rows, F32),
            rows_of(link_rows, F32),
        ],
        [HB] + [VM] * 4,
        [
            pltpu.SMEM((3, count), jnp.int32),
            pltpu.VMEM((2, LANES, 4 * LANES), BF16),
            pltpu.VMEM((2 * LANES, 4 * LANES), BF16),
            pltpu.SemaphoreType.DMA,
        ],
        1,
    )(pinned(momenta.T), fat_v, long_v, packed, y_field)
    dacc, left = call(
        functools.partial(side_kernel, times, depth, vectors, rotate),
        [
            jax.ShapeDtypeStruct(shape6, F32),
            jax.ShapeDtypeStruct((times, 2 * left_rows, width), BF16),
        ],
        [HB] * 2 + [VM] * 7,
        [
            pltpu.SMEM((slots,), jnp.int32),
            pltpu.SMEM((slots,), jnp.int32),
            pltpu.VMEM((3,) + shape6, F32),
            pltpu.SemaphoreType.DMA((2,)),
        ],
        1,
    )(
        pinned(current_dirs), pinned(taste_masks), packed, before_z, after_z, fatf, longf, dacc, back_xy
    )

    def piece_of(slices):
        return jax.ShapeDtypeStruct((slices, 2, vectors, count * vectors), F32)

    (dacc,) = call(
        functools.partial(before_kernel, times, depth, vectors),
        [jax.ShapeDtypeStruct(shape6, F32)],
        [VM] * 4,
        [],
        1,
    )(before_t, fatf, longf, dacc)
    odd16 = jax.ShapeDtypeStruct(shape6, BF16)
    edge, dirac16, *early = call(
        functools.partial(early_kernel, times, depth, vectors),
        [jax.ShapeDtypeStruct((3, 1) + shape6[2:], F32), odd16] + [piece_of(times - 1)] * slots,
        [VM] * 6,
        [],
        1,
    )(after_t, fatf, longf, dacc, weights, left)
    dirac16, *late = call(
        functools.partial(late_kernel, times, depth, vectors),
        [odd16] + [piece_of(1)] * slots,
        [VM] * 6,
        [],
        1,
    )(after_last, longf, edge, weights, left, dirac16)

    odd_shape = rows_of(size)
    turned = dirac16.reshape(per_vector, vectors, LANES)
    scratch = [pltpu.VMEM((size, LANES), F32)]
    if rotate:
        send, partial, other = send_parts(early, [])
        _, partial_last, other_last = send_parts(late, [send])
        (odd_rows,) = call(spread_kernel, [odd_shape], [VM] * 2, scratch, 1)(turned, partial_last)
        meson_shape = jax.ShapeDtypeStruct((count, times, 2, vectors, vectors), F32)
        meson_fields = finish(meson_shape, 0, partial, other, [])
        meson_fields = finish(meson_shape, times - 1, partial_last, other_last, [meson_fields])
    else:
        (odd_rows,) = call(spread_kernel, [odd_shape], [VM], scratch, 1)(turned)
        pieces = [jnp.concatenate(pair, axis=0) for pair in zip(early, late)]
        whole = jnp.stack(pieces).reshape(slots, times, 2, vectors, count, vectors)
        whole = whole.transpose(0, 4, 1, 2, 3, 5).reshape(
            slots * count, times, 2, vectors, vectors
        )
        meson_fields = lax.psum_scatter(whole, ("gz", "gy"), scatter_dimension=0, tiled=True)
    odd_vectors = odd_rows.reshape(vectors, 3, times, depth, 2, LANES).transpose(0, 1, 4, 2, 3, 5)
    return odd_vectors, meson_fields


def solution(mesh):
    in_specs = (
        P(None, None, None, ("cfg", "ta"), "gz", "gy"),
        P(None, None, None, None, None, ("cfg", "ta"), "gz", "gy"),
        P(None, None, None, None, None, ("cfg", "ta"), "gz", "gy"),
        P("cfg"),
        P(),
        P(),
        P(),
    )
    out_specs = (
        P(None, None, None, ("cfg", "ta"), "gz", "gy"),
        P(("gz", "gy"), ("cfg", "ta"), None, None, None),
    )
    return jax.shard_map(
        on_device, mesh=mesh, in_specs=in_specs, out_specs=out_specs, check_vma=False
    )
```
